32 devices in a mesh: seq: 8 (over z, x), tp: 4 (over y, core).
Axes of the slice: x: 2, y: 2, z: 4, core: 2. Of those that a mesh axis runs over, the one named last changes fastest.
Arguments:
- x_in: bfloat16 [6144, 1024], P('seq', 'tp'), may hold values from -6 to 6
- ln_gain: float32 [1024], replicated, may hold values from 0.1 to 1.9
- ln_bias: float32 [1024], replicated, may hold values from -4 to 4
- w_qkv: bfloat16 [3, 1024, 1024], P(None, None, 'tp'), may hold values from -0.25 to 0.25
- w_o: bfloat16 [1024, 1024], P('tp'), may hold values from -1 to 1
- w_in: bfloat16 [1024, 4096], P(None, 'tp'), may hold values from -0.1875 to 0.1875
- b_in: float32 [4096], P('tp'), may hold values from -4 to 4
- w_out: bfloat16 [4096, 1024], P('tp'), may hold values from -0.09375 to 0.09375
- b_out: float32 [1024], P('tp'), may hold values from -4 to 4
- grad_out: bfloat16 [6144, 1024], P('seq', 'tp'), may hold values from -6 to 6
- segment_ids: int32 [6144], P('seq'), may hold values from 0 to 215, as said below
- pad_mask: int32 [6144], P('seq'), may hold values from 0 to 1, as said below
Outputs:
- mixed: bfloat16 [6144, 1024], P('seq', 'tp')
- grad_input: float32 [6144, 1024], P('seq', 'tp')
- grad_gain: float32 [1024], P('tp')
- grad_bias: float32 [1024], P('tp')
- grad_qkv: float32 [3, 1024, 1024], P(None, None, 'tp')
- grad_wo: float32 [1024, 1024], P('tp')
- grad_win: float32 [1024, 4096], P(None, 'tp')
- grad_bin: float32 [4096], P('tp')
- grad_wout: float32 [4096, 1024], P('tp')
- grad_bout: float32 [1024], P('tp')
The draws below stay inside these ranges and needn't reach their ends.
Inputs may be any that keep to these rules, and one draw needn't show every extreme that they name: `segment_ids`: ids never fall along the tokens; the tokens form packs of 1024 that no id crosses; a pack holds whole proteins of 30 to 1024 residues, each with an id of its own, followed by the pack's padding, which has one more id of its own; some pack holds a single protein of exactly 1024 residues; the last pack ends in padding. `pad_mask`: 0 exactly on the padding tokens of each pack.
All inputs are finite; a program needn't handle non-finite values.
Results may differ from the reference program's by a relative error of at most 0.012.
The reference program's roundings to bfloat16 on the way count: a program that leaves them out, or rounds other values in their place, can miss the bound.
Values may be sent and summed in bfloat16 or wider, within the bound.
A program may use at most 128 MiB of HBM per device.

```python
import jax
import jax.numpy as jnp
from jax import lax

D = 1024
HEADS = 16
HEAD = 64
FF = 4096
PACK = 1024
SHORTEST = 30
TOKENS = 6144


def layout(key):
    first_key, second_key = jax.random.split(key)
    pack_count = TOKENS // PACK
    slots = PACK // SHORTEST + 1
    spread = PACK - SHORTEST
    numbers = jax.random.randint(first_key, (pack_count, slots, 3), 0, spread + 1)
    lengths = SHORTEST + numbers[..., 0] * numbers[..., 1] // spread * numbers[..., 2] // spread
    chosen = jax.random.randint(second_key, (), 0, pack_count - 1)
    slot_index = jnp.arange(slots, dtype=jnp.int32)[None, :]
    pack_index = jnp.arange(pack_count, dtype=jnp.int32)[:, None]
    lengths = jnp.where((pack_index == chosen) & (slot_index == 0), PACK, lengths)
    ends = jnp.cumsum(lengths, 1)
    room = jnp.where(pack_index == pack_count - 1, PACK - 1, PACK)
    filled = jnp.max(jnp.where(ends <= room, ends, 0), 1)
    positions = jnp.arange(TOKENS, dtype=jnp.int32)
    pack_of = positions // PACK
    inner = positions % PACK
    local = jnp.sum((ends[pack_of] <= inner[:, None]).astype(jnp.int32), 1)
    unpadded = (inner < filled[pack_of]).astype(jnp.int32)
    local = jnp.where(unpadded == 1, local, slots)
    segment = pack_of * (slots + 1) + local
    return (segment.astype(jnp.int32), unpadded)


def draw_segment_ids(key, part):
    segment, unpadded = layout(key)
    return segment


def draw_pad_mask(key, part):
    segment, unpadded = layout(key)
    return unpadded


def shard_levels(rng, shape, shards, smallest, high):
    def one(axis_at, shards_of):
        heights = jax.random.uniform(jax.random.fold_in(jax.random.fold_in(rng, 6), axis_at), (shards_of,), jnp.float32, smallest / len(shards), high / len(shards))
        return jnp.repeat(jnp.exp(heights), shape[axis_at] // shards_of).reshape((-1,) + (1,) * (len(shape) - axis_at - 1))

    level = one(*shards[0])
    for cut in shards[1:]:
        level = level * one(*cut)
    return level


def normal_values(stream_key, dims, scale, bound, cuts=(), kind=jnp.bfloat16):
    entries = scale * jax.random.normal(stream_key, dims, jnp.float32)
    if cuts:
        entries = entries * shard_levels(stream_key, dims, cuts, -0.22, 0.18)
    return jnp.clip(entries, -bound, bound).astype(kind)


def setup_inputs(seed: int = 0) -> dict:
    arg_keys = jax.random.split(jax.random.key(seed), 13)
    return {
        "x_in": normal_values(arg_keys[0], (TOKENS, D), 1.0, 6.0, ((0, 8), (1, 4))),
        "ln_gain": jnp.clip(1.0 + 0.18 * jax.random.normal(arg_keys[1], (D,), jnp.float32), 0.1, 1.9),
        "ln_bias": normal_values(arg_keys[2], (D,), 0.3, 4.0, (), jnp.float32),
        "w_qkv": normal_values(arg_keys[3], (3, D, D), (D // 2) ** -0.5, 0.25, ((2, 4),)),
        "w_o": normal_values(arg_keys[4], (D, D), (max(1, D * 32 // PACK)) ** -0.5, 1.0, ((0, 4),)),
        "w_in": normal_values(arg_keys[5], (D, FF), D ** -0.5, 0.1875, ((1, 4),)),
        "b_in": normal_values(arg_keys[6], (FF,), 0.3, 4.0, ((0, 4),), jnp.float32),
        "w_out": normal_values(arg_keys[7], (FF, D), FF ** -0.5, 0.09375, ((0, 4),)),
        "b_out": normal_values(arg_keys[8], (D,), 0.3, 4.0, ((0, 4),), jnp.float32),
        "grad_out": normal_values(arg_keys[9], (TOKENS, D), 1.0, 6.0, ((0, 8), (1, 4))),
        "segment_ids": draw_segment_ids(jax.random.fold_in(arg_keys[12], 71), 0),
        "pad_mask": draw_pad_mask(jax.random.fold_in(arg_keys[12], 71), 0),
    }


LOG2E = 1.4426950408889634
EPSILON = 1e-05
HIGHEST = lax.Precision.HIGHEST

@jax.custom_vjp
def low(v):
    return lax.optimization_barrier(v.astype(jnp.bfloat16)).astype(jnp.float32)

@jax.custom_vjp
def low_back(v):
    return v

def low_keep(v):
    return (low(v), None)

def low_pass(kept, grad):
    return (grad,)

def back_keep(v):
    return (v, None)

def back_low(kept, grad):
    return (low(grad),)
low.defvjp(low_keep, low_pass)
low_back.defvjp(back_keep, back_low)

def rotary(source, places, sense):
    rows_count, head_count = (source.shape[0], source.shape[1])
    inverse = 10000.0 ** (-(jnp.arange(16, dtype=jnp.float32) * 2.0) / 32.0)
    phase = places[:, None] * inverse[None, :]
    cosine = jnp.cos(phase)[:, None, :]
    sine = sense * jnp.sin(phase)[:, None, :]
    paired = source[..., :32].reshape(rows_count, head_count, 16, 2)
    even_part = paired[..., 0]
    odd_part = paired[..., 1]
    turned = jnp.stack([even_part * cosine - odd_part * sine, odd_part * cosine + even_part * sine], -1)
    return jnp.concatenate([turned.reshape(rows_count, head_count, 32), source[..., 32:]], -1)

def permitted(query_tags, query_first, key_tags, key_first, limit):
    query_place = query_first + jnp.arange(query_tags.shape[0], dtype=jnp.int32)
    key_place = key_first + jnp.arange(key_tags.shape[0], dtype=jnp.int32)
    causal = (key_place[None, :] <= query_place[:, None]) & (key_place[None, :] >= 0) & (query_place[:, None] < limit)
    same_doc = key_tags[None, :] == query_tags[:, None]
    return causal & same_doc | (key_place[None, :] == query_place[:, None])

def attention_pack(query_rot, key_rot, values, query_tags, key_tags):
    logit = low_back(0.125 * jnp.einsum('qhd,khd->hqk', query_rot, key_rot, precision=HIGHEST)) * LOG2E
    mask_now = permitted(query_tags, jnp.int32(0), key_tags, jnp.int32(0), PACK)[None]
    ceiling = jnp.floor(lax.optimization_barrier(jnp.max(jnp.where(mask_now, logit, -1e+30), axis=2)))
    weight = jnp.where(mask_now, jnp.exp2(logit - ceiling[:, :, None]), 0.0)
    totals = lax.optimization_barrier(jnp.sum(weight, 2))
    accum = jnp.einsum('hqk,khd->qhd', low(weight), values, precision=HIGHEST)
    return low_back(accum) / totals.T[:, :, None]

def layer_forward(x_in, ln_gain, ln_bias, w_qkv, w_o, w_in, b_in, w_out, b_out, segment_ids, key_tags):
    center = x_in - lax.optimization_barrier(jnp.mean(x_in, -1, keepdims=True))
    inverse = lax.rsqrt(lax.optimization_barrier(jnp.mean(center * center, -1, keepdims=True)) + EPSILON)
    ln_out = low(center * inverse * ln_gain + ln_bias)
    places = (jnp.arange(TOKENS, dtype=jnp.int32) % PACK).astype(jnp.float32)

    def project(which):
        return low_back(jnp.dot(ln_out, w_qkv[which], precision=HIGHEST)).reshape(TOKENS, HEADS, HEAD)
    query_rot = low(rotary(project(0), places, 1.0))
    key_rot = low(rotary(project(1), places, 1.0))
    values = low(project(2))
    count_packs = TOKENS // PACK
    checked = jax.checkpoint(attention_pack)
    context = lax.map(lambda parts: checked(parts[0], parts[1], parts[2], parts[3], parts[4]), (query_rot.reshape(count_packs, PACK, HEADS, HEAD), key_rot.reshape(count_packs, PACK, HEADS, HEAD), values.reshape(count_packs, PACK, HEADS, HEAD), segment_ids.reshape(count_packs, PACK), key_tags.reshape(count_packs, PACK)))
    context_low = low(context.reshape(TOKENS, HEADS * HEAD))
    hidden_pre = low_back(jnp.dot(ln_out, w_in, precision=HIGHEST) + b_in)
    activ_low = low(jax.nn.gelu(hidden_pre, approximate=True))
    return x_in + jnp.dot(context_low, w_o, precision=HIGHEST) + jnp.dot(activ_low, w_out, precision=HIGHEST) + b_out

def reference(x_in, ln_gain, ln_bias, w_qkv, w_o, w_in, b_in, w_out, b_out, grad_out, segment_ids, pad_mask):
    key_tags = jnp.where(pad_mask == 1, segment_ids, -1).astype(jnp.int32)

    def forward(inputs, gains, biases, proj_qkv, proj_o, proj_in, bias_in, proj_out, bias_out):
        return layer_forward(inputs, gains, biases, proj_qkv, proj_o, proj_in, bias_in, proj_out, bias_out, segment_ids, key_tags)
    mixed, pull = jax.vjp(forward, x_in.astype(jnp.float32), ln_gain.astype(jnp.float32), ln_bias.astype(jnp.float32), w_qkv.astype(jnp.float32), w_o.astype(jnp.float32), w_in.astype(jnp.float32), b_in.astype(jnp.float32), w_out.astype(jnp.float32), b_out.astype(jnp.float32))
    grads = pull(grad_out.astype(jnp.float32))
    return (mixed.astype(jnp.bfloat16), grads[0], grads[1], grads[2], grads[3], grads[4], grads[5], grads[6], grads[7], grads[8])
```

```python
import functools

import jax
import jax.numpy as jnp
from jax import lax
from jax.experimental import pallas as pl
from jax.experimental.pallas import tpu as pltpu
from jax.sharding import PartitionSpec as P

PACK = 1024


LOG2E = 1.4426950408889634
EPSILON = 1e-05


MESH = pl.DeviceIdType.MESH


class Ring:
    def __init__(self, seq_count):
        self.count = seq_count
        self.m = seq_count // 2
        self.s = lax.axis_index("seq")
        self.t = lax.axis_index("tp")
        self.z = self.s // 2
        self.x = self.s % 2
        low = (self.z < self.m // 2).astype(jnp.int32)
        self.near = low
        self.far = 1 - low

    def at(self, z, x):
        return (z * 2 + x, self.t)

    def peer(self):
        return self.at(self.z, 1 - self.x)

    def step(self, piece, sign):
        return self.at(self.z + sign * (2 * piece - 1), self.x)

    def first(self, piece):
        return self.z == (1 - piece) * (self.m - 1)

    def last(self, piece):
        return self.z == piece * (self.m - 1)


def aligned(value):
    return pl.multiple_of(value, 16)


def add_rows(acc, acc_first, got, rows):
    step = 16 if rows % 32 else 32

    def body(i, carry):
        at = pl.ds(aligned(acc_first + i * step), step)
        here = pl.ds(aligned(i * step), step)
        acc[at, :] = (acc[at, :].astype(jnp.float32) + got[here, :].astype(jnp.float32)).astype(
            acc.dtype
        )
        return carry

    lax.fori_loop(0, rows // step, body, 0)


class Unit:
    def __init__(self, ring, index, part, out, out_first, rows, pair_buf, line_buf, send, recv, own):
        self.r, self.u = ring, index
        self.part, self.out, self.out_first, self.rows = part, out, out_first, rows
        self.pair_buf, self.line_buf = pair_buf, line_buf
        self.send, self.recv, self.own = send, recv, own

    def copy(self, src, dst, kind, to):
        return pltpu.make_async_remote_copy(
            src_ref=src,
            dst_ref=dst,
            send_sem=self.send.at[self.u, kind],
            recv_sem=self.recv.at[self.u, kind],
            device_id=to,
            device_id_type=MESH,
        )

    def p(self, first, rows):
        return self.part.at[pl.ds(aligned(first), rows)]

    def o(self, first, rows):
        return self.out.at[pl.ds(aligned(self.out_first + first), rows)]

    def keep(self, first, rows):
        return pltpu.make_async_copy(self.p(first, rows), self.o(first, rows), self.own.at[self.u])


class PairFirst(Unit):
    def pair(self):
        half = self.rows // 2
        return self.copy(self.p((1 - self.r.x) * half, half), self.pair_buf, 0, self.r.peer())

    def first_row(self, piece, member):
        return member * (self.rows // 2) + piece * (self.rows // 4)

    def line(self, piece):
        quarter = self.rows // 4
        return self.copy(
            self.p(self.first_row(piece, self.r.x), quarter),
            self.line_buf.at[piece],
            1 + piece,
            self.r.step(piece, 1),
        )

    def back(self, piece, origin):
        quarter = self.rows // 4
        row = self.first_row(piece, self.r.x)
        src = self.p(row, quarter) if origin else self.o(row, quarter)
        return self.copy(src, self.o(row, quarter), 3 + piece, self.r.step(piece, -1))

    def over(self, piece, origin):
        quarter = self.rows // 4
        row = self.first_row(piece, self.r.x)
        src = self.p(row, quarter) if origin else self.o(row, quarter)
        return self.copy(src, self.o(row, quarter), 5 + piece, self.r.peer())

    def start(self):
        self.pair().start()

    def paired(self):
        half = self.rows // 2
        self.pair().wait_recv()
        add_rows(self.part, self.r.x * half, self.pair_buf, half)
        piece = self.r.near

        @pl.when(self.r.first(piece))
        def _():
            self.line(piece).start()

    def chain_near(self):
        piece = self.r.near

        @pl.when(jnp.logical_not(self.r.first(piece)))
        def _():
            self.line(piece).wait_recv()
            add_rows(
                self.part, self.first_row(piece, self.r.x), self.line_buf.at[piece], self.rows // 4
            )
            self.line(piece).start()

    def chain_far(self):
        piece = self.r.far
        self.line(piece).wait_recv()
        add_rows(self.part, self.first_row(piece, self.r.x), self.line_buf.at[piece], self.rows // 4)

        @pl.when(jnp.logical_not(self.r.last(piece)))
        def _():
            self.line(piece).start()

        @pl.when(self.r.last(piece))
        def _():
            self.back(piece, True).start()
            self.over(piece, True).start()
            self.keep(self.first_row(piece, self.r.x), self.rows // 4).start()

    def exchanged(self):
        pass

    def back_near(self):
        piece = self.r.far

        @pl.when(jnp.logical_not(self.r.last(piece)))
        def _():
            self.back(piece, False).wait_recv()
            self.back(piece, False).start()
            self.over(piece, False).start()

    def back_far(self):
        piece = self.r.near
        self.back(piece, False).wait_recv()

        @pl.when(jnp.logical_not(self.r.first(piece)))
        def _():
            self.back(piece, False).start()

        self.over(piece, False).start()

    def finish(self):
        quarter = self.rows // 4
        for piece in (0, 1):
            row = self.first_row(piece, 1 - self.r.x)
            self.copy(self.o(row, quarter), self.o(row, quarter), 5 + piece, self.r.peer()).wait_recv()
        self.pair().wait_send()
        for piece in (0, 1):

            @pl.when(jnp.logical_not(self.r.last(piece)))
            def _():
                self.line(piece).wait_send()

            @pl.when(jnp.logical_not(self.r.first(piece)))
            def _():
                self.back(piece, False).wait_send()

            self.over(piece, False).wait_send()

        @pl.when(self.r.last(self.r.far))
        def _():
            self.keep(self.first_row(self.r.far, self.r.x), quarter).wait()


class LineFirst(Unit):
    def line(self, piece):
        half = self.rows // 2
        return self.copy(
            self.p(piece * half, half), self.line_buf.at[piece], 1 + piece, self.r.step(piece, 1)
        )

    def row_of(self, piece, member):
        return piece * (self.rows // 2) + member * (self.rows // 4)

    def pair(self, piece):
        quarter = self.rows // 4
        return self.copy(
            self.p(self.row_of(piece, 1 - self.r.x), quarter), self.pair_buf, 0, self.r.peer()
        )

    def over(self, piece, member, origin):
        quarter = self.rows // 4
        row = self.row_of(piece, member)
        src = self.p(row, quarter) if origin else self.o(row, quarter)
        return self.copy(src, self.o(row, quarter), 3, self.r.peer())

    def back(self, piece, member, origin):
        quarter = self.rows // 4
        row = self.row_of(piece, member)
        src = self.p(row, quarter) if origin else self.o(row, quarter)
        return self.copy(src, self.o(row, quarter), 4 + 2 * piece + member, self.r.step(piece, -1))

    def start(self):
        piece = self.r.near

        @pl.when(self.r.first(piece))
        def _():
            self.line(piece).start()

    def paired(self):
        pass

    def chain_near(self):
        piece = self.r.near

        @pl.when(jnp.logical_not(self.r.first(piece)))
        def _():
            self.line(piece).wait_recv()
            add_rows(self.part, piece * (self.rows // 2), self.line_buf.at[piece], self.rows // 2)
            self.line(piece).start()

    def chain_far(self):
        piece = self.r.far
        self.line(piece).wait_recv()
        add_rows(self.part, piece * (self.rows // 2), self.line_buf.at[piece], self.rows // 2)

        @pl.when(jnp.logical_not(self.r.last(piece)))
        def _():
            self.line(piece).start()

        @pl.when(self.r.last(piece))
        def _():
            self.pair(piece).start()

    def exchanged(self):
        piece = self.r.far
        quarter = self.rows // 4

        @pl.when(self.r.last(piece))
        def _():
            self.pair(piece).wait_recv()
            row = self.row_of(piece, self.r.x)
            add_rows(self.part, row, self.pair_buf, quarter)
            self.over(piece, self.r.x, True).start()
            self.back(piece, self.r.x, True).start()
            self.keep(row, quarter).start()

    def back_near(self):
        piece = self.r.far
        other = 1 - self.r.x

        @pl.when(self.r.last(piece))
        def _():
            self.over(piece, other, False).wait_recv()
            self.back(piece, other, False).start()

        @pl.when(jnp.logical_not(self.r.last(piece)))
        def _():
            for member in (self.r.x, other):
                self.back(piece, member, False).wait_recv()
                self.back(piece, member, False).start()

    def back_far(self):
        piece = self.r.near
        for member in (self.r.x, 1 - self.r.x):
            self.back(piece, member, False).wait_recv()

            @pl.when(jnp.logical_not(self.r.first(piece)))
            def _():
                self.back(piece, member, False).start()

    def finish(self):
        quarter = self.rows // 4
        for piece in (0, 1):

            @pl.when(jnp.logical_not(self.r.last(piece)))
            def _():
                self.line(piece).wait_send()

            @pl.when(jnp.logical_not(self.r.first(piece)))
            def _():
                for member in (0, 1):
                    self.back(piece, member, False).wait_send()

        piece = self.r.far

        @pl.when(self.r.last(piece))
        def _():
            self.pair(piece).wait_send()
            self.over(piece, self.r.x, False).wait_send()
            self.keep(self.row_of(piece, self.r.x), quarter).wait()


ROLES = ("start", "paired", "chain_near", "chain_far", "exchanged", "back_near", "back_far")


def greet(ring, with_tp):
    barrier = pltpu.get_barrier_semaphore()
    s, t, count = ring.s, ring.t, ring.count

    def signal(to):
        pl.semaphore_signal(barrier, inc=1, device_id=to, device_id_type=MESH)

    total = jnp.int32(0)
    bit = 1
    while bit < count:
        signal((s + bit - 2 * bit * ((s // bit) % 2), t))
        total = total + 1
        bit *= 2
    for sign in (-1, 1):
        ok = (ring.z + sign >= 0) & (ring.z + sign < ring.m)

        @pl.when(ok)
        def _():
            signal(ring.at(ring.z + sign, ring.x))

        total = total + ok.astype(jnp.int32)
    pl.semaphore_wait(barrier, total)


def vector_sum(ring, vec, got, send, recv):
    bit, level = 1, 0
    copies = []
    while bit < ring.count:
        other = ring.s + bit - 2 * bit * ((ring.s // bit) % 2)
        copy = pltpu.make_async_remote_copy(
            src_ref=vec.at[level],
            dst_ref=got.at[level],
            send_sem=send.at[level],
            recv_sem=recv.at[level],
            device_id=(other, ring.t),
            device_id_type=MESH,
        )
        copy.start()
        copy.wait_recv()
        vec[level + 1] = vec[level] + got[level]
        copies.append(copy)
        bit *= 2
        level += 1
    return copies


def sum_kernel(count, wout_in, win_in, wo_in, qkv_in, vec_in, wout, win, wo, qkv, vec_out,
               wide, tall, pair_wide, line_wide, pair_tall, line_tall, pair_wide2, line_wide2,
               pair_tall2, line_tall2, vec, got, send, recv, own, vsend, vrecv, lsem):
    ring = Ring(count)
    loads = []
    for i, (ref, first, rows) in enumerate(((wout_in, 0, 1024), (win_in, 1024, 1024), (wo_in, 2048, 256))):
        loads.append(pltpu.make_async_copy(ref, wide.at[pl.ds(first, rows)], lsem.at[i]))
    loads.append(pltpu.make_async_copy(qkv_in, tall, lsem.at[3]))
    for load in loads:
        load.start()
    greet(ring, False)
    for load in loads:
        load.wait()
    units = []
    for u in range(12):
        if u < 9:
            out, first = ((wout, u * 256) if u < 4 else (win, (u - 4) * 256) if u < 8 else (wo, 0))
            args = (wide.at[pl.ds(u * 256, 256)], out, first, 256)
            bufs = (pair_wide, line_wide) if u % 2 == 0 else (pair_wide2, line_wide2)
            slot = u // 2
        else:
            args = (tall.at[u - 9], qkv.at[u - 9], 0, 1024)
            bufs = (pair_tall, line_tall) if u % 2 == 0 else (pair_tall2, line_tall2)
            slot = (u - 9) // 2
        kind = PairFirst if u % 2 == 0 else LineFirst
        units.append(kind(ring, u, *args, bufs[0].at[slot], bufs[1].at[slot], send, recv, own))
    for unit in units:
        unit.start()
    vec[0] = vec_in[...]
    copies = vector_sum(ring, vec, got, vsend, vrecv)
    vec_out[...] = vec[len(copies)]
    for tick in range(6 + len(ROLES) - 1):
        for late, role in enumerate(ROLES[1:]):
            k = tick - late
            if 0 <= k < 6:
                getattr(units[2 * k + 1], role)()
                getattr(units[2 * k], role)()
    for unit in units:
        unit.finish()
    for copy in copies:
        copy.wait_send()


def sum_over_seq(count, wout, win, wo, qkv, vec):
    levels = count.bit_length() - 1
    any_spec = pl.BlockSpec(memory_space=pl.ANY)
    vm = pl.BlockSpec(memory_space=pltpu.VMEM)
    bf = jnp.bfloat16
    return pl.pallas_call(
        functools.partial(sum_kernel, count),
        out_shape=[
            jax.ShapeDtypeStruct(wout.shape, bf),
            jax.ShapeDtypeStruct(win.shape, bf),
            jax.ShapeDtypeStruct(wo.shape, bf),
            jax.ShapeDtypeStruct(qkv.shape, bf),
            jax.ShapeDtypeStruct(vec.shape, jnp.float32),
        ],
        in_specs=[any_spec] * 4 + [vm],
        out_specs=[any_spec] * 4 + [vm],
        scratch_shapes=[
            pltpu.VMEM((2304, 1024), bf),
            pltpu.VMEM((3, 1024, 256), bf),
            pltpu.VMEM((5, 128, 1024), bf),
            pltpu.VMEM((5, 2, 64, 1024), bf),
            pltpu.VMEM((2, 512, 256), bf),
            pltpu.VMEM((2, 2, 256, 256), bf),
            pltpu.VMEM((4, 64, 1024), bf),
            pltpu.VMEM((4, 2, 128, 1024), bf),
            pltpu.VMEM((2, 256, 256), bf),
            pltpu.VMEM((2, 2, 512, 256), bf),
            pltpu.VMEM((levels + 1,) + vec.shape, jnp.float32),
            pltpu.VMEM((levels,) + vec.shape, jnp.float32),
            pltpu.SemaphoreType.DMA((12, 8)),
            pltpu.SemaphoreType.DMA((12, 8)),
            pltpu.SemaphoreType.DMA((12,)),
            pltpu.SemaphoreType.DMA((levels,)),
            pltpu.SemaphoreType.DMA((levels,)),
            pltpu.SemaphoreType.DMA((4,)),
        ],
        compiler_params=pltpu.CompilerParams(
            collective_id=0, has_side_effects=True, vmem_limit_bytes=48 * 2**20
        ),
    )(wout, win, wo, qkv, vec)


def passed_along(value, axis, steps):
    count = lax.axis_size(axis)
    leading, last = (max(0, -steps), min(count, count - steps))
    return lax.ppermute(value, axis, [(source, source + steps) for source in range(leading, last)])


def angles(first_row, rows_count):
    places = ((first_row + jnp.arange(rows_count, dtype=jnp.int32)) % PACK).astype(jnp.float32)
    inverse = 10000.0 ** (-(jnp.arange(16, dtype=jnp.float32) * 2.0) / 32.0)
    phase = places[:, None] * inverse[None, :]
    return (jnp.cos(phase), jnp.sin(phase))


def rotate(source, cosine, sine, sense):
    rows_count, head_count = (source.shape[0], source.shape[1])
    paired = source[..., :32].reshape(rows_count, head_count, 16, 2)
    even_part = paired[..., 0]
    odd_part = paired[..., 1]
    cos_rows = cosine[:, None, :]
    sin_rows = sense * sine[:, None, :]
    turned = jnp.stack(
        [even_part * cos_rows - odd_part * sin_rows, odd_part * cos_rows + even_part * sin_rows], -1
    )
    return jnp.concatenate([turned.reshape(rows_count, head_count, 32), source[..., 32:]], -1)


def permitted(query_tags, query_first, key_tags, key_first, limit):
    query_place = query_first + jnp.arange(query_tags.shape[0], dtype=jnp.int32)
    key_place = key_first + jnp.arange(key_tags.shape[0], dtype=jnp.int32)
    causal = (
        (key_place[None, :] <= query_place[:, None])
        & (key_place[None, :] >= 0)
        & (query_place[:, None] < limit)
    )
    same_doc = key_tags[None, :] == query_tags[:, None]
    return causal & same_doc | (key_place[None, :] == query_place[:, None])


def base_two(query_rot, key_part):
    return (
        0.125
        * jnp.einsum("qhd,khd->hqk", query_rot, key_part, preferred_element_type=jnp.float32)
        * LOG2E
    )


def shards(
    x_in, ln_gain, ln_bias, w_qkv, w_o, w_in, b_in, w_out, b_out, grad_out, segment_ids, pad_mask
):
    rows_local = x_in.shape[0]
    width_local = x_in.shape[1]
    head_count = w_qkv.shape[2] // 64
    head_width = head_count * 64
    tp_rank = lax.axis_index("tp")
    row_first = lax.axis_index("seq") * rows_local
    limit = lax.axis_size("seq") * rows_local
    reach = (PACK - 2) // rows_local + 1
    key_tags = jnp.where(pad_mask == 1, segment_ids, -1)
    cosine, sine = angles(row_first, rows_local)
    whole = lax.all_gather(x_in, "tp", axis=1, tiled=True)
    inputs = whole.astype(jnp.float32)
    center = inputs - jnp.mean(inputs, -1, keepdims=True)
    inverse = lax.rsqrt(jnp.mean(center * center, -1, keepdims=True) + EPSILON)
    normed = center * inverse
    ln_out = (normed * ln_gain + ln_bias).astype(jnp.bfloat16)

    def project(which):
        return jnp.dot(ln_out, w_qkv[which], preferred_element_type=jnp.float32).reshape(
            rows_local, head_count, 64
        )

    query_rot = rotate(project(0), cosine, sine, 1.0).astype(jnp.bfloat16)
    key_rot = rotate(project(1), cosine, sine, 1.0).astype(jnp.bfloat16)
    values = project(2).astype(jnp.bfloat16)
    query_flat = query_rot.reshape(rows_local, head_width)
    key_flat = key_rot.reshape(rows_local, head_width)
    value_flat = values.reshape(rows_local, head_width)
    received = []
    for step in range(1, reach + 1):
        received.append(passed_along((key_flat, value_flat, key_tags), "seq", step))
    earliest = received[::-1]
    key_cat = jnp.concatenate([part[0] for part in earliest] + [key_flat], 0)
    value_cat = jnp.concatenate([part[1] for part in earliest] + [value_flat], 0)
    tag_cat = jnp.concatenate([part[2] for part in earliest] + [key_tags], 0)
    key_first = row_first - reach * rows_local
    key_heads = key_cat.reshape(-1, head_count, 64)
    value_heads = value_cat.reshape(-1, head_count, 64)
    mask_now = permitted(segment_ids, row_first, tag_cat, key_first, limit)[None]
    logit = base_two(query_rot, key_heads)
    ceiling = jnp.floor(jnp.max(jnp.where(mask_now, logit, -1e30), axis=2))
    weight = jnp.where(mask_now, jnp.exp2(logit - ceiling[:, :, None]), 0.0)
    totals = jnp.sum(weight, 2)
    accum = jnp.einsum(
        "hqk,khd->qhd", weight.astype(jnp.bfloat16), value_heads, preferred_element_type=jnp.float32
    )
    context = accum / totals.T[:, :, None]
    context_low = context.astype(jnp.bfloat16).reshape(rows_local, head_width)
    hidden_pre = jnp.dot(ln_out, w_in, preferred_element_type=jnp.float32) + b_in
    activ_low = jax.nn.gelu(hidden_pre, approximate=True).astype(jnp.bfloat16)
    branch = jnp.dot(context_low, w_o, preferred_element_type=jnp.float32) + jnp.dot(
        activ_low, w_out, preferred_element_type=jnp.float32
    )
    summed = lax.psum_scatter(branch, "tp", scatter_dimension=1, tiled=True)
    mixed = (x_in.astype(jnp.float32) + summed + b_out).astype(jnp.bfloat16)
    grad_whole = lax.all_gather(grad_out, "tp", axis=1, tiled=True)
    grad_wo = jnp.dot(context_low.T, grad_whole, preferred_element_type=jnp.float32)
    grad_wout = jnp.dot(activ_low.T, grad_whole, preferred_element_type=jnp.float32)
    grad_bout = jnp.sum(grad_out.astype(jnp.float32), 0)
    grad_context = jnp.dot(grad_whole, w_o.T, preferred_element_type=jnp.float32).reshape(
        rows_local, head_count, 64
    )
    grad_activ = jnp.dot(grad_whole, w_out.T, preferred_element_type=jnp.float32)
    gelu_pull = jax.vjp(lambda pre: jax.nn.gelu(pre, approximate=True), hidden_pre)[1]
    grad_hidden = gelu_pull(grad_activ)[0].astype(jnp.bfloat16)
    grad_win = jnp.dot(ln_out.T, grad_hidden, preferred_element_type=jnp.float32)
    grad_bin = jnp.sum(grad_hidden.astype(jnp.float32), 0)
    grad_accum = (grad_context / totals.T[:, :, None]).astype(jnp.bfloat16)
    offset_term = jnp.sum(grad_context * context, -1).T / totals
    grad_accum_flat = grad_accum.reshape(rows_local, head_width)

    def score_grads(
        query_part,
        grad_part,
        ceil_part,
        offs_part,
        query_tags,
        query_first,
        key_part,
        value_part,
        tag_part,
        part_first,
    ):
        mask_part = permitted(query_tags, query_first, tag_part, part_first, limit)[None]
        weight_part = jnp.where(
            mask_part, jnp.exp2(base_two(query_part, key_part) - ceil_part[:, :, None]), 0.0
        )
        grad_weight = (
            jnp.einsum("qhd,khd->hqk", grad_part, value_part, preferred_element_type=jnp.float32)
            - offs_part[:, :, None]
        )
        return (weight_part.astype(jnp.bfloat16), (weight_part * grad_weight).astype(jnp.bfloat16))

    weight_low, grad_logit = score_grads(
        query_rot,
        grad_accum,
        ceiling,
        offset_term,
        segment_ids,
        row_first,
        key_heads,
        value_heads,
        tag_cat,
        key_first,
    )
    grad_query_rot = 0.125 * jnp.einsum(
        "hqk,khd->qhd", grad_logit, key_heads, preferred_element_type=jnp.float32
    )
    arrived = [(query_flat, grad_accum_flat, ceiling.T, offset_term.T, segment_ids)]
    for step in range(1, reach + 1):
        arrived.append(
            (
                passed_along(query_flat.astype(jnp.float32), "seq", -step).astype(query_flat.dtype),
                passed_along(grad_accum_flat.astype(jnp.float32), "seq", -step).astype(
                    grad_accum_flat.dtype
                ),
                passed_along(ceiling.T, "seq", -step),
                passed_along(offset_term.T, "seq", -step),
                passed_along(segment_ids, "seq", -step),
            )
        )
    query_cat = jnp.concatenate([part[0] for part in arrived], 0)
    grad_cat = jnp.concatenate([part[1] for part in arrived], 0)
    ceil_cat = jnp.concatenate([part[2] for part in arrived], 0).T
    offs_cat = jnp.concatenate([part[3] for part in arrived], 0).T
    qtag_cat = jnp.concatenate([part[4] for part in arrived], 0)
    query_heads = query_cat.reshape(-1, head_count, 64)
    grad_heads = grad_cat.reshape(-1, head_count, 64)
    weight_back, logit_back = score_grads(
        query_heads,
        grad_heads,
        ceil_cat,
        offs_cat,
        qtag_cat,
        row_first,
        key_rot,
        values,
        key_tags,
        row_first,
    )
    grad_key_rot = 0.125 * jnp.einsum(
        "hqk,qhd->khd", logit_back, query_heads, preferred_element_type=jnp.float32
    )
    grad_value_sum = jnp.einsum(
        "hqk,qhd->khd", weight_back, grad_heads, preferred_element_type=jnp.float32
    )
    grad_query = (
        rotate(grad_query_rot, cosine, sine, -1.0)
        .astype(jnp.bfloat16)
        .reshape(rows_local, head_width)
    )
    grad_key = (
        rotate(grad_key_rot, cosine, sine, -1.0)
        .astype(jnp.bfloat16)
        .reshape(rows_local, head_width)
    )
    grad_values = grad_value_sum.astype(jnp.bfloat16).reshape(rows_local, head_width)
    grad_qkv = jnp.stack(
        [
            jnp.dot(ln_out.T, grad_query, preferred_element_type=jnp.float32),
            jnp.dot(ln_out.T, grad_key, preferred_element_type=jnp.float32),
            jnp.dot(ln_out.T, grad_values, preferred_element_type=jnp.float32),
        ]
    )
    grad_norm_part = (
        jnp.dot(grad_query, w_qkv[0].T, preferred_element_type=jnp.float32)
        + jnp.dot(grad_key, w_qkv[1].T, preferred_element_type=jnp.float32)
        + jnp.dot(grad_values, w_qkv[2].T, preferred_element_type=jnp.float32)
        + jnp.dot(grad_hidden, w_in.T, preferred_element_type=jnp.float32)
    )
    feature_first = tp_rank * width_local
    grad_norm = lax.psum(grad_norm_part, "tp")
    grad_gain = lax.dynamic_slice_in_dim(
        jnp.sum(grad_norm * normed, 0), feature_first, width_local, 0
    )
    grad_bias = lax.dynamic_slice_in_dim(jnp.sum(grad_norm, 0), feature_first, width_local, 0)
    grad_hat = grad_norm * ln_gain
    row_mean = jnp.mean(grad_hat, -1, keepdims=True)
    row_cross = jnp.mean(grad_hat * normed, -1, keepdims=True)
    grad_full = inverse * (grad_hat - row_mean - normed * row_cross)
    grad_input = lax.dynamic_slice_in_dim(
        grad_full, feature_first, width_local, 1
    ) + grad_out.astype(jnp.float32)
    bf = jnp.bfloat16
    vec = jnp.zeros((8, 1024), jnp.float32)
    vec = vec.at[0].set(grad_bin).at[1, :256].set(grad_gain).at[1, 256:512].set(grad_bias)
    vec = vec.at[1, 512:768].set(grad_bout)
    wout, win, wo, qkv, vec = sum_over_seq(
        lax.axis_size("seq"), grad_wout.astype(bf), grad_win.astype(bf), grad_wo.astype(bf),
        grad_qkv.astype(bf), vec
    )
    f32 = jnp.float32
    return (
        mixed,
        grad_input,
        vec[1, :256],
        vec[1, 256:512],
        qkv.astype(f32),
        wo.astype(f32),
        win.astype(f32),
        vec[0],
        wout.astype(f32),
        vec[1, 512:768],
    )


def solution(mesh):
    return jax.shard_map(
        shards,
        mesh=mesh,
        in_specs=(
            P("seq", "tp"),
            P(),
            P(),
            P(None, None, "tp"),
            P("tp", None),
            P(None, "tp"),
            P("tp"),
            P("tp", None),
            P("tp"),
            P("seq", "tp"),
            P("seq"),
            P("seq"),
        ),
        out_specs=(
            P("seq", "tp"),
            P("seq", "tp"),
            P("tp"),
            P("tp"),
            P(None, None, "tp"),
            P("tp", None),
            P(None, "tp"),
            P("tp"),
            P("tp", None),
            P("tp"),
        ),
        check_vma=False,
    )
```

```python
import functools

import jax
import jax.numpy as jnp
import numpy as np
from jax import lax
from jax.experimental import pallas as pl
from jax.experimental.pallas import tpu as pltpu
from jax.sharding import PartitionSpec as P

PACK = 1024
LOG2E = 1.4426950408889634
EPSILON = 1e-05
BLOCK = 256
MESH = pl.DeviceIdType.MESH
BF = jnp.bfloat16
F32 = jnp.float32


class Ring:
    def __init__(self, seq_count):
        self.count = seq_count
        self.m = seq_count // 2
        self.s = lax.axis_index("seq")
        self.t = lax.axis_index("tp")
        self.z = self.s // 2
        self.x = self.s % 2
        low = (self.z < self.m // 2).astype(jnp.int32)
        self.near = low
        self.far = 1 - low

    def at(self, z, x):
        return (z * 2 + x, self.t)

    def peer(self):
        return self.at(self.z, 1 - self.x)

    def step(self, piece, sign):
        return self.at(self.z + sign * (2 * piece - 1), self.x)

    def first(self, piece):
        return self.z == (1 - piece) * (self.m - 1)

    def last(self, piece):
        return self.z == piece * (self.m - 1)


def aligned(value):
    return pl.multiple_of(value, 16)


def add_rows(acc, acc_first, got, rows):
    step = 16 if rows % 32 else 32

    def body(i, carry):
        at = pl.ds(aligned(acc_first + i * step), step)
        here = pl.ds(aligned(i * step), step)
        acc[at, :] = (acc[at, :].astype(jnp.float32) + got[here, :].astype(jnp.float32)).astype(
            acc.dtype
        )
        return carry

    lax.fori_loop(0, rows // step, body, 0)


class Unit:
    def __init__(self, ring, index, part, out, out_first, rows, pair_buf, line_buf, send, recv, own):
        self.r, self.u = ring, index
        self.part, self.out, self.out_first, self.rows = part, out, out_first, rows
        self.pair_buf, self.line_buf = pair_buf, line_buf
        self.send, self.recv, self.own = send, recv, own

    def copy(self, src, dst, kind, to):
        return pltpu.make_async_remote_copy(
            src_ref=src,
            dst_ref=dst,
            send_sem=self.send.at[self.u, kind],
            recv_sem=self.recv.at[self.u, kind],
            device_id=to,
            device_id_type=MESH,
        )

    def p(self, first, rows):
        return self.part.at[pl.ds(aligned(first), rows)]

    def o(self, first, rows):
        return self.out.at[pl.ds(aligned(self.out_first + first), rows)]

    def keep(self, first, rows):
        return pltpu.make_async_copy(self.p(first, rows), self.o(first, rows), self.own.at[self.u])


class PairFirst(Unit):
    def pair(self):
        half = self.rows // 2
        return self.copy(self.p((1 - self.r.x) * half, half), self.pair_buf, 0, self.r.peer())

    def first_row(self, piece, member):
        return member * (self.rows // 2) + piece * (self.rows // 4)

    def line(self, piece):
        quarter = self.rows // 4
        return self.copy(
            self.p(self.first_row(piece, self.r.x), quarter),
            self.line_buf.at[piece],
            1 + piece,
            self.r.step(piece, 1),
        )

    def back(self, piece, origin):
        quarter = self.rows // 4
        row = self.first_row(piece, self.r.x)
        src = self.p(row, quarter) if origin else self.o(row, quarter)
        return self.copy(src, self.o(row, quarter), 3 + piece, self.r.step(piece, -1))

    def over(self, piece, origin):
        quarter = self.rows // 4
        row = self.first_row(piece, self.r.x)
        src = self.p(row, quarter) if origin else self.o(row, quarter)
        return self.copy(src, self.o(row, quarter), 5 + piece, self.r.peer())

    def start(self):
        self.pair().start()

    def paired(self):
        half = self.rows // 2
        self.pair().wait_recv()
        add_rows(self.part, self.r.x * half, self.pair_buf, half)
        piece = self.r.near

        @pl.when(self.r.first(piece))
        def _():
            self.line(piece).start()

    def chain_near(self):
        piece = self.r.near

        @pl.when(jnp.logical_not(self.r.first(piece)))
        def _():
            self.line(piece).wait_recv()
            add_rows(
                self.part, self.first_row(piece, self.r.x), self.line_buf.at[piece], self.rows // 4
            )
            self.line(piece).start()

    def chain_far(self):
        piece = self.r.far
        self.line(piece).wait_recv()
        add_rows(self.part, self.first_row(piece, self.r.x), self.line_buf.at[piece], self.rows // 4)

        @pl.when(jnp.logical_not(self.r.last(piece)))
        def _():
            self.line(piece).start()

        @pl.when(self.r.last(piece))
        def _():
            self.back(piece, True).start()
            self.over(piece, True).start()
            self.keep(self.first_row(piece, self.r.x), self.rows // 4).start()

    def exchanged(self):
        pass

    def back_near(self):
        piece = self.r.far

        @pl.when(jnp.logical_not(self.r.last(piece)))
        def _():
            self.back(piece, False).wait_recv()
            self.back(piece, False).start()
            self.over(piece, False).start()

    def back_far(self):
        piece = self.r.near
        self.back(piece, False).wait_recv()

        @pl.when(jnp.logical_not(self.r.first(piece)))
        def _():
            self.back(piece, False).start()

        self.over(piece, False).start()

    def finish(self):
        quarter = self.rows // 4
        for piece in (0, 1):
            row = self.first_row(piece, 1 - self.r.x)
            self.copy(self.o(row, quarter), self.o(row, quarter), 5 + piece, self.r.peer()).wait_recv()
        self.pair().wait_send()
        for piece in (0, 1):

            @pl.when(jnp.logical_not(self.r.last(piece)))
            def _():
                self.line(piece).wait_send()

            @pl.when(jnp.logical_not(self.r.first(piece)))
            def _():
                self.back(piece, False).wait_send()

            self.over(piece, False).wait_send()

        @pl.when(self.r.last(self.r.far))
        def _():
            self.keep(self.first_row(self.r.far, self.r.x), quarter).wait()


class LineFirst(Unit):
    def line(self, piece):
        half = self.rows // 2
        return self.copy(
            self.p(piece * half, half), self.line_buf.at[piece], 1 + piece, self.r.step(piece, 1)
        )

    def row_of(self, piece, member):
        return piece * (self.rows // 2) + member * (self.rows // 4)

    def pair(self, piece):
        quarter = self.rows // 4
        return self.copy(
            self.p(self.row_of(piece, 1 - self.r.x), quarter), self.pair_buf, 0, self.r.peer()
        )

    def over(self, piece, member, origin):
        quarter = self.rows // 4
        row = self.row_of(piece, member)
        src = self.p(row, quarter) if origin else self.o(row, quarter)
        return self.copy(src, self.o(row, quarter), 3, self.r.peer())

    def back(self, piece, member, origin):
        quarter = self.rows // 4
        row = self.row_of(piece, member)
        src = self.p(row, quarter) if origin else self.o(row, quarter)
        return self.copy(src, self.o(row, quarter), 4 + 2 * piece + member, self.r.step(piece, -1))

    def start(self):
        piece = self.r.near

        @pl.when(self.r.first(piece))
        def _():
            self.line(piece).start()

    def paired(self):
        pass

    def chain_near(self):
        piece = self.r.near

        @pl.when(jnp.logical_not(self.r.first(piece)))
        def _():
            self.line(piece).wait_recv()
            add_rows(self.part, piece * (self.rows // 2), self.line_buf.at[piece], self.rows // 2)
            self.line(piece).start()

    def chain_far(self):
        piece = self.r.far
        self.line(piece).wait_recv()
        add_rows(self.part, piece * (self.rows // 2), self.line_buf.at[piece], self.rows // 2)

        @pl.when(jnp.logical_not(self.r.last(piece)))
        def _():
            self.line(piece).start()

        @pl.when(self.r.last(piece))
        def _():
            self.pair(piece).start()

    def exchanged(self):
        piece = self.r.far
        quarter = self.rows // 4

        @pl.when(self.r.last(piece))
        def _():
            self.pair(piece).wait_recv()
            row = self.row_of(piece, self.r.x)
            add_rows(self.part, row, self.pair_buf, quarter)
            self.over(piece, self.r.x, True).start()
            self.back(piece, self.r.x, True).start()
            self.keep(row, quarter).start()

    def back_near(self):
        piece = self.r.far
        other = 1 - self.r.x

        @pl.when(self.r.last(piece))
        def _():
            self.over(piece, other, False).wait_recv()
            self.back(piece, other, False).start()

        @pl.when(jnp.logical_not(self.r.last(piece)))
        def _():
            for member in (self.r.x, other):
                self.back(piece, member, False).wait_recv()
                self.back(piece, member, False).start()

    def back_far(self):
        piece = self.r.near
        for member in (self.r.x, 1 - self.r.x):
            self.back(piece, member, False).wait_recv()

            @pl.when(jnp.logical_not(self.r.first(piece)))
            def _():
                self.back(piece, member, False).start()

    def finish(self):
        quarter = self.rows // 4
        for piece in (0, 1):

            @pl.when(jnp.logical_not(self.r.last(piece)))
            def _():
                self.line(piece).wait_send()

            @pl.when(jnp.logical_not(self.r.first(piece)))
            def _():
                for member in (0, 1):
                    self.back(piece, member, False).wait_send()

        piece = self.r.far

        @pl.when(self.r.last(piece))
        def _():
            self.pair(piece).wait_send()
            self.over(piece, self.r.x, False).wait_send()
            self.keep(self.row_of(piece, self.r.x), quarter).wait()


KINDS = (
    PairFirst,
    PairFirst,
    LineFirst,
    PairFirst,
    PairFirst,
    LineFirst,
    PairFirst,
    PairFirst,
    LineFirst,
    PairFirst,
    PairFirst,
    LineFirst,
)

STEPS = (
    (-1, "wout0"),
    (0, "start"),
    (-1, "wout1"),
    (1, "start"),
    (-1, "wout2"),
    (2, "start"),
    (-1, "wout3"),
    (3, "start"),
    (-1, "win0"),
    (4, "start"),
    (-1, "win1"),
    (5, "start"),
    (-1, "win2"),
    (6, "start"),
    (-1, "win3"),
    (7, "start"),
    (-1, "context_pull"),
    (-1, "receive_keys"),
    (-1, "attend0"),
    (-1, "attend1"),
    (-1, "attend2"),
    (-1, "send_key_grads"),
    (-1, "grad_wo"),
    (8, "start"),
    (-1, "near0"),
    (-1, "far0"),
    (-1, "own0"),
    (-1, "join_keys"),
    (-1, "grad_qkv"),
    (9, "start"),
    (10, "start"),
    (11, "start"),
    (-1, "near1"),
    (-1, "far1"),
    (-1, "own1"),
    (-1, "join_branch"),
    (-1, "norm_grad"),
    (-1, "stats_join"),
    (-1, "input_grad"),
    (-1, "vec_start"),
    (-1, "vec0"),
    (-1, "vec1"),
    (-1, "vec_rest"),
    (2, "chain_near"),
    (5, "chain_near"),
    (0, "paired"),
    (8, "chain_near"),
    (11, "chain_near"),
    (1, "paired"),
    (0, "chain_near"),
    (3, "paired"),
    (2, "chain_far"),
    (1, "chain_near"),
    (4, "paired"),
    (5, "chain_far"),
    (3, "chain_near"),
    (6, "paired"),
    (4, "chain_near"),
    (8, "chain_far"),
    (2, "exchanged"),
    (6, "chain_near"),
    (7, "paired"),
    (11, "chain_far"),
    (5, "exchanged"),
    (7, "chain_near"),
    (0, "chain_far"),
    (8, "exchanged"),
    (9, "paired"),
    (1, "chain_far"),
    (9, "chain_near"),
    (3, "chain_far"),
    (11, "exchanged"),
    (0, "back_near"),
    (10, "paired"),
    (4, "chain_far"),
    (1, "back_near"),
    (6, "chain_far"),
    (10, "chain_near"),
    (3, "back_near"),
    (7, "chain_far"),
    (9, "chain_far"),
    (4, "back_near"),
    (0, "back_far"),
    (6, "back_near"),
    (1, "back_far"),
    (10, "chain_far"),
    (7, "back_near"),
    (3, "back_far"),
    (9, "back_near"),
    (4, "back_far"),
    (10, "back_near"),
    (6, "back_far"),
    (2, "back_near"),
    (5, "back_near"),
    (7, "back_far"),
    (8, "back_near"),
    (9, "back_far"),
    (11, "back_near"),
    (10, "back_far"),
    (2, "back_far"),
    (5, "back_far"),
    (8, "back_far"),
    (11, "back_far"),
)


def greet(ring):
    barrier = pltpu.get_barrier_semaphore()
    s, t, count = ring.s, ring.t, ring.count

    def signal(to):
        pl.semaphore_signal(barrier, inc=1, device_id=to, device_id_type=MESH)

    signal((s, mate(t, 1)))
    signal((s, mate(t, 2)))
    total = jnp.int32(2)
    bit = 1
    while bit < count:
        signal((mate(s, bit), t))
        total = total + 1
        bit *= 2
    for hop in (-2, -1, 1, 2):
        ok = (s + hop >= 0) & (s + hop < count)

        @pl.when(ok)
        def _():
            signal((s + hop, t))

        total = total + ok.astype(jnp.int32)
    pl.semaphore_wait(barrier, total)


def mate(place, bit):
    return place + bit - 2 * bit * ((place // bit) % 2)


def dot(a, b):
    return jnp.dot(a, b, preferred_element_type=F32)


def dot_rows(a, b):
    return lax.dot_general(a, b, (((0,), (0,)), ((), ())), preferred_element_type=F32)


def dot_columns(a, b):
    return lax.dot_general(a, b, (((1,), (1,)), ((), ())), preferred_element_type=F32)


def layer_kernel(
    count, rows, names, *refs
):
    r = dict(zip(names, refs))
    ring = Ring(count)
    s, t = ring.s, ring.t
    blocks = rows // BLOCK
    per_pack = PACK // BLOCK
    x_all, g_all, ln = r["x_all"], r["g_all"], r["ln"]
    wqkv, wo, win, wout = r["wqkv"], r["wo"], r["win"], r["wout"]
    hidden_tiles = win.shape[1] // BLOCK
    width_tiles = win.shape[0] // BLOCK

    def blk(b):
        return pl.ds(b * BLOCK, BLOCK) if isinstance(b, int) else pl.ds(pl.multiple_of(b * BLOCK, BLOCK), BLOCK)

    loads = {}

    def load(name, src, dst):
        copy = pltpu.make_async_copy(src, dst, r["load_sem"].at[len(loads)])
        loads[name] = copy
        copy.start()

    load("x", r["x_in"], x_all.at[:, blk(t)])
    load("wqkv", r["wqkv_in"], wqkv)
    load("win", r["win_in"], win)
    load("g", r["g_in"], g_all.at[:, blk(t)])
    load("wout", r["wout_in"], wout)
    load("wo", r["wo_in"], wo)
    for b in range(blocks):
        place = (blocks * s + b) % per_pack
        load(("cos", b), r["cos_in"].at[place], r["cos"].at[b])
        load(("sin", b), r["sin_in"].at[place], r["sin"].at[b])
    greet(ring)

    def gather(which, b, kind):
        src_ref, whole = ((r["x_in"], x_all), (r["g_in"], g_all))[which]
        to = mate(t, 2) if kind == 1 else mate(t, 1)
        shard = mate(t, 2) if kind == 2 else t
        dst = whole.at[blk(b), blk(shard)]
        src = dst if kind == 2 else src_ref.at[blk(b)]
        return pltpu.make_async_remote_copy(
            src_ref=src,
            dst_ref=dst,
            send_sem=r["ag_send"].at[which, b, kind],
            recv_sem=r["ag_recv"].at[which, b, kind],
            device_id=(s, to),
            device_id_type=MESH,
        )

    for which in (0, 1):
        for b in range(blocks):
            gather(which, b, 1).start()
            gather(which, b, 0).start()
    r["dk"][...] = jnp.zeros(r["dk"].shape, F32)
    r["dv"][...] = jnp.zeros(r["dv"].shape, F32)

    def relay(which, b):
        gather(which, b, 1).wait_recv()
        gather(which, b, 2).start()

    def arrived(which, b):
        gather(which, b, 0).wait_recv()
        gather(which, b, 2).wait_recv()

    lane = lax.broadcasted_iota(jnp.int32, (BLOCK, BLOCK), 1)
    gain_own = r["gain"][:, blk(t)]

    def norm(b):
        xb = x_all[blk(b), :].astype(F32)
        mean = jnp.mean(xb, -1, keepdims=True)
        center = xb - mean
        inverse = lax.rsqrt(jnp.mean(center * center, -1, keepdims=True) + EPSILON)
        ln[blk(b), :] = (center * inverse * r["gain"][...] + r["bias"][...]).astype(BF)
        own = x_all[blk(b), blk(t)].astype(F32)
        r["normed"][blk(b), :] = (own - mean) * inverse
        r["inv"][blk(b), :] = jnp.broadcast_to(inverse, (BLOCK, 128))

    def turn(v, b, sense):
        cosine = jnp.concatenate([r["cos"][b]] * 2, 1)
        sine = jnp.concatenate([r["sin"][b]] * 2, 1)
        swapped = jnp.where(lane % 2 == 0, pltpu.roll(v, BLOCK - 1, 1), pltpu.roll(v, 1, 1))
        return v * cosine + sense * sine * swapped

    def goes_on(place, b):
        return ((blocks * place + b) // per_pack == (blocks * (place + 1)) // per_pack) & (
            place < count - 1
        )

    def forward(b, which):
        here, there = blk(blocks + b), blk(b)
        if which == 2:
            src, dst = r["kt"].at[blocks + b], r["kt"].at[b]
        else:
            ref = (r["kb"], r["vb"])[which]
            src, dst = ref.at[here], ref.at[there]
        return pltpu.make_async_remote_copy(
            src_ref=src,
            dst_ref=dst,
            send_sem=r["kv_send"].at[b, which],
            recv_sem=r["kv_recv"].at[b, which],
            device_id=(s + 1, t),
            device_id_type=MESH,
        )

    def project(b):
        lnb = ln[blk(b), :]
        r["kt"][blocks + b] = r["tags"][b]
        r["kb"][blk(blocks + b), :] = turn(dot(lnb, wqkv[1]), b, 1.0).astype(BF)
        r["vb"][blk(blocks + b), :] = dot(lnb, wqkv[2]).astype(BF)

        @pl.when(goes_on(s, b))
        def _():
            for which in range(3):
                forward(b, which).start()

        r["q"][blk(b), :] = turn(dot(lnb, wqkv[0]), b, 1.0).astype(BF)

    for b in range(blocks):
        relay(0, b)
    loads["x"].wait()
    for b in range(blocks):
        arrived(0, b)
        norm(b)
        if b == 0:
            loads["wqkv"].wait()
            for b2 in range(blocks):
                loads[("cos", b2)].wait()
                loads[("sin", b2)].wait()
        project(b)

    loads["win"].wait()

    def expand(j):
        for b in range(blocks):
            pre = dot(ln[blk(b), :], win[:, blk(j)]) + r["b_in"][:, blk(j)]
            scale = 0.7978845608028654
            square = pre * pre
            th = jnp.tanh(scale * (pre + 0.044715 * (square * pre)))
            half = 0.5 * (1.0 + th)
            r["act"][blk(b), blk(j)] = (pre * half).astype(BF)
            r["dg"][blk(b), blk(j)] = half + (0.5 * scale) * pre * (1.0 - th * th) * (
                1.0 + (3 * 0.044715) * square
            )

    for j in range(hidden_tiles):
        expand(j)
        if j < blocks:
            relay(1, j)
    loads["g"].wait()
    loads["wout"].wait()
    loads["wo"].wait()
    for b in range(blocks):
        arrived(1, b)

    units = []
    slots = {}
    for u, kind in enumerate(KINDS):
        wide = u < 9
        if wide:
            out, first = (
                (r["wout_out"], u * 256)
                if u < 4
                else (r["win_out"], (u - 4) * 256)
                if u < 8
                else (r["wo_out"], 0)
            )
            args = (r["wide"].at[pl.ds(u * 256, 256)], out, first, 256)
        else:
            args = (r["tall"].at[u - 9], r["qkv_out"].at[u - 9], 0, 1024)
        key = ("wide" if wide else "tall") + ("_x" if kind is PairFirst else "_z")
        slot = slots.get(key, 0)
        slots[key] = slot + 1
        units.append(
            kind(
                ring,
                u,
                *args,
                r["pair_" + key].at[slot],
                r["line_" + key].at[slot],
                r["w_send"],
                r["w_recv"],
                r["w_own"],
            )
        )

    def grad_out_tile(j):
        bin_sum = jnp.zeros((1, BLOCK), F32)
        for b in range(blocks):
            pulled = dot_columns(g_all[blk(b), :], wout[blk(j), :])
            gh = (pulled * r["dg"][blk(b), blk(j)]).astype(BF)
            r["gh"][blk(b), blk(j)] = gh
            bin_sum = bin_sum + jnp.sum(gh.astype(F32), 0, keepdims=True)
        r["vec"][0, 0:1, blk(j)] = bin_sum
        r["wide"][blk(j), :] = dot_rows(r["act"][:, blk(j)], g_all[...]).astype(BF)

    def grad_in_tile(j):
        r["wide"][blk(hidden_tiles + j), :] = dot_rows(ln[:, blk(j)], r["gh"][...]).astype(BF)

    def context_pull():
        for b in range(blocks):
            r["gc"][blk(b), :] = dot_columns(g_all[blk(b), :], wo[...])
        own = g_all[:, blk(t)].astype(F32)
        r["vec"][0, 1:2, blk(2)] = jnp.sum(own, 0, keepdims=True)

    def receive_keys():
        for b in range(blocks):

            @pl.when(goes_on(s - 1, b) & (s > 0))
            def _():
                for which in range(3):
                    forward(b, which).wait_recv()

    def attend(i):
        held = (blocks * s + i) % per_pack + 1
        for nb in range(1, per_pack + 1):

            @pl.when(held == nb)
            def _():
                attend_window(i, nb)

    def attend_window(i, nb):
        n = nb * BLOCK
        first = blocks + i - nb + 1
        if first < 0:
            return
        window = pl.ds(first * BLOCK, n)
        row = lax.broadcasted_iota(jnp.int32, (BLOCK, BLOCK), 0)
        seg = r["seg"][blk(i), :]
        for c in range(nb):
            same = r["kt"][first + c, 0:1, :] == seg
            if c == nb - 1:
                same = (same & (lane <= row)) | (lane == row)
            r["mask"][:, blk(c)] = jnp.where(same, 0.0, -1e30)
        qb = r["q"][blk(i), :]
        gcb = r["gc"][blk(i), :]
        kw = r["kb"][window, :]
        vw = r["vb"][window, :]

        def head(h, carry):
            mine = lane // 64 == h
            at = pl.ds(pl.multiple_of(h * BLOCK, BLOCK), BLOCK)
            qm = jnp.where(mine, qb, jnp.zeros_like(qb))
            r["qm"][at, :] = qm
            logit = dot_columns(qm, kw) * (0.125 * LOG2E) + r["mask"][:, :n]
            ceiling = jnp.floor(jnp.max(logit, -1, keepdims=True))
            weight = jnp.exp2(logit - ceiling)
            total = 1.0 / jnp.sum(weight, -1, keepdims=True)
            low = weight.astype(BF)
            r["wl"][at, :n] = low
            context = dot(low, vw) * total
            gm = jnp.where(mine, gcb, 0.0)
            ga = (gm * total).astype(BF)
            r["gm"][at, :] = ga
            offset = jnp.sum(gm * context, -1, keepdims=True) * total
            ds = (weight * (dot_columns(ga, vw) - offset)).astype(BF)
            r["ds"][at, :n] = ds
            dq = dot(ds, kw)
            ctx, dqs = carry
            return (jnp.where(mine, context, ctx), jnp.where(mine, dq, dqs))

        zero = jnp.zeros((BLOCK, BLOCK), F32)
        ctx, dqs = lax.fori_loop(0, 4, head, (zero, zero))
        r["ctx"][blk(i), :] = ctx.astype(BF)
        r["g3"][blk(i), 0:BLOCK] = turn(0.125 * dqs, i, -1.0).astype(BF)
        for c in range(nb):
            r["dk"][blk(first + c), :] += dot_rows(r["ds"][:, blk(c)], r["qm"][...])
            r["dv"][blk(first + c), :] += dot_rows(r["wl"][:, blk(c)], r["gm"][...])

    def backward(b, which):
        return pltpu.make_async_remote_copy(
            src_ref=r["dks"].at[which, blk(b)],
            dst_ref=r["dkr"].at[which, blk(b)],
            send_sem=r["dk_send"].at[b, which],
            recv_sem=r["dk_recv"].at[b, which],
            device_id=(s - 1, t),
            device_id_type=MESH,
        )

    def send_key_grads():
        for b in range(blocks):

            @pl.when(goes_on(s - 1, b) & (s > 0))
            def _():
                for which, name in enumerate(("dk", "dv")):
                    r["dks"][which, blk(b), :] = r[name][blk(b), :].astype(BF)
                    backward(b, which).start()

    def grad_wo_tile():
        r["wide"][blk(2 * hidden_tiles), :] = dot_rows(r["ctx"][...], g_all[...]).astype(BF)

    def split(which, slot):
        to = mate(t, 2) if slot == 2 else mate(t, 1)
        return pltpu.make_async_remote_copy(
            src_ref=r["tp_out"].at[which, slot],
            dst_ref=r["tp_got"].at[which, slot],
            send_sem=r["tp_send"].at[which, slot],
            recv_sem=r["tp_recv"].at[which, slot],
            device_id=(s, to),
            device_id_type=MESH,
        )

    def share(which, owner, b):
        if which == 0:
            return dot(r["ctx"][blk(b), :], wo[:, blk(owner)]) + dot(
                r["act"][blk(b), :], wout[:, blk(owner)]
            )
        total = dot_columns(r["gh"][blk(b), :], win[blk(owner), :])
        for k in range(3):
            total = total + dot_columns(r["g3"][blk(b), blk(k)], wqkv[k, blk(owner), :])
        return total

    far_mate = mate(mate(t, 1), 2)

    def split_near(which):
        for slot, owner in ((1, far_mate), (0, mate(t, 1))):
            for b in range(blocks):
                r["tp_out"][which, slot, blk(b), :] = share(which, owner, b).astype(BF)
            split(which, slot).start()

    def split_far(which):
        split(which, 1).wait_recv()
        for b in range(blocks):
            mine = share(which, mate(t, 2), b)
            r["tp_out"][which, 2, blk(b), :] = (
                mine + r["tp_got"][which, 1, blk(b), :].astype(F32)
            ).astype(BF)
        split(which, 2).start()

    def split_own(which):
        for b in range(blocks):
            r["tp_sum"][which, blk(b), :] = share(which, t, b)

    def split_join(which):
        split(which, 0).wait_recv()
        split(which, 2).wait_recv()
        for b in range(blocks):
            r["tp_sum"][which, blk(b), :] += r["tp_got"][which, 0, blk(b), :].astype(F32) + r[
                "tp_got"
            ][which, 2, blk(b), :].astype(F32)

    def join_branch():
        split_join(0)
        r["summed"][...] = r["tp_sum"][0]

    def join_key_grads():
        for b in range(blocks):
            for which, name in enumerate(("dk", "dv")):

                @pl.when(goes_on(s, b))
                def _():
                    backward_in = pltpu.make_async_remote_copy(
                        src_ref=r["dks"].at[which, blk(b)],
                        dst_ref=r["dkr"].at[which, blk(b)],
                        send_sem=r["dk_send"].at[b, which],
                        recv_sem=r["dk_recv"].at[b, which],
                        device_id=(s + 1, t),
                        device_id_type=MESH,
                    )
                    backward_in.wait_recv()
                    r[name][blk(blocks + b), :] += r["dkr"][which, blk(b), :].astype(F32)

            r["g3"][blk(b), blk(1)] = turn(0.125 * r["dk"][blk(blocks + b), :], b, -1.0).astype(BF)
            r["g3"][blk(b), blk(2)] = r["dv"][blk(blocks + b), :].astype(BF)

    def grad_qkv_tiles():
        for j in range(width_tiles):
            tile = dot_rows(ln[:, blk(j)], r["g3"][...]).astype(BF)
            for k in range(3):
                r["tall"][k, blk(j), :] = tile[:, k * BLOCK : (k + 1) * BLOCK]

    def stats_copy(level):
        return pltpu.make_async_remote_copy(
            src_ref=r["stats"].at[level],
            dst_ref=r["stats_got"].at[level],
            send_sem=r["st_send"].at[level],
            recv_sem=r["st_recv"].at[level],
            device_id=(s, mate(t, 1 << level)),
            device_id_type=MESH,
        )

    def norm_grad():
        split_join(1)
        gain_sum = jnp.zeros((1, BLOCK), F32)
        bias_sum = jnp.zeros((1, BLOCK), F32)
        lane_one = lax.broadcasted_iota(jnp.int32, (BLOCK, 128), 1)
        for b in range(blocks):
            grad = r["tp_sum"][1, blk(b), :]
            normed = r["normed"][blk(b), :]
            gain_sum = gain_sum + jnp.sum(grad * normed, 0, keepdims=True)
            bias_sum = bias_sum + jnp.sum(grad, 0, keepdims=True)
            hat = grad * gain_own
            first = jnp.sum(hat, -1, keepdims=True)
            second = jnp.sum(hat * normed, -1, keepdims=True)
            both = jnp.where(lane_one == 0, first, second)
            r["stats"][0, :, blk(b)] = both.T[0:8, :]
        r["vec"][0, 1:2, blk(0)] = gain_sum
        r["vec"][0, 1:2, blk(1)] = bias_sum
        stats_copy(0).start()

    def stats_join():
        stats_copy(0).wait_recv()
        r["stats"][1] = r["stats"][0] + r["stats_got"][0]
        stats_copy(1).start()

    def input_grad():
        stats_copy(1).wait_recv()
        for b in range(blocks):
            both = (r["stats"][1, :, blk(b)] + r["stats_got"][1, :, blk(b)]) * (1.0 / ln.shape[1])
            columns = jnp.concatenate([both] * 16, 0).T
            hat = r["tp_sum"][1, blk(b), :] * gain_own
            r["pulled"][blk(b), :] = r["inv"][blk(b), 0:1] * (
                hat - columns[:, 0:1] - r["normed"][blk(b), :] * columns[:, 1:2]
            )

    levels = count.bit_length() - 1

    def vec_copy(level):
        return pltpu.make_async_remote_copy(
            src_ref=r["vec"].at[level],
            dst_ref=r["vec_got"].at[level],
            send_sem=r["v_send"].at[level],
            recv_sem=r["v_recv"].at[level],
            device_id=(mate(s, 1 << level), t),
            device_id_type=MESH,
        )

    def vec_start():
        vec_copy(0).start()

    def vec_step(level):
        vec_copy(level).wait_recv()
        r["vec"][level + 1] = r["vec"][level] + r["vec_got"][level]
        if level + 1 < levels:
            vec_copy(level + 1).start()

    def vec_rest():
        for level in range(2, levels):
            vec_step(level)
        r["vec_out"][...] = r["vec"][levels]

    tasks = {
        "context_pull": context_pull,
        "receive_keys": receive_keys,
        "send_key_grads": send_key_grads,
        "grad_wo": grad_wo_tile,
        "join_branch": join_branch,
        "join_keys": join_key_grads,
        "grad_qkv": grad_qkv_tiles,
        "norm_grad": norm_grad,
        "stats_join": stats_join,
        "input_grad": input_grad,
        "vec_start": vec_start,
        "vec_rest": vec_rest,
    }
    for j in range(hidden_tiles):
        tasks["wout%d" % j] = functools.partial(grad_out_tile, j)
        tasks["win%d" % j] = functools.partial(grad_in_tile, j)
    for i in range(blocks):
        tasks["attend%d" % i] = functools.partial(attend, i)
    for which in (0, 1):
        tasks["near%d" % which] = functools.partial(split_near, which)
        tasks["far%d" % which] = functools.partial(split_far, which)
        tasks["own%d" % which] = functools.partial(split_own, which)
        tasks["vec%d" % which] = functools.partial(vec_step, which)
    r["vec"][0] = jnp.zeros(r["vec"].shape[1:], F32)
    for who, what in STEPS:
        if who < 0:
            tasks[what]()
        else:
            getattr(units[who], what)()

    for unit in units:
        unit.finish()
    for which in (0, 1):
        for b in range(blocks):
            for kind in range(3):
                gather(which, b, kind).wait_send()
        for slot in range(3):
            split(which, slot).wait_send()
        stats_copy(which).wait_send()
    for level in range(levels):
        vec_copy(level).wait_send()
    for b in range(blocks):

        @pl.when(goes_on(s, b))
        def _():
            for which in range(3):
                forward(b, which).wait_send()

        @pl.when(goes_on(s - 1, b) & (s > 0))
        def _():
            for which in range(2):
                backward(b, which).wait_send()


def rotary_tables():
    places = np.arange(PACK, dtype=np.float32)
    inverse = (10000.0 ** (-(np.arange(16, dtype=np.float32) * 2.0) / 32.0)).astype(np.float32)
    phase = (places[:, None] * inverse[None, :]).astype(np.float32)
    cosine, sine = np.cos(phase), np.sin(phase)
    cos_head = np.ones((PACK, 64), np.float32)
    sin_head = np.zeros((PACK, 64), np.float32)
    cos_head[:, 0:32] = np.repeat(cosine, 2, 1)
    sin_head[:, 0:32:2] = -sine
    sin_head[:, 1:32:2] = sine
    shape = (PACK // BLOCK, BLOCK, 128)
    return (
        np.concatenate([cos_head] * 2, 1).reshape(shape),
        np.concatenate([sin_head] * 2, 1).reshape(shape),
    )


def shards(
    x_in, ln_gain, ln_bias, w_qkv, w_o, w_in, b_in, w_out, b_out, grad_out, segment_ids, pad_mask
):
    count = lax.axis_size("seq")
    rows, own_width = x_in.shape
    width = w_in.shape[0]
    hidden = w_in.shape[1]
    blocks = rows // BLOCK
    assert own_width == BLOCK and rows % BLOCK == 0 and w_qkv.shape[2] == BLOCK
    assert hidden == width == 4 * BLOCK and lax.axis_size("tp") == 4 and rows < PACK
    assert count & (count - 1) == 0 and (count * rows) % PACK == 0
    tags = jnp.where(pad_mask == 1, segment_ids, -1)
    tags = jnp.broadcast_to(tags.reshape(blocks, 1, BLOCK), (blocks, 8, BLOCK))
    cos_table, sin_table = rotary_tables()
    levels = count.bit_length() - 1
    pairs = sum(kind is PairFirst for kind in KINDS[:9])
    tall_pairs = sum(kind is PairFirst for kind in KINDS[9:])
    hbm = pl.BlockSpec(memory_space=pl.ANY)
    vmem = pl.BlockSpec(memory_space=pltpu.VMEM)
    vm = pltpu.VMEM
    dma = pltpu.SemaphoreType.DMA
    ins = {
        "x_in": (x_in, hbm),
        "g_in": (grad_out, hbm),
        "gain": (ln_gain.reshape(1, -1), vmem),
        "bias": (ln_bias.reshape(1, -1), vmem),
        "b_in": (b_in.reshape(1, -1), vmem),
        "wqkv_in": (w_qkv, hbm),
        "wo_in": (w_o, hbm),
        "win_in": (w_in, hbm),
        "wout_in": (w_out, hbm),
        "seg": (segment_ids.reshape(-1, 1), vmem),
        "tags": (tags, vmem),
        "cos_in": (jnp.asarray(cos_table), hbm),
        "sin_in": (jnp.asarray(sin_table), hbm),
    }
    outs = {
        "wout_out": (w_out.shape, BF, hbm),
        "win_out": (w_in.shape, BF, hbm),
        "wo_out": (w_o.shape, BF, hbm),
        "qkv_out": (w_qkv.shape, BF, hbm),
        "vec_out": ((8, width), F32, vmem),
        "summed": ((rows, BLOCK), F32, vmem),
        "pulled": ((rows, BLOCK), F32, vmem),
    }
    scratch = {
        "x_all": vm((rows, width), BF),
        "g_all": vm((rows, width), BF),
        "ln": vm((rows, width), BF),
        "wqkv": vm(w_qkv.shape, BF),
        "wo": vm(w_o.shape, BF),
        "win": vm(w_in.shape, BF),
        "wout": vm(w_out.shape, BF),
        "act": vm((rows, hidden), BF),
        "dg": vm((rows, hidden), F32),
        "gh": vm((rows, hidden), BF),
        "q": vm((rows, BLOCK), BF),
        "kb": vm((2 * rows, BLOCK), BF),
        "vb": vm((2 * rows, BLOCK), BF),
        "kt": vm((2 * blocks, 8, BLOCK), jnp.int32),
        "gc": vm((rows, BLOCK), F32),
        "dk": vm((2 * rows, BLOCK), F32),
        "dv": vm((2 * rows, BLOCK), F32),
        "ctx": vm((rows, BLOCK), BF),
        "g3": vm((rows, 3 * BLOCK), BF),
        "mask": vm((BLOCK, PACK), F32),
        "ds": vm((4 * BLOCK, PACK), BF),
        "wl": vm((4 * BLOCK, PACK), BF),
        "qm": vm((4 * BLOCK, BLOCK), BF),
        "gm": vm((4 * BLOCK, BLOCK), BF),
        "dks": vm((2, rows, BLOCK), BF),
        "dkr": vm((2, rows, BLOCK), BF),
        "tp_out": vm((2, 3, rows, BLOCK), BF),
        "tp_got": vm((2, 3, rows, BLOCK), BF),
        "tp_sum": vm((2, rows, BLOCK), F32),
        "normed": vm((rows, BLOCK), F32),
        "inv": vm((rows, 128), F32),
        "cos": vm((blocks, BLOCK, 128), F32),
        "sin": vm((blocks, BLOCK, 128), F32),
        "stats": vm((2, 8, rows), F32),
        "stats_got": vm((2, 8, rows), F32),
        "vec": vm((levels + 1, 8, width), F32),
        "vec_got": vm((levels, 8, width), F32),
        "wide": vm((9 * 256, 1024), BF),
        "tall": vm((3, 1024, 256), BF),
        "pair_wide_x": vm((max(pairs, 1), 128, 1024), BF),
        "line_wide_x": vm((max(pairs, 1), 2, 64, 1024), BF),
        "pair_wide_z": vm((max(9 - pairs, 1), 64, 1024), BF),
        "line_wide_z": vm((max(9 - pairs, 1), 2, 128, 1024), BF),
        "pair_tall_x": vm((max(tall_pairs, 1), 512, 256), BF),
        "line_tall_x": vm((max(tall_pairs, 1), 2, 256, 256), BF),
        "pair_tall_z": vm((max(3 - tall_pairs, 1), 256, 256), BF),
        "line_tall_z": vm((max(3 - tall_pairs, 1), 2, 512, 256), BF),
        "load_sem": dma((6 + 2 * blocks,)),
        "ag_send": dma((2, blocks, 3)),
        "ag_recv": dma((2, blocks, 3)),
        "kv_send": dma((blocks, 3)),
        "kv_recv": dma((blocks, 3)),
        "dk_send": dma((blocks, 2)),
        "dk_recv": dma((blocks, 2)),
        "tp_send": dma((2, 3)),
        "tp_recv": dma((2, 3)),
        "st_send": dma((2,)),
        "st_recv": dma((2,)),
        "v_send": dma((levels,)),
        "v_recv": dma((levels,)),
        "w_send": dma((12, 8)),
        "w_recv": dma((12, 8)),
        "w_own": dma((12,)),
    }
    names = list(ins) + list(outs) + list(scratch)
    wout, win, wo, qkv, vec, summed, pulled = pl.pallas_call(
        functools.partial(layer_kernel, count, rows, names),
        out_shape=[jax.ShapeDtypeStruct(o[0], o[1]) for o in outs.values()],
        in_specs=[i[1] for i in ins.values()],
        out_specs=[o[2] for o in outs.values()],
        scratch_shapes=list(scratch.values()),
        compiler_params=pltpu.CompilerParams(
            collective_id=0, has_side_effects=True, vmem_limit_bytes=62 * 2**20
        ),
    )(*[i[0] for i in ins.values()])
    mixed = (x_in.astype(F32) + summed + b_out).astype(BF)
    grad_input = pulled + grad_out.astype(F32)
    return (
        mixed,
        grad_input,
        vec[1, 0:256],
        vec[1, 256:512],
        qkv.astype(F32),
        wo.astype(F32),
        win.astype(F32),
        vec[0],
        wout.astype(F32),
        vec[1, 512:768],
    )


def solution(mesh):
    return jax.shard_map(
        shards,
        mesh=mesh,
        in_specs=(
            P("seq", "tp"),
            P(),
            P(),
            P(None, None, "tp"),
            P("tp", None),
            P(None, "tp"),
            P("tp"),
            P("tp", None),
            P("tp"),
            P("seq", "tp"),
            P("seq"),
            P("seq"),
        ),
        out_specs=(
            P("seq", "tp"),
            P("seq", "tp"),
            P("tp"),
            P("tp"),
            P(None, None, "tp"),
            P("tp", None),
            P(None, "tp"),
            P("tp"),
            P("tp", None),
            P("tp"),
        ),
        check_vma=False,
    )
```

```python
import functools

import jax
import jax.numpy as jnp
import numpy as np
from jax import lax
from jax.experimental import pallas as pl
from jax.experimental.pallas import tpu as pltpu
from jax.sharding import PartitionSpec as P

PACK = 1024
LOG2E = 1.4426950408889634
EPSILON = 1e-05
BLOCK = 256
MESH = pl.DeviceIdType.MESH
BF = jnp.bfloat16
F32 = jnp.float32


class Ring:
    def __init__(self, seq_count):
        self.count = seq_count
        self.m = seq_count // 2
        self.s = lax.axis_index("seq")
        self.t = lax.axis_index("tp")
        self.z = self.s // 2
        self.x = self.s % 2
        low = (self.z < self.m // 2).astype(jnp.int32)
        self.near = low
        self.far = 1 - low

    def at(self, z, x):
        return (z * 2 + x, self.t)

    def peer(self):
        return self.at(self.z, 1 - self.x)

    def step(self, piece, sign):
        return self.at(self.z + sign * (2 * piece - 1), self.x)

    def first(self, piece):
        return self.z == (1 - piece) * (self.m - 1)

    def last(self, piece):
        return self.z == piece * (self.m - 1)


def aligned(value):
    return pl.multiple_of(value, 16)


def add_rows(acc, acc_first, got, rows):
    step = 16 if rows % 32 else 32

    def body(i, carry):
        at = pl.ds(aligned(acc_first + i * step), step)
        here = pl.ds(aligned(i * step), step)
        acc[at, :] = (acc[at, :].astype(jnp.float32) + got[here, :].astype(jnp.float32)).astype(
            acc.dtype
        )
        return carry

    lax.fori_loop(0, rows // step, body, 0)


class Unit:
    def __init__(self, ring, index, part, out, out_first, rows, pair_buf, line_buf, send, recv, own):
        self.r, self.u = ring, index
        self.part, self.out, self.out_first, self.rows = part, out, out_first, rows
        self.pair_buf, self.line_buf = pair_buf, line_buf
        self.send, self.recv, self.own = send, recv, own

    def copy(self, src, dst, kind, to):
        return pltpu.make_async_remote_copy(
            src_ref=src,
            dst_ref=dst,
            send_sem=self.send.at[self.u, kind],
            recv_sem=self.recv.at[self.u, kind],
            device_id=to,
            device_id_type=MESH,
        )

    def p(self, first, rows):
        return self.part.at[pl.ds(aligned(first), rows)]

    def o(self, first, rows):
        return self.out.at[pl.ds(aligned(self.out_first + first), rows)]

    def keep(self, first, rows):
        return pltpu.make_async_copy(self.p(first, rows), self.o(first, rows), self.own.at[self.u])


class PairFirst(Unit):
    def pair(self):
        half = self.rows // 2
        return self.copy(self.p((1 - self.r.x) * half, half), self.pair_buf, 0, self.r.peer())

    def first_row(self, piece, member):
        return member * (self.rows // 2) + piece * (self.rows // 4)

    def line(self, piece):
        quarter = self.rows // 4
        return self.copy(
            self.p(self.first_row(piece, self.r.x), quarter),
            self.line_buf.at[piece],
            1 + piece,
            self.r.step(piece, 1),
        )

    def back(self, piece, origin):
        quarter = self.rows // 4
        row = self.first_row(piece, self.r.x)
        src = self.p(row, quarter) if origin else self.o(row, quarter)
        return self.copy(src, self.o(row, quarter), 3 + piece, self.r.step(piece, -1))

    def over(self, piece, origin):
        quarter = self.rows // 4
        row = self.first_row(piece, self.r.x)
        src = self.p(row, quarter) if origin else self.o(row, quarter)
        return self.copy(src, self.o(row, quarter), 5 + piece, self.r.peer())

    def start(self):
        self.pair().start()

    def paired(self):
        half = self.rows // 2
        self.pair().wait_recv()
        add_rows(self.part, self.r.x * half, self.pair_buf, half)
        piece = self.r.near

        @pl.when(self.r.first(piece))
        def _():
            self.line(piece).start()

    def chain_near(self):
        piece = self.r.near

        @pl.when(jnp.logical_not(self.r.first(piece)))
        def _():
            self.line(piece).wait_recv()
            add_rows(
                self.part, self.first_row(piece, self.r.x), self.line_buf.at[piece], self.rows // 4
            )
            self.line(piece).start()

    def chain_far(self):
        piece = self.r.far
        self.line(piece).wait_recv()
        add_rows(self.part, self.first_row(piece, self.r.x), self.line_buf.at[piece], self.rows // 4)

        @pl.when(jnp.logical_not(self.r.last(piece)))
        def _():
            self.line(piece).start()

        @pl.when(self.r.last(piece))
        def _():
            self.back(piece, True).start()
            self.over(piece, True).start()
            self.keep(self.first_row(piece, self.r.x), self.rows // 4).start()

    def exchanged(self):
        pass

    def back_near(self):
        piece = self.r.far

        @pl.when(jnp.logical_not(self.r.last(piece)))
        def _():
            self.back(piece, False).wait_recv()
            self.back(piece, False).start()
            self.over(piece, False).start()

    def back_far(self):
        piece = self.r.near
        self.back(piece, False).wait_recv()

        @pl.when(jnp.logical_not(self.r.first(piece)))
        def _():
            self.back(piece, False).start()

        self.over(piece, False).start()

    def finish(self):
        quarter = self.rows // 4
        for piece in (0, 1):
            row = self.first_row(piece, 1 - self.r.x)
            self.copy(self.o(row, quarter), self.o(row, quarter), 5 + piece, self.r.peer()).wait_recv()
        self.pair().wait_send()
        for piece in (0, 1):

            @pl.when(jnp.logical_not(self.r.last(piece)))
            def _():
                self.line(piece).wait_send()

            @pl.when(jnp.logical_not(self.r.first(piece)))
            def _():
                self.back(piece, False).wait_send()

            self.over(piece, False).wait_send()

        @pl.when(self.r.last(self.r.far))
        def _():
            self.keep(self.first_row(self.r.far, self.r.x), quarter).wait()


class LineFirst(Unit):
    def line(self, piece):
        half = self.rows // 2
        return self.copy(
            self.p(piece * half, half), self.line_buf.at[piece], 1 + piece, self.r.step(piece, 1)
        )

    def row_of(self, piece, member):
        return piece * (self.rows // 2) + member * (self.rows // 4)

    def pair(self, piece):
        quarter = self.rows // 4
        return self.copy(
            self.p(self.row_of(piece, 1 - self.r.x), quarter), self.pair_buf, 0, self.r.peer()
        )

    def over(self, piece, member, origin):
        quarter = self.rows // 4
        row = self.row_of(piece, member)
        src = self.p(row, quarter) if origin else self.o(row, quarter)
        return self.copy(src, self.o(row, quarter), 3, self.r.peer())

    def back(self, piece, member, origin):
        quarter = self.rows // 4
        row = self.row_of(piece, member)
        src = self.p(row, quarter) if origin else self.o(row, quarter)
        return self.copy(src, self.o(row, quarter), 4 + 2 * piece + member, self.r.step(piece, -1))

    def start(self):
        piece = self.r.near

        @pl.when(self.r.first(piece))
        def _():
            self.line(piece).start()

    def paired(self):
        pass

    def chain_near(self):
        piece = self.r.near

        @pl.when(jnp.logical_not(self.r.first(piece)))
        def _():
            self.line(piece).wait_recv()
            add_rows(self.part, piece * (self.rows // 2), self.line_buf.at[piece], self.rows // 2)
            self.line(piece).start()

    def chain_far(self):
        piece = self.r.far
        self.line(piece).wait_recv()
        add_rows(self.part, piece * (self.rows // 2), self.line_buf.at[piece], self.rows // 2)

        @pl.when(jnp.logical_not(self.r.last(piece)))
        def _():
            self.line(piece).start()

        @pl.when(self.r.last(piece))
        def _():
            self.pair(piece).start()

    def exchanged(self):
        piece = self.r.far
        quarter = self.rows // 4

        @pl.when(self.r.last(piece))
        def _():
            self.pair(piece).wait_recv()
            row = self.row_of(piece, self.r.x)
            add_rows(self.part, row, self.pair_buf, quarter)
            self.over(piece, self.r.x, True).start()
            self.back(piece, self.r.x, True).start()
            self.keep(row, quarter).start()

    def back_near(self):
        piece = self.r.far
        other = 1 - self.r.x

        @pl.when(self.r.last(piece))
        def _():
            self.over(piece, other, False).wait_recv()
            self.back(piece, other, False).start()

        @pl.when(jnp.logical_not(self.r.last(piece)))
        def _():
            for member in (self.r.x, other):
                self.back(piece, member, False).wait_recv()
                self.back(piece, member, False).start()

    def back_far(self):
        piece = self.r.near
        for member in (self.r.x, 1 - self.r.x):
            self.back(piece, member, False).wait_recv()

            @pl.when(jnp.logical_not(self.r.first(piece)))
            def _():
                self.back(piece, member, False).start()

    def finish(self):
        quarter = self.rows // 4
        for piece in (0, 1):

            @pl.when(jnp.logical_not(self.r.last(piece)))
            def _():
                self.line(piece).wait_send()

            @pl.when(jnp.logical_not(self.r.first(piece)))
            def _():
                for member in (0, 1):
                    self.back(piece, member, False).wait_send()

        piece = self.r.far

        @pl.when(self.r.last(piece))
        def _():
            self.pair(piece).wait_send()
            self.over(piece, self.r.x, False).wait_send()
            self.keep(self.row_of(piece, self.r.x), quarter).wait()


KINDS = (
    PairFirst,
    PairFirst,
    LineFirst,
    PairFirst,
    PairFirst,
    LineFirst,
    PairFirst,
    PairFirst,
    PairFirst,
    PairFirst,
    PairFirst,
    PairFirst,
)

STEPS = (
    (-1, "wout0"),
    (0, "start"),
    (-1, "wout3"),
    (-1, "wout2"),
    (-1, "context_pull"),
    (3, "start"),
    (-1, "wout1"),
    (-1, "receive_keys"),
    (-1, "win0"),
    (4, "start"),
    (-1, "win3"),
    (7, "start"),
    (-1, "attend1"),
    (2, "start"),
    (1, "start"),
    (-1, "attend2"),
    (2, "chain_near"),
    (-1, "win2"),
    (-1, "win1"),
    (6, "start"),
    (4, "paired"),
    (0, "paired"),
    (4, "chain_near"),
    (-1, "attend0"),
    (7, "paired"),
    (-1, "send_key_grads"),
    (1, "paired"),
    (5, "start"),
    (-1, "grad_wo"),
    (2, "chain_far"),
    (8, "start"),
    (1, "chain_near"),
    (3, "paired"),
    (0, "chain_near"),
    (4, "chain_far"),
    (1, "chain_far"),
    (7, "chain_near"),
    (6, "paired"),
    (-1, "join_keys"),
    (-1, "grad_qkv"),
    (11, "start"),
    (3, "chain_near"),
    (10, "start"),
    (5, "chain_near"),
    (4, "back_near"),
    (-1, "near1"),
    (8, "paired"),
    (6, "chain_near"),
    (9, "start"),
    (3, "chain_far"),
    (0, "chain_far"),
    (1, "back_near"),
    (5, "chain_far"),
    (2, "exchanged"),
    (8, "chain_near"),
    (10, "paired"),
    (-1, "near0"),
    (7, "chain_far"),
    (3, "back_near"),
    (11, "paired"),
    (-1, "far1"),
    (1, "back_far"),
    (6, "chain_far"),
    (9, "paired"),
    (4, "back_far"),
    (5, "exchanged"),
    (0, "back_near"),
    (8, "chain_far"),
    (10, "chain_near"),
    (3, "back_far"),
    (10, "chain_far"),
    (11, "chain_near"),
    (0, "back_far"),
    (-1, "own1"),
    (6, "back_near"),
    (-1, "norm_grad"),
    (-1, "vec_start"),
    (9, "chain_near"),
    (11, "chain_far"),
    (7, "back_near"),
    (-1, "stats_join"),
    (6, "back_far"),
    (8, "back_near"),
    (9, "chain_far"),
    (-1, "input_grad"),
    (-1, "vec0"),
    (10, "back_near"),
    (7, "back_far"),
    (11, "back_near"),
    (5, "back_near"),
    (2, "back_near"),
    (11, "back_far"),
    (9, "back_near"),
    (8, "back_far"),
    (-1, "vec1"),
    (-1, "far0"),
    (5, "back_far"),
    (10, "back_far"),
    (9, "back_far"),
    (-1, "own0"),
    (-1, "vec_rest"),
    (2, "back_far"),
    (-1, "join_branch"),
)


def greet(ring):
    barrier = pltpu.get_barrier_semaphore()
    s, t, count = ring.s, ring.t, ring.count

    def signal(to):
        pl.semaphore_signal(barrier, inc=1, device_id=to, device_id_type=MESH)

    signal((s, mate(t, 1)))
    signal((s, mate(t, 2)))
    total = jnp.int32(2)
    bit = 1
    while bit < count:
        signal((mate(s, bit), t))
        total = total + 1
        bit *= 2
    for hop in (-2, -1, 1, 2):
        ok = (s + hop >= 0) & (s + hop < count)

        @pl.when(ok)
        def _():
            signal((s + hop, t))

        total = total + ok.astype(jnp.int32)
    pl.semaphore_wait(barrier, total)


def mate(place, bit):
    return place + bit - 2 * bit * ((place // bit) % 2)


def dot(a, b):
    return jnp.dot(a, b, preferred_element_type=F32)


def dot_rows(a, b):
    return lax.dot_general(a, b, (((0,), (0,)), ((), ())), preferred_element_type=F32)


def dot_columns(a, b):
    return lax.dot_general(a, b, (((1,), (1,)), ((), ())), preferred_element_type=F32)


def layer_kernel(
    count, rows, names, *refs
):
    r = dict(zip(names, refs))
    ring = Ring(count)
    s, t = ring.s, ring.t
    blocks = rows // BLOCK
    per_pack = PACK // BLOCK
    x_all, g_all, ln = r["x_all"], r["g_all"], r["ln"]
    wqkv, wo, win, wout = r["wqkv"], r["wo"], r["win"], r["wout"]
    hidden_tiles = win.shape[1] // BLOCK
    width_tiles = win.shape[0] // BLOCK

    def blk(b):
        return pl.ds(b * BLOCK, BLOCK) if isinstance(b, int) else pl.ds(pl.multiple_of(b * BLOCK, BLOCK), BLOCK)

    loads = {}

    def load(name, src, dst):
        copy = pltpu.make_async_copy(src, dst, r["load_sem"].at[len(loads)])
        loads[name] = copy
        copy.start()

    load("x", r["x_in"], x_all.at[:, blk(t)])
    load("wqkv", r["wqkv_in"], wqkv)
    load("win", r["win_in"], win)
    load("g", r["g_in"], g_all.at[:, blk(t)])
    load("wout", r["wout_in"], wout)
    load("wo", r["wo_in"], wo)
    for b in range(blocks):
        place = (blocks * s + b) % per_pack
        load(("cos", b), r["cos_in"].at[place], r["cos"].at[b])
        load(("sin", b), r["sin_in"].at[place], r["sin"].at[b])
    greet(ring)

    def gather(which, b, kind):
        src_ref, whole = ((r["x_in"], x_all), (r["g_in"], g_all))[which]
        to = mate(t, 2) if kind == 1 else mate(t, 1)
        shard = mate(t, 2) if kind == 2 else t
        dst = whole.at[blk(b), blk(shard)]
        src = dst if kind == 2 else src_ref.at[blk(b)]
        return pltpu.make_async_remote_copy(
            src_ref=src,
            dst_ref=dst,
            send_sem=r["ag_send"].at[which, b, kind],
            recv_sem=r["ag_recv"].at[which, b, kind],
            device_id=(s, to),
            device_id_type=MESH,
        )

    for which in (0, 1):
        for b in range(blocks):
            gather(which, b, 1).start()
            gather(which, b, 0).start()
    r["dk"][...] = jnp.zeros(r["dk"].shape, F32)
    r["dv"][...] = jnp.zeros(r["dv"].shape, F32)

    def relay(which, b):
        gather(which, b, 1).wait_recv()
        gather(which, b, 2).start()

    def arrived(which, b):
        gather(which, b, 0).wait_recv()
        gather(which, b, 2).wait_recv()

    lane = lax.broadcasted_iota(jnp.int32, (BLOCK, BLOCK), 1)
    gain_own = r["gain"][:, blk(t)]

    def norm(b):
        xb = x_all[blk(b), :].astype(F32)
        mean = jnp.mean(xb, -1, keepdims=True)
        center = xb - mean
        inverse = lax.rsqrt(jnp.mean(center * center, -1, keepdims=True) + EPSILON)
        ln[blk(b), :] = (center * inverse * r["gain"][...] + r["bias"][...]).astype(BF)
        own = x_all[blk(b), blk(t)].astype(F32)
        r["normed"][blk(b), :] = (own - mean) * inverse
        r["inv"][blk(b), :] = jnp.broadcast_to(inverse, (BLOCK, 128))

    def turn(v, b, sense):
        cosine = jnp.concatenate([r["cos"][b]] * 2, 1)
        sine = jnp.concatenate([r["sin"][b]] * 2, 1)
        swapped = jnp.where(lane % 2 == 0, pltpu.roll(v, BLOCK - 1, 1), pltpu.roll(v, 1, 1))
        return v * cosine + sense * sine * swapped

    def goes_on(place, b):
        return ((blocks * place + b) // per_pack == (blocks * (place + 1)) // per_pack) & (
            place < count - 1
        )

    def forward(b, which):
        here, there = blk(blocks + b), blk(b)
        if which == 2:
            src, dst = r["kt"].at[blocks + b], r["kt"].at[b]
        else:
            ref = (r["kb"], r["vb"])[which]
            src, dst = ref.at[here], ref.at[there]
        return pltpu.make_async_remote_copy(
            src_ref=src,
            dst_ref=dst,
            send_sem=r["kv_send"].at[b, which],
            recv_sem=r["kv_recv"].at[b, which],
            device_id=(s + 1, t),
            device_id_type=MESH,
        )

    def project(b):
        lnb = ln[blk(b), :]
        r["kt"][blocks + b] = r["tags"][b]
        r["kb"][blk(blocks + b), :] = turn(dot(lnb, wqkv[1]), b, 1.0).astype(BF)
        r["vb"][blk(blocks + b), :] = dot(lnb, wqkv[2]).astype(BF)

        @pl.when(goes_on(s, b))
        def _():
            for which in range(3):
                forward(b, which).start()

        r["q"][blk(b), :] = turn(dot(lnb, wqkv[0]), b, 1.0).astype(BF)

    for b in range(blocks):
        relay(0, b)
    loads["x"].wait()
    for b in range(blocks):
        arrived(0, b)
        norm(b)
        if b == 0:
            loads["wqkv"].wait()
            for b2 in range(blocks):
                loads[("cos", b2)].wait()
                loads[("sin", b2)].wait()
        project(b)

    loads["win"].wait()

    def expand(j):
        for b in range(blocks):
            pre = dot(ln[blk(b), :], win[:, blk(j)]) + r["b_in"][:, blk(j)]
            scale = 0.7978845608028654
            square = pre * pre
            th = jnp.tanh(scale * (pre + 0.044715 * (square * pre)))
            half = 0.5 * (1.0 + th)
            r["act"][blk(b), blk(j)] = (pre * half).astype(BF)
            r["dg"][blk(b), blk(j)] = half + (0.5 * scale) * pre * (1.0 - th * th) * (
                1.0 + (3 * 0.044715) * square
            )

    for j in range(hidden_tiles):
        expand(j)
        if j < blocks:
            relay(1, j)
    loads["g"].wait()
    loads["wout"].wait()
    loads["wo"].wait()
    for b in range(blocks):
        arrived(1, b)

    units = []
    slots = {}
    for u, kind in enumerate(KINDS):
        wide = u < 9
        if wide:
            out, first = (
                (r["wout_out"], u * 256)
                if u < 4
                else (r["win_out"], (u - 4) * 256)
                if u < 8
                else (r["wo_out"], 0)
            )
            args = (r["wide"].at[pl.ds(u * 256, 256)], out, first, 256)
        else:
            args = (r["tall"].at[u - 9], r["qkv_out"].at[u - 9], 0, 1024)
        key = ("wide" if wide else "tall") + ("_x" if kind is PairFirst else "_z")
        slot = slots.get(key, 0)
        slots[key] = slot + 1
        units.append(
            kind(
                ring,
                u,
                *args,
                r["pair_" + key].at[slot],
                r["line_" + key].at[slot],
                r["w_send"],
                r["w_recv"],
                r["w_own"],
            )
        )

    def grad_out_tile(j):
        bin_sum = jnp.zeros((1, BLOCK), F32)
        for b in range(blocks):
            pulled = dot_columns(g_all[blk(b), :], wout[blk(j), :])
            gh = (pulled * r["dg"][blk(b), blk(j)]).astype(BF)
            r["gh"][blk(b), blk(j)] = gh
            bin_sum = bin_sum + jnp.sum(gh.astype(F32), 0, keepdims=True)
        r["vec"][0, 0:1, blk(j)] = bin_sum
        r["wide"][blk(j), :] = dot_rows(r["act"][:, blk(j)], g_all[...]).astype(BF)

    def grad_in_tile(j):
        r["wide"][blk(hidden_tiles + j), :] = dot_rows(ln[:, blk(j)], r["gh"][...]).astype(BF)

    def context_pull():
        for b in range(blocks):
            r["gc"][blk(b), :] = dot_columns(g_all[blk(b), :], wo[...])
        own = g_all[:, blk(t)].astype(F32)
        r["vec"][0, 1:2, blk(2)] = jnp.sum(own, 0, keepdims=True)

    def receive_keys():
        for b in range(blocks):

            @pl.when(goes_on(s - 1, b) & (s > 0))
            def _():
                for which in range(3):
                    forward(b, which).wait_recv()

    def attend(i):
        held = (blocks * s + i) % per_pack + 1
        for nb in range(1, per_pack + 1):

            @pl.when(held == nb)
            def _():
                attend_window(i, nb)

    def attend_window(i, nb):
        n = nb * BLOCK
        first = blocks + i - nb + 1
        if first < 0:
            return
        window = pl.ds(first * BLOCK, n)
        row = lax.broadcasted_iota(jnp.int32, (BLOCK, BLOCK), 0)
        seg = r["seg"][blk(i), :]
        for c in range(nb):
            same = r["kt"][first + c, 0:1, :] == seg
            if c == nb - 1:
                same = (same & (lane <= row)) | (lane == row)
            r["mask"][:, blk(c)] = jnp.where(same, 0.0, -1e30)
        qb = r["q"][blk(i), :]
        gcb = r["gc"][blk(i), :]
        kw = r["kb"][window, :]
        vw = r["vb"][window, :]

        def head(h, carry):
            mine = lane // 64 == h
            at = pl.ds(pl.multiple_of(h * BLOCK, BLOCK), BLOCK)
            qm = jnp.where(mine, qb, jnp.zeros_like(qb))
            r["qm"][at, :] = qm
            logit = dot_columns(qm, kw) * (0.125 * LOG2E) + r["mask"][:, :n]
            ceiling = jnp.floor(jnp.max(logit, -1, keepdims=True))
            weight = jnp.exp2(logit - ceiling)
            total = 1.0 / jnp.sum(weight, -1, keepdims=True)
            low = weight.astype(BF)
            r["wl"][at, :n] = low
            context = dot(low, vw) * total
            gm = jnp.where(mine, gcb, 0.0)
            ga = (gm * total).astype(BF)
            r["gm"][at, :] = ga
            offset = jnp.sum(gm * context, -1, keepdims=True) * total
            ds = (weight * (dot_columns(ga, vw) - offset)).astype(BF)
            r["ds"][at, :n] = ds
            dq = dot(ds, kw)
            ctx, dqs = carry
            return (jnp.where(mine, context, ctx), jnp.where(mine, dq, dqs))

        zero = jnp.zeros((BLOCK, BLOCK), F32)
        ctx, dqs = lax.fori_loop(0, 4, head, (zero, zero))
        r["ctx"][blk(i), :] = ctx.astype(BF)
        r["g3"][blk(i), 0:BLOCK] = turn(0.125 * dqs, i, -1.0).astype(BF)
        for c in range(nb):
            r["dk"][blk(first + c), :] += dot_rows(r["ds"][:, blk(c)], r["qm"][...])
            r["dv"][blk(first + c), :] += dot_rows(r["wl"][:, blk(c)], r["gm"][...])

    def backward(b, which):
        return pltpu.make_async_remote_copy(
            src_ref=r["dks"].at[which, blk(b)],
            dst_ref=r["dkr"].at[which, blk(b)],
            send_sem=r["dk_send"].at[b, which],
            recv_sem=r["dk_recv"].at[b, which],
            device_id=(s - 1, t),
            device_id_type=MESH,
        )

    def send_key_grads():
        for b in range(blocks):

            @pl.when(goes_on(s - 1, b) & (s > 0))
            def _():
                for which, name in enumerate(("dk", "dv")):
                    r["dks"][which, blk(b), :] = r[name][blk(b), :].astype(BF)
                    backward(b, which).start()

    def grad_wo_tile():
        r["wide"][blk(2 * hidden_tiles), :] = dot_rows(r["ctx"][...], g_all[...]).astype(BF)

    def split(which, slot):
        to = mate(t, 2) if slot == 2 else mate(t, 1)
        return pltpu.make_async_remote_copy(
            src_ref=r["tp_out"].at[which, slot],
            dst_ref=r["tp_got"].at[which, slot],
            send_sem=r["tp_send"].at[which, slot],
            recv_sem=r["tp_recv"].at[which, slot],
            device_id=(s, to),
            device_id_type=MESH,
        )

    def share(which, owner, b):
        if which == 0:
            return dot(r["ctx"][blk(b), :], wo[:, blk(owner)]) + dot(
                r["act"][blk(b), :], wout[:, blk(owner)]
            )
        total = dot_columns(r["gh"][blk(b), :], win[blk(owner), :])
        for k in range(3):
            total = total + dot_columns(r["g3"][blk(b), blk(k)], wqkv[k, blk(owner), :])
        return total

    far_mate = mate(mate(t, 1), 2)

    def split_near(which):
        for slot, owner in ((1, far_mate), (0, mate(t, 1))):
            for b in range(blocks):
                r["tp_out"][which, slot, blk(b), :] = share(which, owner, b).astype(BF)
            split(which, slot).start()

    def split_far(which):
        split(which, 1).wait_recv()
        for b in range(blocks):
            mine = share(which, mate(t, 2), b)
            r["tp_out"][which, 2, blk(b), :] = (
                mine + r["tp_got"][which, 1, blk(b), :].astype(F32)
            ).astype(BF)
        split(which, 2).start()

    def split_own(which):
        for b in range(blocks):
            r["tp_sum"][which, blk(b), :] = share(which, t, b)

    def split_join(which):
        split(which, 0).wait_recv()
        split(which, 2).wait_recv()
        for b in range(blocks):
            r["tp_sum"][which, blk(b), :] += r["tp_got"][which, 0, blk(b), :].astype(F32) + r[
                "tp_got"
            ][which, 2, blk(b), :].astype(F32)

    def join_branch():
        split_join(0)
        r["summed"][...] = r["tp_sum"][0]

    def join_key_grads():
        for b in range(blocks):
            for which, name in enumerate(("dk", "dv")):

                @pl.when(goes_on(s, b))
                def _():
                    backward_in = pltpu.make_async_remote_copy(
                        src_ref=r["dks"].at[which, blk(b)],
                        dst_ref=r["dkr"].at[which, blk(b)],
                        send_sem=r["dk_send"].at[b, which],
                        recv_sem=r["dk_recv"].at[b, which],
                        device_id=(s + 1, t),
                        device_id_type=MESH,
                    )
                    backward_in.wait_recv()
                    r[name][blk(blocks + b), :] += r["dkr"][which, blk(b), :].astype(F32)

            r["g3"][blk(b), blk(1)] = turn(0.125 * r["dk"][blk(blocks + b), :], b, -1.0).astype(BF)
            r["g3"][blk(b), blk(2)] = r["dv"][blk(blocks + b), :].astype(BF)

    def grad_qkv_tiles():
        for j in range(width_tiles):
            tile = dot_rows(ln[:, blk(j)], r["g3"][...]).astype(BF)
            for k in range(3):
                r["tall"][k, blk(j), :] = tile[:, k * BLOCK : (k + 1) * BLOCK]

    def stats_copy(level):
        return pltpu.make_async_remote_copy(
            src_ref=r["stats"].at[level],
            dst_ref=r["stats_got"].at[level],
            send_sem=r["st_send"].at[level],
            recv_sem=r["st_recv"].at[level],
            device_id=(s, mate(t, 1 << level)),
            device_id_type=MESH,
        )

    def norm_grad():
        split_join(1)
        gain_sum = jnp.zeros((1, BLOCK), F32)
        bias_sum = jnp.zeros((1, BLOCK), F32)
        lane_one = lax.broadcasted_iota(jnp.int32, (BLOCK, 128), 1)
        for b in range(blocks):
            grad = r["tp_sum"][1, blk(b), :]
            normed = r["normed"][blk(b), :]
            gain_sum = gain_sum + jnp.sum(grad * normed, 0, keepdims=True)
            bias_sum = bias_sum + jnp.sum(grad, 0, keepdims=True)
            hat = grad * gain_own
            first = jnp.sum(hat, -1, keepdims=True)
            second = jnp.sum(hat * normed, -1, keepdims=True)
            both = jnp.where(lane_one == 0, first, second)
            r["stats"][0, :, blk(b)] = both.T[0:8, :]
        r["vec"][0, 1:2, blk(0)] = gain_sum
        r["vec"][0, 1:2, blk(1)] = bias_sum
        stats_copy(0).start()

    def stats_join():
        stats_copy(0).wait_recv()
        r["stats"][1] = r["stats"][0] + r["stats_got"][0]
        stats_copy(1).start()

    def input_grad():
        stats_copy(1).wait_recv()
        for b in range(blocks):
            both = (r["stats"][1, :, blk(b)] + r["stats_got"][1, :, blk(b)]) * (1.0 / ln.shape[1])
            columns = jnp.concatenate([both] * 16, 0).T
            hat = r["tp_sum"][1, blk(b), :] * gain_own
            r["pulled"][blk(b), :] = r["inv"][blk(b), 0:1] * (
                hat - columns[:, 0:1] - r["normed"][blk(b), :] * columns[:, 1:2]
            )

    levels = count.bit_length() - 1

    def vec_copy(level):
        return pltpu.make_async_remote_copy(
            src_ref=r["vec"].at[level],
            dst_ref=r["vec_got"].at[level],
            send_sem=r["v_send"].at[level],
            recv_sem=r["v_recv"].at[level],
            device_id=(mate(s, 1 << level), t),
            device_id_type=MESH,
        )

    def vec_start():
        vec_copy(0).start()

    def vec_step(level):
        vec_copy(level).wait_recv()
        r["vec"][level + 1] = r["vec"][level] + r["vec_got"][level]
        if level + 1 < levels:
            vec_copy(level + 1).start()

    def vec_rest():
        for level in range(2, levels):
            vec_step(level)
        r["vec_out"][...] = r["vec"][levels]

    tasks = {
        "context_pull": context_pull,
        "receive_keys": receive_keys,
        "send_key_grads": send_key_grads,
        "grad_wo": grad_wo_tile,
        "join_branch": join_branch,
        "join_keys": join_key_grads,
        "grad_qkv": grad_qkv_tiles,
        "norm_grad": norm_grad,
        "stats_join": stats_join,
        "input_grad": input_grad,
        "vec_start": vec_start,
        "vec_rest": vec_rest,
    }
    for j in range(hidden_tiles):
        tasks["wout%d" % j] = functools.partial(grad_out_tile, j)
        tasks["win%d" % j] = functools.partial(grad_in_tile, j)
    for i in range(blocks):
        tasks["attend%d" % i] = functools.partial(attend, i)
    for which in (0, 1):
        tasks["near%d" % which] = functools.partial(split_near, which)
        tasks["far%d" % which] = functools.partial(split_far, which)
        tasks["own%d" % which] = functools.partial(split_own, which)
        tasks["vec%d" % which] = functools.partial(vec_step, which)
    r["vec"][0] = jnp.zeros(r["vec"].shape[1:], F32)
    for who, what in STEPS:
        if who < 0:
            tasks[what]()
        else:
            getattr(units[who], what)()

    for unit in units:
        unit.finish()
    for which in (0, 1):
        for b in range(blocks):
            for kind in range(3):
                gather(which, b, kind).wait_send()
        for slot in range(3):
            split(which, slot).wait_send()
        stats_copy(which).wait_send()
    for level in range(levels):
        vec_copy(level).wait_send()
    for b in range(blocks):

        @pl.when(goes_on(s, b))
        def _():
            for which in range(3):
                forward(b, which).wait_send()

        @pl.when(goes_on(s - 1, b) & (s > 0))
        def _():
            for which in range(2):
                backward(b, which).wait_send()


def rotary_tables():
    places = np.arange(PACK, dtype=np.float32)
    inverse = (10000.0 ** (-(np.arange(16, dtype=np.float32) * 2.0) / 32.0)).astype(np.float32)
    phase = (places[:, None] * inverse[None, :]).astype(np.float32)
    cosine, sine = np.cos(phase), np.sin(phase)
    cos_head = np.ones((PACK, 64), np.float32)
    sin_head = np.zeros((PACK, 64), np.float32)
    cos_head[:, 0:32] = np.repeat(cosine, 2, 1)
    sin_head[:, 0:32:2] = -sine
    sin_head[:, 1:32:2] = sine
    shape = (PACK // BLOCK, BLOCK, 128)
    return (
        np.concatenate([cos_head] * 2, 1).reshape(shape),
        np.concatenate([sin_head] * 2, 1).reshape(shape),
    )


def shards(
    x_in, ln_gain, ln_bias, w_qkv, w_o, w_in, b_in, w_out, b_out, grad_out, segment_ids, pad_mask
):
    count = lax.axis_size("seq")
    rows, own_width = x_in.shape
    width = w_in.shape[0]
    hidden = w_in.shape[1]
    blocks = rows // BLOCK
    assert own_width == BLOCK and rows % BLOCK == 0 and w_qkv.shape[2] == BLOCK
    assert hidden == width == 4 * BLOCK and lax.axis_size("tp") == 4 and rows < PACK
    assert count & (count - 1) == 0 and (count * rows) % PACK == 0
    tags = jnp.where(pad_mask == 1, segment_ids, -1)
    tags = jnp.broadcast_to(tags.reshape(blocks, 1, BLOCK), (blocks, 8, BLOCK))
    cos_table, sin_table = rotary_tables()
    levels = count.bit_length() - 1
    pairs = sum(kind is PairFirst for kind in KINDS[:9])
    tall_pairs = sum(kind is PairFirst for kind in KINDS[9:])
    hbm = pl.BlockSpec(memory_space=pl.ANY)
    vmem = pl.BlockSpec(memory_space=pltpu.VMEM)
    vm = pltpu.VMEM
    dma = pltpu.SemaphoreType.DMA
    ins = {
        "x_in": (x_in, hbm),
        "g_in": (grad_out, hbm),
        "gain": (ln_gain.reshape(1, -1), vmem),
        "bias": (ln_bias.reshape(1, -1), vmem),
        "b_in": (b_in.reshape(1, -1), vmem),
        "wqkv_in": (w_qkv, hbm),
        "wo_in": (w_o, hbm),
        "win_in": (w_in, hbm),
        "wout_in": (w_out, hbm),
        "seg": (segment_ids.reshape(-1, 1), vmem),
        "tags": (tags, vmem),
        "cos_in": (jnp.asarray(cos_table), hbm),
        "sin_in": (jnp.asarray(sin_table), hbm),
    }
    outs = {
        "wout_out": (w_out.shape, BF, hbm),
        "win_out": (w_in.shape, BF, hbm),
        "wo_out": (w_o.shape, BF, hbm),
        "qkv_out": (w_qkv.shape, BF, hbm),
        "vec_out": ((8, width), F32, vmem),
        "summed": ((rows, BLOCK), F32, vmem),
        "pulled": ((rows, BLOCK), F32, vmem),
    }
    scratch = {
        "x_all": vm((rows, width), BF),
        "g_all": vm((rows, width), BF),
        "ln": vm((rows, width), BF),
        "wqkv": vm(w_qkv.shape, BF),
        "wo": vm(w_o.shape, BF),
        "win": vm(w_in.shape, BF),
        "wout": vm(w_out.shape, BF),
        "act": vm((rows, hidden), BF),
        "dg": vm((rows, hidden), F32),
        "gh": vm((rows, hidden), BF),
        "q": vm((rows, BLOCK), BF),
        "kb": vm((2 * rows, BLOCK), BF),
        "vb": vm((2 * rows, BLOCK), BF),
        "kt": vm((2 * blocks, 8, BLOCK), jnp.int32),
        "gc": vm((rows, BLOCK), F32),
        "dk": vm((2 * rows, BLOCK), F32),
        "dv": vm((2 * rows, BLOCK), F32),
        "ctx": vm((rows, BLOCK), BF),
        "g3": vm((rows, 3 * BLOCK), BF),
        "mask": vm((BLOCK, PACK), F32),
        "ds": vm((4 * BLOCK, PACK), BF),
        "wl": vm((4 * BLOCK, PACK), BF),
        "qm": vm((4 * BLOCK, BLOCK), BF),
        "gm": vm((4 * BLOCK, BLOCK), BF),
        "dks": vm((2, rows, BLOCK), BF),
        "dkr": vm((2, rows, BLOCK), BF),
        "tp_out": vm((2, 3, rows, BLOCK), BF),
        "tp_got": vm((2, 3, rows, BLOCK), BF),
        "tp_sum": vm((2, rows, BLOCK), F32),
        "normed": vm((rows, BLOCK), F32),
        "inv": vm((rows, 128), F32),
        "cos": vm((blocks, BLOCK, 128), F32),
        "sin": vm((blocks, BLOCK, 128), F32),
        "stats": vm((2, 8, rows), F32),
        "stats_got": vm((2, 8, rows), F32),
        "vec": vm((levels + 1, 8, width), F32),
        "vec_got": vm((levels, 8, width), F32),
        "wide": vm((9 * 256, 1024), BF),
        "tall": vm((3, 1024, 256), BF),
        "pair_wide_x": vm((max(pairs, 1), 128, 1024), BF),
        "line_wide_x": vm((max(pairs, 1), 2, 64, 1024), BF),
        "pair_wide_z": vm((max(9 - pairs, 1), 64, 1024), BF),
        "line_wide_z": vm((max(9 - pairs, 1), 2, 128, 1024), BF),
        "pair_tall_x": vm((max(tall_pairs, 1), 512, 256), BF),
        "line_tall_x": vm((max(tall_pairs, 1), 2, 256, 256), BF),
        "pair_tall_z": vm((max(3 - tall_pairs, 1), 256, 256), BF),
        "line_tall_z": vm((max(3 - tall_pairs, 1), 2, 512, 256), BF),
        "load_sem": dma((6 + 2 * blocks,)),
        "ag_send": dma((2, blocks, 3)),
        "ag_recv": dma((2, blocks, 3)),
        "kv_send": dma((blocks, 3)),
        "kv_recv": dma((blocks, 3)),
        "dk_send": dma((blocks, 2)),
        "dk_recv": dma((blocks, 2)),
        "tp_send": dma((2, 3)),
        "tp_recv": dma((2, 3)),
        "st_send": dma((2,)),
        "st_recv": dma((2,)),
        "v_send": dma((levels,)),
        "v_recv": dma((levels,)),
        "w_send": dma((12, 8)),
        "w_recv": dma((12, 8)),
        "w_own": dma((12,)),
    }
    names = list(ins) + list(outs) + list(scratch)
    wout, win, wo, qkv, vec, summed, pulled = pl.pallas_call(
        functools.partial(layer_kernel, count, rows, names),
        out_shape=[jax.ShapeDtypeStruct(o[0], o[1]) for o in outs.values()],
        in_specs=[i[1] for i in ins.values()],
        out_specs=[o[2] for o in outs.values()],
        scratch_shapes=list(scratch.values()),
        compiler_params=pltpu.CompilerParams(
            collective_id=0, has_side_effects=True, vmem_limit_bytes=62 * 2**20
        ),
    )(*[i[0] for i in ins.values()])
    mixed = (x_in.astype(F32) + summed + b_out).astype(BF)
    grad_input = pulled + grad_out.astype(F32)
    return (
        mixed,
        grad_input,
        vec[1, 0:256],
        vec[1, 256:512],
        qkv.astype(F32),
        wo.astype(F32),
        win.astype(F32),
        vec[0],
        wout.astype(F32),
        vec[1, 512:768],
    )


def solution(mesh):
    return jax.shard_map(
        shards,
        mesh=mesh,
        in_specs=(
            P("seq", "tp"),
            P(),
            P(),
            P(None, None, "tp"),
            P("tp", None),
            P(None, "tp"),
            P("tp"),
            P("tp", None),
            P("tp"),
            P("seq", "tp"),
            P("seq"),
            P("seq"),
        ),
        out_specs=(
            P("seq", "tp"),
            P("seq", "tp"),
            P("tp"),
            P("tp"),
            P(None, None, "tp"),
            P("tp", None),
            P(None, "tp"),
            P("tp"),
            P("tp", None),
            P("tp"),
        ),
        check_vma=False,
    )
```

```python
import functools
from types import SimpleNamespace

import jax
import jax.numpy as jnp
import numpy as np
from jax import lax
from jax.experimental import pallas as pl
from jax.experimental.pallas import tpu as pltpu
from jax.sharding import PartitionSpec as P

PACK = 1024
LOG2E = 1.4426950408889634
EPSILON = 1e-05
BLOCK = 256
MESH = pl.DeviceIdType.MESH
BF = jnp.bfloat16
F32 = jnp.float32


class Ring:
    def __init__(self, seq_count):
        self.count = seq_count
        self.m = seq_count // 2
        self.s = lax.axis_index("seq")
        self.t = lax.axis_index("tp")
        self.z = self.s // 2
        self.x = self.s % 2
        low = (self.z < self.m // 2).astype(jnp.int32)
        self.near = low
        self.far = 1 - low

    def at(self, z, x):
        return (z * 2 + x, self.t)

    def peer(self):
        return self.at(self.z, 1 - self.x)

    def step(self, piece, sign):
        return self.at(self.z + sign * (2 * piece - 1), self.x)


def aligned(value):
    return pl.multiple_of(value, 16)


def add_rows(acc, acc_first, got, rows):
    step = 16 if rows % 32 else 32

    def body(i, carry):
        at = pl.ds(aligned(acc_first + i * step), step)
        here = pl.ds(aligned(i * step), step)
        acc[at, :] = (acc[at, :].astype(jnp.float32) + got[here, :].astype(jnp.float32)).astype(
            acc.dtype
        )
        return carry

    lax.fori_loop(0, rows // step, body, 0)


class Unit:
    def __init__(self, ring, index, part, out, out_first, rows, pair_buf, line_buf, send, recv, own):
        self.r, self.u = ring, index
        self.part, self.out, self.out_first, self.rows = part, out, out_first, rows
        self.pair_buf, self.line_buf = pair_buf, line_buf
        self.send, self.recv, self.own = send, recv, own

    def copy(self, src, dst, kind, to):
        return pltpu.make_async_remote_copy(
            src_ref=src,
            dst_ref=dst,
            send_sem=self.send.at[self.u, kind],
            recv_sem=self.recv.at[self.u, kind],
            device_id=to,
            device_id_type=MESH,
        )

    def p(self, first, rows):
        return self.part.at[pl.ds(aligned(first), rows)]

    def o(self, first, rows):
        return self.out.at[pl.ds(aligned(self.out_first + first), rows)]

    def keep(self, first, rows):
        return pltpu.make_async_copy(self.p(first, rows), self.o(first, rows), self.own.at[self.u])


class PairFirst(Unit):
    def pair(self):
        half = self.rows // 2
        return self.copy(self.p((1 - self.r.x) * half, half), self.pair_buf, 0, self.r.peer())

    def first_row(self, piece, member):
        return member * (self.rows // 2) + piece * (self.rows // 4)

    def line(self, piece):
        return self.copy(
            self.p(self.first_row(piece, self.r.x), self.rows // 4),
            self.line_buf.at[piece],
            1 + piece,
            self.r.step(piece, 1),
        )

    def result(self, piece, origin):
        at = self.p if origin else self.o
        return at(self.first_row(piece, self.r.x), self.rows // 4)

    def back(self, piece, origin):
        dst = self.result(piece, False)
        return self.copy(self.result(piece, origin), dst, 3 + piece, self.r.step(piece, -1))

    def over(self, piece, origin):
        dst = self.result(piece, False)
        return self.copy(self.result(piece, origin), dst, 5 + piece, self.r.peer())

    def add(self, piece):
        self.line(piece).wait_recv()
        row = self.first_row(piece, self.r.x)
        add_rows(self.part, row, self.line_buf.at[piece], self.rows // 4)

    def start(self):
        self.pair().start()

    def paired(self):
        half = self.rows // 2
        self.pair().wait_recv()
        add_rows(self.part, self.r.x * half, self.pair_buf, half)
        if self.end:
            self.line(self.r.near).start()

    def chain_near(self):
        if not self.end:
            self.add(self.r.near)
            self.line(self.r.near).start()

    def chain_far(self):
        piece = self.r.far
        self.add(piece)
        if self.end:
            self.back(piece, True).start()
            self.over(piece, True).start()
            self.keep(self.first_row(piece, self.r.x), self.rows // 4).start()
        else:
            self.line(piece).start()

    def back_near(self):
        piece = self.r.far
        if not self.end:
            self.back(piece, False).wait_recv()
            self.back(piece, False).start()
            self.over(piece, False).start()

    def back_far(self):
        piece = self.r.near
        self.back(piece, False).wait_recv()
        if not self.end:
            self.back(piece, False).start()
        self.over(piece, False).start()

    def finish(self):
        quarter = self.rows // 4
        for piece in (0, 1):
            row = self.first_row(piece, 1 - self.r.x)
            self.copy(self.o(row, quarter), self.o(row, quarter), 5 + piece, self.r.peer()).wait_recv()
            self.over(piece, False).wait_send()
        self.pair().wait_send()
        self.line(self.r.near).wait_send()
        self.back(self.r.far, False).wait_send()
        if self.end:
            self.keep(self.first_row(self.r.far, self.r.x), quarter).wait()
        else:
            self.line(self.r.far).wait_send()
            self.back(self.r.near, False).wait_send()


class LineFirst(Unit):
    def line(self, piece):
        half = self.rows // 2
        return self.copy(
            self.p(piece * half, half), self.line_buf.at[piece], 1 + piece, self.r.step(piece, 1)
        )

    def row_of(self, piece, member):
        return piece * (self.rows // 2) + member * (self.rows // 4)

    def pair(self, piece):
        quarter = self.rows // 4
        return self.copy(
            self.p(self.row_of(piece, 1 - self.r.x), quarter), self.pair_buf, 0, self.r.peer()
        )

    def result(self, piece, member, origin):
        at = self.p if origin else self.o
        return at(self.row_of(piece, member), self.rows // 4)

    def over(self, piece, member, origin):
        dst = self.result(piece, member, False)
        return self.copy(self.result(piece, member, origin), dst, 3, self.r.peer())

    def back(self, piece, member, origin):
        dst = self.result(piece, member, False)
        to = self.r.step(piece, -1)
        return self.copy(self.result(piece, member, origin), dst, 4 + 2 * piece + member, to)

    def add(self, piece):
        half = self.rows // 2
        self.line(piece).wait_recv()
        add_rows(self.part, piece * half, self.line_buf.at[piece], half)

    def start(self):
        if self.end:
            self.line(self.r.near).start()

    def chain_near(self):
        if not self.end:
            self.add(self.r.near)
            self.line(self.r.near).start()

    def chain_far(self):
        piece = self.r.far
        self.add(piece)
        if self.end:
            self.pair(piece).start()
        else:
            self.line(piece).start()

    def exchanged(self):
        piece = self.r.far
        quarter = self.rows // 4
        if self.end:
            self.pair(piece).wait_recv()
            row = self.row_of(piece, self.r.x)
            add_rows(self.part, row, self.pair_buf, quarter)
            self.over(piece, self.r.x, True).start()
            self.back(piece, self.r.x, True).start()
            self.keep(row, quarter).start()

    def back_near(self):
        piece = self.r.far
        other = 1 - self.r.x
        if self.end:
            self.over(piece, other, False).wait_recv()
            self.back(piece, other, False).start()
        else:
            for member in (self.r.x, other):
                self.back(piece, member, False).wait_recv()
                self.back(piece, member, False).start()

    def back_far(self):
        piece = self.r.near
        for member in (self.r.x, 1 - self.r.x):
            self.back(piece, member, False).wait_recv()
            if not self.end:
                self.back(piece, member, False).start()

    def finish(self):
        self.line(self.r.near).wait_send()
        for member in (0, 1):
            self.back(self.r.far, member, False).wait_send()
        if self.end:
            piece = self.r.far
            self.pair(piece).wait_send()
            self.over(piece, self.r.x, False).wait_send()
            self.keep(self.row_of(piece, self.r.x), self.rows // 4).wait()
        else:
            self.line(self.r.far).wait_send()
            for member in (0, 1):
                self.back(self.r.near, member, False).wait_send()


ROLES = ("start", "paired", "chain_near", "chain_far", "exchanged", "back_near", "back_far", "finish")


UNITS = (
    (PairFirst, -1, 0, 128),
    (LineFirst, -1, 128, 128),
    (LineFirst, -1, 256, 128),
    (PairFirst, -1, 384, 128),
    (PairFirst, -1, 512, 128),
    (LineFirst, -1, 640, 128),
    (PairFirst, -1, 768, 128),
    (LineFirst, -1, 896, 128),
    (PairFirst, -1, 1024, 128),
    (PairFirst, -1, 1152, 128),
    (LineFirst, -1, 1280, 128),
    (LineFirst, -1, 1408, 128),
    (PairFirst, -1, 1536, 128),
    (PairFirst, -1, 1664, 128),
    (PairFirst, -1, 1792, 128),
    (LineFirst, -1, 1920, 128),
    (LineFirst, -1, 2048, 128),
    (LineFirst, -1, 2176, 128),
    (PairFirst, 0, 0, 512),
    (LineFirst, 0, 512, 512),
    (PairFirst, 1, 0, 512),
    (LineFirst, 1, 512, 512),
    (LineFirst, 2, 0, 512),
    (PairFirst, 2, 512, 512),
)

STEPS = (
    (3, ((7, 0), (6, 0)), ()),
    (0, ((1, 0),), ((0, 0),)),
    (1, ((2, 0), (0, 0)), ((6, 0),)),
    (2, (), ()),
    (4, ((9, 0), (8, 0)), ((7, 2),)),
    (25, ((3, 0),), ()),
    (6, (), ()),
    (7, ((5, 0), (15, 0)), ()),
    (24, (), ((1, 2), (8, 0))),
    (8, ((6, 1),), ((2, 2),)),
    (5, ((11, 0), (14, 0), (9, 1)), ((9, 0), (7, 3), (0, 1), (3, 0), (12, 0), (13, 0), (6, 1), (1, 3), (5, 2))),
    (9, ((8, 1), (4, 0)), ((2, 3), (15, 2))),
    (10, ((0, 1), (10, 0), (7, 3), (12, 0), (13, 0)), ((5, 3), (9, 1), (6, 2), (11, 2))),
    (11, ((3, 1), (7, 4)), ((15, 3), (9, 2), (8, 1), (12, 1), (8, 2), (4, 0), (6, 3))),
    (12, ((1, 3), (5, 3), (12, 1), (4, 1), (14, 1)), ((11, 3), (0, 2), (14, 0), (10, 2), (9, 3))),
    (13, (), ((0, 3), (12, 2), (3, 1), (8, 3), (4, 1))),
    (26, ((7, 5),), ((4, 2),)),
    (27, ((13, 1), (9, 3), (16, 0)), ((14, 1), (10, 3), (3, 2), (14, 2), (7, 5), (12, 3), (4, 3), (9, 5), (13, 1), (3, 3), (13, 2), (14, 3))),
    (14, ((0, 3), (17, 0), (6, 3), (8, 3), (1, 4)), ((16, 2), (7, 6), (13, 3), (17, 2), (0, 5), (9, 6), (6, 5))),
    (29, (), ((16, 3),)),
    (18, (), ()),
    (23, ((19, 0), (18, 0), (21, 0), (1, 5), (23, 0), (20, 0), (22, 0), (17, 3), (3, 3)), ((17, 3), (18, 0), (8, 5), (19, 2), (0, 6))),
    (21, ((14, 3), (23, 1), (18, 1), (13, 3), (17, 4), (5, 4)), ((23, 0), (20, 0), (8, 6), (21, 2), (1, 5), (6, 6), (19, 3))),
    (19, ((15, 3), (20, 1), (16, 3), (10, 3), (17, 5), (4, 3), (5, 5), (15, 4), (10, 4), (12, 3)), ((21, 3), (22, 2), (14, 5), (23, 1), (18, 1), (1, 6), (18, 2))),
    (16, ((2, 3), (11, 3), (15, 5)), ((3, 5), (22, 3), (23, 2))),
    (20, ((22, 3), (16, 4), (20, 3), (10, 5), (11, 4), (21, 3), (18, 3), (23, 3), (22, 4), (16, 5)), ((13, 5), (14, 6), (18, 3), (20, 1), (3, 6), (20, 2), (23, 3), (17, 5))),
    (15, (), ((4, 5), (5, 5), (20, 3), (17, 6), (4, 6), (12, 5), (15, 5), (13, 6), (5, 6))),
    (30, ((21, 4), (11, 5), (2, 4)), ((20, 5), (12, 6))),
    (33, ((19, 3),), ((10, 5), (15, 6), (20, 6), (18, 5))),
    (17, ((14, 6), (22, 5), (0, 6), (9, 6)), ((23, 5), (10, 6), (16, 5), (18, 6))),
    (22, ((2, 5), (19, 4), (6, 6)), ()),
    (31, (), ((11, 5), (16, 6), (22, 5), (11, 6), (2, 5), (23, 6))),
    (28, ((8, 6), (21, 5), (13, 6), (4, 6), (19, 5), (3, 6), (15, 6)), ((22, 6),)),
    (34, ((20, 6), (23, 6)), ((21, 5), (2, 6), (19, 5), (21, 6))),
    (32, ((11, 6), (12, 6), (18, 6), (5, 6), (2, 6), (19, 6), (1, 6), (7, 6), (21, 6), (10, 6), (17, 6), (22, 6), (16, 6)), ((19, 6),)),
)


def greet(ring):
    barrier = pltpu.get_barrier_semaphore()
    s, t, count = ring.s, ring.t, ring.count

    def signal(to):
        pl.semaphore_signal(barrier, inc=1, device_id=to, device_id_type=MESH)

    signal((s, mate(t, 1)))
    signal((s, mate(t, 2)))
    total = jnp.int32(2)
    bit = 1
    while bit < count:
        signal((mate(s, bit), t))
        total = total + 1
        bit *= 2
    for hop in (-2, -1, 1, 2):
        ok = (s + hop >= 0) & (s + hop < count)

        @pl.when(ok)
        def _():
            signal((s + hop, t))

        total = total + ok.astype(jnp.int32)
    pl.semaphore_wait(barrier, total)


def mate(place, bit):
    return place + bit - 2 * bit * ((place // bit) % 2)


def dot(a, b):
    return jnp.dot(a, b, preferred_element_type=F32)


def dot_rows(a, b):
    return lax.dot_general(a, b, (((0,), (0,)), ((), ())), preferred_element_type=F32)


def dot_columns(a, b):
    return lax.dot_general(a, b, (((1,), (1,)), ((), ())), preferred_element_type=F32)


def layer_kernel(
    count, rows, names, *refs
):
    r = SimpleNamespace(**dict(zip(names, refs)))
    ring = Ring(count)
    s, t = ring.s, ring.t
    blocks = rows // BLOCK
    per_pack = PACK // BLOCK
    x_all, g_all, ln = r.x_all, r.g_all, r.ln
    wqkv, wo, win, wout = r.wqkv, r.wo, r.win, r.wout
    width, hidden = win.shape
    hidden_tiles = hidden // BLOCK
    width_tiles = width // BLOCK

    def blk(b):
        return pl.ds(b * BLOCK, BLOCK) if isinstance(b, int) else pl.ds(pl.multiple_of(b * BLOCK, BLOCK), BLOCK)

    loads = {}

    def load(name, src, dst):
        copy = pltpu.make_async_copy(src, dst, r.load_sem.at[len(loads)])
        loads[name] = copy
        copy.start()

    load("x", r.x_in, x_all.at[:, blk(t)])
    load("wqkv", r.wqkv_in, wqkv)
    load("win", r.win_in, win)
    load("g", r.g_in, g_all.at[:, blk(t)])
    load("wout", r.wout_in, wout)
    load("wo", r.wo_in, wo)
    for b in range(blocks):
        place = (blocks * s + b) % per_pack
        load(("cos", b), r.cos_in.at[place], r.cos.at[b])
        load(("sin", b), r.sin_in.at[place], r.sin.at[b])
    greet(ring)

    def gather(which, b, kind):
        src_ref, whole = ((r.x_in, x_all), (r.g_in, g_all))[which]
        to = mate(t, 2) if kind == 1 else mate(t, 1)
        shard = mate(t, 2) if kind == 2 else t
        dst = whole.at[blk(b), blk(shard)]
        src = dst if kind == 2 else src_ref.at[blk(b)]
        return pltpu.make_async_remote_copy(
            src_ref=src,
            dst_ref=dst,
            send_sem=r.ag_send.at[which, b, kind],
            recv_sem=r.ag_recv.at[which, b, kind],
            device_id=(s, to),
            device_id_type=MESH,
        )

    for which in (0, 1):
        for b in range(blocks):
            gather(which, b, 1).start()
            gather(which, b, 0).start()
    r.dk[...] = jnp.zeros(r.dk.shape, F32)
    r.dv[...] = jnp.zeros(r.dv.shape, F32)

    def relay(which, b):
        gather(which, b, 1).wait_recv()
        gather(which, b, 2).start()

    def arrived(which, b):
        gather(which, b, 0).wait_recv()
        gather(which, b, 2).wait_recv()

    lane = lax.broadcasted_iota(jnp.int32, (BLOCK, BLOCK), 1)
    gain_own = r.gain[:, blk(t)]

    def norm(b):
        xb = x_all[blk(b), :].astype(F32)
        mean = jnp.mean(xb, -1, keepdims=True)
        center = xb - mean
        inverse = lax.rsqrt(jnp.mean(center * center, -1, keepdims=True) + EPSILON)
        ln[blk(b), :] = (center * inverse * r.gain[...] + r.bias[...]).astype(BF)
        own = x_all[blk(b), blk(t)].astype(F32)
        r.normed[blk(b), :] = (own - mean) * inverse
        r.inv[blk(b), :] = jnp.broadcast_to(inverse, (BLOCK, 128))

    def turn(v, b, sense):
        cosine = jnp.concatenate([r.cos[b]] * 2, 1)
        sine = jnp.concatenate([r.sin[b]] * 2, 1)
        swapped = jnp.where(lane % 2 == 0, pltpu.roll(v, BLOCK - 1, 1), pltpu.roll(v, 1, 1))
        return v * cosine + sense * sine * swapped

    def goes_on(place, b):
        return ((blocks * place + b) // per_pack == (blocks * (place + 1)) // per_pack) & (
            place < count - 1
        )

    def forward(b, which):
        here, there = blk(blocks + b), blk(b)
        if which == 2:
            src, dst = r.kt.at[blocks + b], r.kt.at[b]
        else:
            ref = (r.kb, r.vb)[which]
            src, dst = ref.at[here], ref.at[there]
        return pltpu.make_async_remote_copy(
            src_ref=src,
            dst_ref=dst,
            send_sem=r.kv_send.at[b, which],
            recv_sem=r.kv_recv.at[b, which],
            device_id=(s + 1, t),
            device_id_type=MESH,
        )

    def row_of(ref, b):
        return ref[blk(b)].reshape(1, BLOCK)

    def project(b):
        lnb = ln[blk(b), :]
        tags = jnp.where(row_of(r.pad, b) == 1, row_of(r.seg, b), -1)
        r.kt[blocks + b] = jnp.broadcast_to(tags, (8, BLOCK))
        r.kb[blk(blocks + b), :] = turn(dot(lnb, wqkv[1]), b, 1.0).astype(BF)
        r.vb[blk(blocks + b), :] = dot(lnb, wqkv[2]).astype(BF)

        @pl.when(goes_on(s, b))
        def _():
            for which in range(3):
                forward(b, which).start()

        r.q[blk(b), :] = turn(dot(lnb, wqkv[0]), b, 1.0).astype(BF)

    for b in range(blocks):
        relay(0, b)
    loads["x"].wait()
    for b in range(blocks):
        arrived(0, b)
        norm(b)
        if b == 0:
            loads["wqkv"].wait()
            for b2 in range(blocks):
                loads[("cos", b2)].wait()
                loads[("sin", b2)].wait()
        project(b)

    loads["win"].wait()

    def expand(j):
        for b in range(blocks):
            pre = dot(ln[blk(b), :], win[:, blk(j)]) + r.b_in[:, blk(j)]
            scale = 0.7978845608028654
            square = pre * pre
            th = jnp.tanh(scale * (pre + 0.044715 * (square * pre)))
            half = 0.5 * (1.0 + th)
            r.act[blk(b), blk(j)] = (pre * half).astype(BF)
            r.dg[blk(b), blk(j)] = half + (0.5 * scale) * pre * (1.0 - th * th) * (
                1.0 + (3 * 0.044715) * square
            )

    for j in range(hidden_tiles):
        expand(j)
        if j < blocks:
            relay(1, j)
    loads["g"].wait()
    loads["wout"].wait()
    loads["wo"].wait()
    for b in range(blocks):
        arrived(1, b)

    units = []
    slots = {}
    for u, (kind, slab, first, size) in enumerate(UNITS):
        if slab < 0:
            out, base = (
                (r.wout_out, 0)
                if first < hidden
                else (r.win_out, hidden)
                if first < hidden + width
                else (r.wo_out, hidden + width)
            )
            part, out_first = r.wide.at[pl.ds(first, size)], first - base
        else:
            part, out, out_first = r.tall.at[slab, pl.ds(first, size)], r.qkv_out.at[slab], first
        key = group(kind, slab, size)
        slot = slots.get(key, 0)
        slots[key] = slot + 1
        units.append(
            kind(
                ring,
                u,
                part,
                out,
                out_first,
                size,
                getattr(r, "pair" + key).at[slot],
                getattr(r, "line" + key).at[slot],
                r.w_send,
                r.w_recv,
                r.w_own,
            )
        )

    def grad_out_tile(j):
        bin_sum = jnp.zeros((1, BLOCK), F32)
        for b in range(blocks):
            pulled = dot_columns(g_all[blk(b), :], wout[blk(j), :])
            gh = (pulled * r.dg[blk(b), blk(j)]).astype(BF)
            r.gh[blk(b), blk(j)] = gh
            bin_sum = bin_sum + jnp.sum(gh.astype(F32), 0, keepdims=True)
        r.vec[0, 0:1, blk(j)] = bin_sum
        r.wide[blk(j), :] = dot_rows(r.act[:, blk(j)], g_all[...]).astype(BF)

    def grad_in_tile(j):
        r.wide[blk(hidden_tiles + j), :] = dot_rows(ln[:, blk(j)], r.gh[...]).astype(BF)

    def context_pull():
        for b in range(blocks):
            r.gc[blk(b), :] = dot_columns(g_all[blk(b), :], wo[...])
        own = g_all[:, blk(t)].astype(F32)
        r.vec[0, 1:2, blk(2)] = jnp.sum(own, 0, keepdims=True)

    def receive_keys():
        for b in range(blocks):

            @pl.when(goes_on(s - 1, b) & (s > 0))
            def _():
                for which in range(3):
                    forward(b, which).wait_recv()

    def attend(i, part):
        held = (blocks * s + i) % per_pack + 1
        for nb in range(1, per_pack + 1):
            if blocks + i - nb + 1 >= 0:

                @pl.when(held == nb)
                def _():
                    attend_window(i, nb, part)

    def attend_window(i, nb, part):
        n = nb * BLOCK
        first = blocks + i - nb + 1
        window = pl.ds(first * BLOCK, n)
        if part == 0:
            row = lax.broadcasted_iota(jnp.int32, (BLOCK, BLOCK), 0)
            wide_row = jnp.broadcast_to(row_of(r.seg, i), (128, BLOCK))
            seg = wide_row.T[:, 0:1]
            for c in range(nb):
                same = r.kt[first + c, 0:1, :] == seg
                if c == nb - 1:
                    same = (same & (lane <= row)) | (lane == row)
                r.mask[:, blk(c)] = jnp.where(same, 0.0, -1e30)
        qb = r.q[blk(i), :]
        gcb = r.gc[blk(i), :]
        kw = r.kb[window, :]
        vw = r.vb[window, :]

        def head(h, carry):
            mine = lane // 64 == h
            at = pl.ds(pl.multiple_of(h * BLOCK, BLOCK), BLOCK)
            qm = jnp.where(mine, qb, jnp.zeros_like(qb))
            r.qm[at, :] = qm
            logit = dot_columns(qm, kw) * (0.125 * LOG2E) + r.mask[:, :n]
            ceiling = jnp.floor(jnp.max(logit, -1, keepdims=True))
            weight = jnp.exp2(logit - ceiling)
            total = 1.0 / jnp.sum(weight, -1, keepdims=True)
            low = weight.astype(BF)
            r.wl[at, :n] = low
            context = dot(low, vw) * total
            gm = jnp.where(mine, gcb, 0.0)
            ga = (gm * total).astype(BF)
            r.gm[at, :] = ga
            offset = jnp.sum(gm * context, -1, keepdims=True) * total
            ds = (weight * (dot_columns(ga, vw) - offset)).astype(BF)
            r.ds[at, :n] = ds
            dq = dot(ds, kw)
            ctx, dqs = carry
            return (jnp.where(mine, context, ctx), jnp.where(mine, dq, dqs))

        zero = jnp.zeros((BLOCK, BLOCK), F32)
        start = (zero, zero) if part == 0 else (r.both[0], r.both[1])
        ctx, dqs = lax.fori_loop(2 * part, 2 * part + 2, head, start)
        if part == 0:
            r.both[0] = ctx
            r.both[1] = dqs
            return
        r.ctx[blk(i), :] = ctx.astype(BF)
        r.g3[blk(i), 0:BLOCK] = turn(0.125 * dqs, i, -1.0).astype(BF)
        for c in range(nb):
            r.dk[blk(first + c), :] += dot_rows(r.ds[:, blk(c)], r.qm[...])
            r.dv[blk(first + c), :] += dot_rows(r.wl[:, blk(c)], r.gm[...])

    def backward(b, which):
        return pltpu.make_async_remote_copy(
            src_ref=r.dks.at[which, blk(b)],
            dst_ref=r.dkr.at[which, blk(b)],
            send_sem=r.dk_send.at[b, which],
            recv_sem=r.dk_recv.at[b, which],
            device_id=(s - 1, t),
            device_id_type=MESH,
        )

    def send_key_grads():
        for b in range(blocks):

            @pl.when(goes_on(s - 1, b) & (s > 0))
            def _():
                for which, ref in enumerate((r.dk, r.dv)):
                    r.dks[which, blk(b), :] = ref[blk(b), :].astype(BF)
                    backward(b, which).start()

    def grad_wo_tile():
        r.wide[blk(2 * hidden_tiles), :] = dot_rows(r.ctx[...], g_all[...]).astype(BF)

    def split(which, slot):
        to = mate(t, 2) if slot == 2 else mate(t, 1)
        return pltpu.make_async_remote_copy(
            src_ref=r.tp_out.at[which, slot],
            dst_ref=r.tp_got.at[which, slot],
            send_sem=r.tp_send.at[which, slot],
            recv_sem=r.tp_recv.at[which, slot],
            device_id=(s, to),
            device_id_type=MESH,
        )

    def share(which, owner, b):
        if which == 0:
            return dot(r.ctx[blk(b), :], wo[:, blk(owner)]) + dot(
                r.act[blk(b), :], wout[:, blk(owner)]
            )
        total = dot_columns(r.gh[blk(b), :], win[blk(owner), :])
        for k in range(3):
            total = total + dot_columns(r.g3[blk(b), blk(k)], wqkv[k, blk(owner), :])
        return total

    far_mate = mate(mate(t, 1), 2)

    def split_near(which):
        for slot, owner in ((1, far_mate), (0, mate(t, 1))):
            for b in range(blocks):
                r.tp_out[which, slot, blk(b), :] = share(which, owner, b).astype(BF)
            split(which, slot).start()

    def split_far(which):
        split(which, 1).wait_recv()
        for b in range(blocks):
            mine = share(which, mate(t, 2), b)
            r.tp_out[which, 2, blk(b), :] = (
                mine + r.tp_got[which, 1, blk(b), :].astype(F32)
            ).astype(BF)
        split(which, 2).start()

    def split_own(which):
        for b in range(blocks):
            r.tp_sum[which, blk(b), :] = share(which, t, b)

    def split_join(which):
        split(which, 0).wait_recv()
        split(which, 2).wait_recv()
        for b in range(blocks):
            r.tp_sum[which, blk(b), :] += r.tp_got[which, 0, blk(b), :].astype(F32) + r.tp_got[which, 2, blk(b), :].astype(F32)

    def join_branch():
        split_join(0)
        r.summed[...] = r.tp_sum[0]

    def join_key_grads():
        for b in range(blocks):
            for which, ref in enumerate((r.dk, r.dv)):

                @pl.when(goes_on(s, b))
                def _():
                    backward_in = pltpu.make_async_remote_copy(
                        src_ref=r.dks.at[which, blk(b)],
                        dst_ref=r.dkr.at[which, blk(b)],
                        send_sem=r.dk_send.at[b, which],
                        recv_sem=r.dk_recv.at[b, which],
                        device_id=(s + 1, t),
                        device_id_type=MESH,
                    )
                    backward_in.wait_recv()
                    ref[blk(blocks + b), :] += r.dkr[which, blk(b), :].astype(F32)

            r.g3[blk(b), blk(1)] = turn(0.125 * r.dk[blk(blocks + b), :], b, -1.0).astype(BF)
            r.g3[blk(b), blk(2)] = r.dv[blk(blocks + b), :].astype(BF)

    def grad_qkv_tiles(part):
        half = width_tiles // 2
        for j in range(part * half, part * half + half):
            tile = dot_rows(ln[:, blk(j)], r.g3[...]).astype(BF)
            for k in range(3):
                r.tall[k, blk(j), :] = tile[:, k * BLOCK : (k + 1) * BLOCK]

    def stats_copy(level):
        return pltpu.make_async_remote_copy(
            src_ref=r.stats.at[level],
            dst_ref=r.stats_got.at[level],
            send_sem=r.st_send.at[level],
            recv_sem=r.st_recv.at[level],
            device_id=(s, mate(t, 1 << level)),
            device_id_type=MESH,
        )

    def norm_grad():
        split_join(1)
        gain_sum = jnp.zeros((1, BLOCK), F32)
        bias_sum = jnp.zeros((1, BLOCK), F32)
        lane_one = lax.broadcasted_iota(jnp.int32, (BLOCK, 128), 1)
        for b in range(blocks):
            grad = r.tp_sum[1, blk(b), :]
            normed = r.normed[blk(b), :]
            gain_sum = gain_sum + jnp.sum(grad * normed, 0, keepdims=True)
            bias_sum = bias_sum + jnp.sum(grad, 0, keepdims=True)
            hat = grad * gain_own
            first = jnp.sum(hat, -1, keepdims=True)
            second = jnp.sum(hat * normed, -1, keepdims=True)
            both = jnp.where(lane_one == 0, first, second)
            r.stats[0, :, blk(b)] = both.T[0:8, :]
        r.vec[0, 1:2, blk(0)] = gain_sum
        r.vec[0, 1:2, blk(1)] = bias_sum
        stats_copy(0).start()

    def stats_join():
        stats_copy(0).wait_recv()
        r.stats[1] = r.stats[0] + r.stats_got[0]
        stats_copy(1).start()

    def input_grad():
        stats_copy(1).wait_recv()
        for b in range(blocks):
            both = (r.stats[1, :, blk(b)] + r.stats_got[1, :, blk(b)]) * (1.0 / ln.shape[1])
            columns = jnp.concatenate([both] * 16, 0).T
            hat = r.tp_sum[1, blk(b), :] * gain_own
            r.pulled[blk(b), :] = r.inv[blk(b), 0:1] * (
                hat - columns[:, 0:1] - r.normed[blk(b), :] * columns[:, 1:2]
            )

    levels = count.bit_length() - 1

    def vec_copy(level):
        return pltpu.make_async_remote_copy(
            src_ref=r.vec.at[level],
            dst_ref=r.vec_got.at[level],
            send_sem=r.v_send.at[level],
            recv_sem=r.v_recv.at[level],
            device_id=(mate(s, 1 << level), t),
            device_id_type=MESH,
        )

    def vec_start():
        vec_copy(0).start()

    def vec_step(level):
        vec_copy(level).wait_recv()
        r.vec[level + 1] = r.vec[level] + r.vec_got[level]
        if level + 1 < levels:
            vec_copy(level + 1).start()

    def vec_rest():
        for level in range(2, levels):
            vec_step(level)
        r.vec_out[...] = r.vec[levels]

    part = functools.partial
    tasks = [part(grad_out_tile, j) for j in range(hidden_tiles)]
    tasks += [part(grad_in_tile, j) for j in range(width_tiles)]
    tasks += [part(attend, i, half) for i in range(blocks) for half in (0, 1)]
    for which in (0, 1):
        tasks += [part(step, which) for step in (split_near, split_far, split_own, vec_step)]
        tasks.append(part(grad_qkv_tiles, which))
    tasks += [context_pull, receive_keys, send_key_grads, grad_wo_tile, join_branch, join_key_grads]
    tasks += [norm_grad, stats_join, input_grad, vec_start, vec_rest]
    r.vec[0] = jnp.zeros(r.vec.shape[1:], F32)
    at_end = (ring.z == 0) | (ring.z == ring.m - 1)

    def messages(events, end):
        for who, role in events:
            units[who].end = end
            getattr(units[who], ROLES[role])()

    for task, ends, middles in STEPS:
        tasks[task]()

        @pl.when(at_end)
        def _():
            messages(ends, True)

        @pl.when(jnp.logical_not(at_end))
        def _():
            messages(middles, False)

    closing = [(u, len(ROLES) - 1) for u in range(len(units))]

    @pl.when(at_end)
    def _():
        messages(closing, True)

    @pl.when(jnp.logical_not(at_end))
    def _():
        messages(closing, False)

    for which in (0, 1):
        for b in range(blocks):
            for kind in range(3):
                gather(which, b, kind).wait_send()
        for slot in range(3):
            split(which, slot).wait_send()
        stats_copy(which).wait_send()
    for level in range(levels):
        vec_copy(level).wait_send()
    for b in range(blocks):

        @pl.when(goes_on(s, b))
        def _():
            for which in range(3):
                forward(b, which).wait_send()

        @pl.when(goes_on(s - 1, b) & (s > 0))
        def _():
            for which in range(2):
                backward(b, which).wait_send()


def group(kind, slab, size):
    return "%d_%d_%d" % (kind is PairFirst, slab < 0, size)


FINISH_STEPS = 8


def rotary_tables():
    places = np.arange(PACK, dtype=np.float32)
    inverse = (10000.0 ** (-(np.arange(16, dtype=np.float32) * 2.0) / 32.0)).astype(np.float32)
    phase = (places[:, None] * inverse[None, :]).astype(np.float32)
    cosine, sine = np.cos(phase), np.sin(phase)
    cos_head = np.ones((PACK, 64), np.float32)
    sin_head = np.zeros((PACK, 64), np.float32)
    cos_head[:, 0:32] = np.repeat(cosine, 2, 1)
    sin_head[:, 0:32:2] = -sine
    sin_head[:, 1:32:2] = sine
    shape = (PACK // BLOCK, BLOCK, 128)
    return (
        np.concatenate([cos_head] * 2, 1).reshape(shape),
        np.concatenate([sin_head] * 2, 1).reshape(shape),
    )


def shards(
    x_in, ln_gain, ln_bias, w_qkv, w_o, w_in, b_in, w_out, b_out, grad_out, segment_ids, pad_mask
):
    count = lax.axis_size("seq")
    rows, own_width = x_in.shape
    width = w_in.shape[0]
    hidden = w_in.shape[1]
    blocks = rows // BLOCK
    assert own_width == BLOCK and rows % BLOCK == 0 and w_qkv.shape[2] == BLOCK
    assert hidden == width == 4 * BLOCK and lax.axis_size("tp") == 4 and rows < PACK
    assert count & (count - 1) == 0 and (count * rows) % PACK == 0
    cos_table, sin_table = rotary_tables()
    levels = count.bit_length() - 1
    groups = {}
    for kind, slab, first, size in UNITS:
        key = group(kind, slab, size)
        groups[key] = (kind, 1024 if slab < 0 else BLOCK, size, groups.get(key, (0, 0, 0, 0))[3] + 1)
    hbm = pl.BlockSpec(memory_space=pl.ANY)
    vmem = pl.BlockSpec(memory_space=pltpu.VMEM)
    vm = pltpu.VMEM
    dma = pltpu.SemaphoreType.DMA
    ins = dict(
        x_in=(x_in, hbm),
        g_in=(grad_out, hbm),
        gain=(ln_gain.reshape(1, -1), vmem),
        bias=(ln_bias.reshape(1, -1), vmem),
        b_in=(b_in.reshape(1, -1), vmem),
        wqkv_in=(w_qkv, hbm),
        wo_in=(w_o, hbm),
        win_in=(w_in, hbm),
        wout_in=(w_out, hbm),
        seg=(segment_ids, vmem),
        pad=(pad_mask, vmem),
        cos_in=(jnp.asarray(cos_table), hbm),
        sin_in=(jnp.asarray(sin_table), hbm),
    )
    outs = dict(
        wout_out=(w_out.shape, BF, hbm),
        win_out=(w_in.shape, BF, hbm),
        wo_out=(w_o.shape, BF, hbm),
        qkv_out=(w_qkv.shape, BF, hbm),
        vec_out=((8, width), F32, vmem),
        summed=((rows, BLOCK), F32, vmem),
        pulled=((rows, BLOCK), F32, vmem),
    )
    scratch = dict(
        x_all=vm((rows, width), BF),
        g_all=vm((rows, width), BF),
        ln=vm((rows, width), BF),
        wqkv=vm(w_qkv.shape, BF),
        wo=vm(w_o.shape, BF),
        win=vm(w_in.shape, BF),
        wout=vm(w_out.shape, BF),
        act=vm((rows, hidden), BF),
        dg=vm((rows, hidden), F32),
        gh=vm((rows, hidden), BF),
        q=vm((rows, BLOCK), BF),
        kb=vm((2 * rows, BLOCK), BF),
        vb=vm((2 * rows, BLOCK), BF),
        kt=vm((2 * blocks, 8, BLOCK), jnp.int32),
        gc=vm((rows, BLOCK), F32),
        dk=vm((2 * rows, BLOCK), F32),
        dv=vm((2 * rows, BLOCK), F32),
        ctx=vm((rows, BLOCK), BF),
        g3=vm((rows, 3 * BLOCK), BF),
        mask=vm((BLOCK, PACK), F32),
        ds=vm((4 * BLOCK, PACK), BF),
        wl=vm((4 * BLOCK, PACK), BF),
        qm=vm((4 * BLOCK, BLOCK), BF),
        gm=vm((4 * BLOCK, BLOCK), BF),
        dks=vm((2, rows, BLOCK), BF),
        dkr=vm((2, rows, BLOCK), BF),
        tp_out=vm((2, 3, rows, BLOCK), BF),
        tp_got=vm((2, 3, rows, BLOCK), BF),
        tp_sum=vm((2, rows, BLOCK), F32),
        normed=vm((rows, BLOCK), F32),
        inv=vm((rows, 128), F32),
        cos=vm((blocks, BLOCK, 128), F32),
        sin=vm((blocks, BLOCK, 128), F32),
        stats=vm((2, 8, rows), F32),
        stats_got=vm((2, 8, rows), F32),
        vec=vm((levels + 1, 8, width), F32),
        vec_got=vm((levels, 8, width), F32),
        wide=vm((9 * 256, 1024), BF),
        tall=vm((3, 1024, 256), BF),
        load_sem=dma((6 + 2 * blocks,)),
        ag_send=dma((2, blocks, 3)),
        ag_recv=dma((2, blocks, 3)),
        kv_send=dma((blocks, 3)),
        kv_recv=dma((blocks, 3)),
        dk_send=dma((blocks, 2)),
        dk_recv=dma((blocks, 2)),
        tp_send=dma((2, 3)),
        tp_recv=dma((2, 3)),
        st_send=dma((2,)),
        st_recv=dma((2,)),
        v_send=dma((levels,)),
        v_recv=dma((levels,)),
        w_send=dma((len(UNITS), 8)),
        w_recv=dma((len(UNITS), 8)),
        w_own=dma((len(UNITS),)),
        both=vm((2, BLOCK, BLOCK), F32),
    )
    for key, (kind, columns, size, number) in groups.items():
        pair, line = (2, 4) if kind is PairFirst else (4, 2)
        scratch["pair" + key] = vm((number, size // pair, columns), BF)
        scratch["line" + key] = vm((number, 2, size // line, columns), BF)
    names = list(ins) + list(outs) + list(scratch)
    wout, win, wo, qkv, vec, summed, pulled = pl.pallas_call(
        functools.partial(layer_kernel, count, rows, names),
        out_shape=[jax.ShapeDtypeStruct(o[0], o[1]) for o in outs.values()],
        in_specs=[i[1] for i in ins.values()],
        out_specs=[o[2] for o in outs.values()],
        scratch_shapes=list(scratch.values()),
        compiler_params=pltpu.CompilerParams(
            collective_id=0, has_side_effects=True, vmem_limit_bytes=62 * 2**20
        ),
    )(*[i[0] for i in ins.values()])
    return finish(x_in, grad_out, b_out, wout, win, wo, qkv, vec, summed, pulled)


def finish_kernel(
    x_in, g_in, b_out, wout, win, wo, qkv, vec, summed, pulled,
    mixed, grad_input, gain, bias, qkv_out, wo_out, win_out, bin_out, wout_out, bout_out,
):
    wout_out[...] = wout[...].astype(F32)
    win_out[...] = win[...].astype(F32)
    wo_out[...] = wo[...].astype(F32)
    qkv_out[...] = qkv[...].astype(F32)
    mixed[...] = (x_in[...].astype(F32) + summed[...] + b_out[...]).astype(BF)
    grad_input[...] = pulled[...] + g_in[...].astype(F32)

    @pl.when(pl.program_id(0) == 0)
    def _():
        gain[...] = vec[1:2, 0:BLOCK]
        bias[...] = vec[1:2, BLOCK : 2 * BLOCK]
        bout_out[...] = vec[1:2, 2 * BLOCK : 3 * BLOCK]
        bin_out[...] = vec[0:1, :]


def finish(x_in, grad_out, b_out, wout, win, wo, qkv, vec, summed, pulled):
    steps = FINISH_STEPS

    def split(shape):
        if len(shape) == 3:
            return pl.BlockSpec((shape[0], shape[1] // steps, shape[2]), lambda i: (0, i, 0))
        return pl.BlockSpec((shape[0] // steps, shape[1]), lambda i: (i, 0))

    def whole(shape):
        return pl.BlockSpec(shape, lambda i: (0,) * len(shape))

    def struct(shape, kind=F32):
        return jax.ShapeDtypeStruct(shape, kind)

    row = (1, BLOCK)
    outs = pl.pallas_call(
        finish_kernel,
        grid=(steps,),
        in_specs=[
            split(x_in.shape),
            split(grad_out.shape),
            whole(row),
            split(wout.shape),
            split(win.shape),
            split(wo.shape),
            split(qkv.shape),
            whole(vec.shape),
            split(summed.shape),
            split(pulled.shape),
        ],
        out_specs=[
            split(x_in.shape),
            split(x_in.shape),
            whole(row),
            whole(row),
            split(qkv.shape),
            split(wo.shape),
            split(win.shape),
            whole((1, vec.shape[1])),
            split(wout.shape),
            whole(row),
        ],
        out_shape=[
            struct(x_in.shape, BF),
            struct(x_in.shape),
            struct(row),
            struct(row),
            struct(qkv.shape),
            struct(wo.shape),
            struct(win.shape),
            struct((1, vec.shape[1])),
            struct(wout.shape),
            struct(row),
        ],
        compiler_params=pltpu.CompilerParams(vmem_limit_bytes=62 * 2**20),
    )(x_in, grad_out, b_out.reshape(row), wout, win, wo, qkv, vec, summed, pulled)
    outs = list(outs)
    for i in (2, 3, 7, 9):
        outs[i] = outs[i].reshape(-1)
    return tuple(outs)


def solution(mesh):
    return jax.shard_map(
        shards,
        mesh=mesh,
        in_specs=(
            P("seq", "tp"),
            P(),
            P(),
            P(None, None, "tp"),
            P("tp", None),
            P(None, "tp"),
            P("tp"),
            P("tp", None),
            P("tp"),
            P("seq", "tp"),
            P("seq"),
            P("seq"),
        ),
        out_specs=(
            P("seq", "tp"),
            P("seq", "tp"),
            P("tp"),
            P("tp"),
            P(None, None, "tp"),
            P("tp", None),
            P(None, "tp"),
            P("tp"),
            P("tp", None),
            P("tp"),
        ),
        check_vma=False,
    )
```

```python
import functools
from types import SimpleNamespace

import jax
import jax.numpy as jnp
import numpy as np
from jax import lax
from jax.experimental import pallas as pl
from jax.experimental.pallas import tpu as pltpu
from jax.sharding import PartitionSpec as P

PACK = 1024
LOG2E = 1.4426950408889634
EPSILON = 1e-05
BLOCK = 256
MESH = pl.DeviceIdType.MESH
BF = jnp.bfloat16
F32 = jnp.float32


class Ring:
    def __init__(self, seq_count):
        self.count = seq_count
        self.m = seq_count // 2
        self.s = lax.axis_index("seq")
        self.t = lax.axis_index("tp")
        self.z = self.s // 2
        self.x = self.s % 2
        low = (self.z < self.m // 2).astype(jnp.int32)
        self.near = low
        self.far = 1 - low

    def at(self, z, x):
        return (z * 2 + x, self.t)

    def peer(self):
        return self.at(self.z, 1 - self.x)

    def step(self, piece, sign):
        return self.at(self.z + sign * (2 * piece - 1), self.x)


def aligned(value):
    return pl.multiple_of(value, 16)


def add_rows(acc, acc_first, got, rows):
    step = 16 if rows % 32 else 32

    def body(i, carry):
        at = pl.ds(aligned(acc_first + i * step), step)
        here = pl.ds(aligned(i * step), step)
        acc[at, :] = (acc[at, :].astype(jnp.float32) + got[here, :].astype(jnp.float32)).astype(
            acc.dtype
        )
        return carry

    lax.fori_loop(0, rows // step, body, 0)


class Unit:
    def __init__(self, ring, index, part, out, out_first, rows, pair_buf, line_buf, send, recv, own):
        self.r, self.u = ring, index
        self.part, self.out, self.out_first, self.rows = part, out, out_first, rows
        self.pair_buf, self.line_buf = pair_buf, line_buf
        self.send, self.recv, self.own = send, recv, own

    def copy(self, src, dst, kind, to, send_kind=None):
        return pltpu.make_async_remote_copy(
            src_ref=src,
            dst_ref=dst,
            send_sem=self.send.at[self.u, kind if send_kind is None else send_kind],
            recv_sem=self.recv.at[self.u, kind],
            device_id=to,
            device_id_type=MESH,
        )

    def p(self, first, rows):
        return self.part.at[pl.ds(aligned(first), rows)]

    def o(self, first, rows):
        return self.out.at[pl.ds(aligned(self.out_first + first), rows)]

    def keep(self, first, rows):
        return pltpu.make_async_copy(self.p(first, rows), self.o(first, rows), self.own.at[self.u])


class PairFirst(Unit):
    def pair(self):
        half = self.rows // 2
        return self.copy(self.p((1 - self.r.x) * half, half), self.pair_buf, 0, self.r.peer())

    def first_row(self, piece, member):
        return member * (self.rows // 2) + piece * (self.rows // 4)

    def line(self, piece):
        return self.copy(
            self.p(self.first_row(piece, self.r.x), self.rows // 4),
            self.line_buf.at[piece],
            1 + piece,
            self.r.step(piece, 1),
        )

    def result(self, piece, origin):
        at = self.p if origin else self.o
        return at(self.first_row(piece, self.r.x), self.rows // 4)

    def back(self, piece, origin):
        dst = self.result(piece, False)
        return self.copy(self.result(piece, origin), dst, 3 + piece, self.r.step(piece, -1))

    def over(self, piece, origin):
        dst = self.result(piece, False)
        return self.copy(self.result(piece, origin), dst, 5 + piece, self.r.peer())

    def add(self, piece):
        self.line(piece).wait_recv()
        row = self.first_row(piece, self.r.x)
        add_rows(self.part, row, self.line_buf.at[piece], self.rows // 4)

    def start(self):
        self.pair().start()

    def paired(self):
        half = self.rows // 2
        self.pair().wait_recv()
        add_rows(self.part, self.r.x * half, self.pair_buf, half)
        if self.end:
            self.line(self.r.near).start()

    def chain_near(self):
        if not self.end:
            self.add(self.r.near)
            self.line(self.r.near).start()

    def chain_far(self):
        piece = self.r.far
        self.add(piece)
        if self.end:
            self.back(piece, True).start()
            self.over(piece, True).start()
            self.keep(self.first_row(piece, self.r.x), self.rows // 4).start()
        else:
            self.line(piece).start()

    def back_near(self):
        piece = self.r.far
        if not self.end:
            self.back(piece, False).wait_recv()
            self.back(piece, False).start()
            self.over(piece, False).start()

    def back_far(self):
        piece = self.r.near
        self.back(piece, False).wait_recv()
        if not self.end:
            self.back(piece, False).start()
        self.over(piece, False).start()

    def finish(self):
        quarter = self.rows // 4
        for piece in (0, 1):
            row = self.first_row(piece, 1 - self.r.x)
            self.copy(self.o(row, quarter), self.o(row, quarter), 5 + piece, self.r.peer()).wait_recv()
            self.over(piece, False).wait_send()
        self.pair().wait_send()
        self.line(self.r.near).wait_send()
        self.back(self.r.far, False).wait_send()
        if self.end:
            self.keep(self.first_row(self.r.far, self.r.x), quarter).wait()
        else:
            self.line(self.r.far).wait_send()
            self.back(self.r.near, False).wait_send()


class LineFirst(Unit):
    def line(self, piece):
        half = self.rows // 2
        return self.copy(
            self.p(piece * half, half), self.line_buf.at[piece], 1 + piece, self.r.step(piece, 1)
        )

    def row_of(self, piece, member):
        return piece * (self.rows // 2) + member * (self.rows // 4)

    def pair(self, piece):
        quarter = self.rows // 4
        return self.copy(
            self.p(self.row_of(piece, 1 - self.r.x), quarter), self.pair_buf, 0, self.r.peer()
        )

    def result(self, piece, member, origin):
        at = self.p if origin else self.o
        return at(self.row_of(piece, member), self.rows // 4)

    def over(self, piece, member, origin):
        dst = self.result(piece, member, False)
        return self.copy(self.result(piece, member, origin), dst, 3, self.r.peer())

    def back(self, piece, member, origin):
        dst = self.result(piece, member, False)
        to = self.r.step(piece, -1)
        return self.copy(self.result(piece, member, origin), dst, 4 + 2 * piece + member, to)

    def add(self, piece):
        half = self.rows // 2
        self.line(piece).wait_recv()
        add_rows(self.part, piece * half, self.line_buf.at[piece], half)

    def start(self):
        if self.end:
            self.line(self.r.near).start()

    def chain_near(self):
        if not self.end:
            self.add(self.r.near)
            self.line(self.r.near).start()

    def chain_far(self):
        piece = self.r.far
        self.add(piece)
        if self.end:
            self.pair(piece).start()
        else:
            self.line(piece).start()

    def exchanged(self):
        piece = self.r.far
        quarter = self.rows // 4
        if self.end:
            self.pair(piece).wait_recv()
            row = self.row_of(piece, self.r.x)
            add_rows(self.part, row, self.pair_buf, quarter)
            self.over(piece, self.r.x, True).start()
            self.back(piece, self.r.x, True).start()
            self.keep(row, quarter).start()

    def back_near(self):
        piece = self.r.far
        other = 1 - self.r.x
        if self.end:
            self.over(piece, other, False).wait_recv()
            self.back(piece, other, False).start()
        else:
            for member in (self.r.x, other):
                self.back(piece, member, False).wait_recv()
                self.back(piece, member, False).start()

    def back_far(self):
        piece = self.r.near
        for member in (self.r.x, 1 - self.r.x):
            self.back(piece, member, False).wait_recv()
            if not self.end:
                self.back(piece, member, False).start()

    def finish(self):
        self.line(self.r.near).wait_send()
        for member in (0, 1):
            self.back(self.r.far, member, False).wait_send()
        if self.end:
            piece = self.r.far
            self.pair(piece).wait_send()
            self.over(piece, self.r.x, False).wait_send()
            self.keep(self.row_of(piece, self.r.x), self.rows // 4).wait()
        else:
            self.line(self.r.far).wait_send()
            for member in (0, 1):
                self.back(self.r.near, member, False).wait_send()


class MiddleLast(LineFirst):
    def by_place(self, run):
        middle = self.r.m // 2
        if self.end:
            run(False)
        elif middle == 2:
            run(True)
        else:
            owner = (self.r.z == middle - 1) | (self.r.z == middle)
            pl.when(owner)(lambda: run(True))
            pl.when(jnp.logical_not(owner))(lambda: run(False))

    def inner(self):
        return self.r.step(self.r.near, 1)

    def outer(self):
        return self.r.step(self.r.near, -1)

    def line(self, piece, slot):
        half = self.rows // 2
        return self.copy(
            self.p(piece * half, half), self.line_buf.at[slot], 1 + slot, self.inner()
        )

    def add(self, piece, slot):
        half = self.rows // 2
        self.line(piece, slot).wait_recv()
        add_rows(self.part, piece * half, self.line_buf.at[slot], half)

    def over(self, piece, member, origin):
        dst = self.result(piece, member, False)
        return self.copy(self.result(piece, member, origin), dst, 4, self.r.peer())

    def back(self, piece, member, origin, outward, again=False):
        dst = self.result(piece, member, False)
        kind = 5 + 2 * piece + member
        to = self.outer() if outward else self.inner()
        src = self.result(piece, member, origin)
        return self.copy(src, dst, kind, to, 9 + member if again else kind)

    def start(self):
        if self.end:
            self.line(self.r.near, self.r.near).start()
            self.line(self.r.far, self.r.far).start()

    def chain_near(self):
        def run(owner):
            near, far = self.r.near, self.r.far
            self.add(near, near)
            self.line(near, 2 if owner else near).start()
            if not owner:
                self.add(far, far)
                self.line(far, far).start()

        if not self.end:
            self.by_place(run)

    def chain_far(self):
        def run(owner):
            if owner:
                self.add(self.r.far, self.r.far)
                self.add(self.r.far, 2)
                self.pair(self.r.far).start()

        self.by_place(run)

    def own_back(self, member, origin):
        self.back(self.r.far, member, origin, False).start()
        self.back(self.r.far, member, origin, True, True).start()

    def exchanged(self):
        def run(owner):
            if owner:
                piece, quarter = self.r.far, self.rows // 4
                self.pair(piece).wait_recv()
                row = self.row_of(piece, self.r.x)
                add_rows(self.part, row, self.pair_buf, quarter)
                self.over(piece, self.r.x, True).start()
                self.own_back(self.r.x, True)
                self.keep(row, quarter).start()

        self.by_place(run)

    def back_near(self):
        def run(owner):
            if owner:
                other = 1 - self.r.x
                self.over(self.r.far, other, False).wait_recv()
                self.own_back(other, False)

        self.by_place(run)

    def back_far(self):
        def run(owner):
            for piece in (self.r.near,) if owner else (self.r.far, self.r.near):
                for member in (self.r.x, 1 - self.r.x):
                    self.back(piece, member, False, False).wait_recv()
                    if not self.end:
                        self.back(piece, member, False, True).start()

        self.by_place(run)

    def finish(self):
        def run(owner):
            near, far = self.r.near, self.r.far
            self.line(near, 2 if owner else near).wait_send()
            if not owner:
                self.line(far, far).wait_send()
            if not self.end:
                for member in (0, 1):
                    self.back(near, member, False, True).wait_send()
                    self.back(far, member, False, True).wait_send()
            if owner:
                for member in (0, 1):
                    self.back(far, member, False, True, True).wait_send()
                self.pair(far).wait_send()
                self.over(far, self.r.x, False).wait_send()
                self.keep(self.row_of(far, self.r.x), self.rows // 4).wait()

        self.by_place(run)


ROLES = ("start", "paired", "chain_near", "chain_far", "exchanged", "back_near", "back_far", "finish")


UNITS = (
    (LineFirst, -1, 0, 256),
    (PairFirst, -1, 256, 256),
    (PairFirst, -1, 512, 256),
    (LineFirst, -1, 768, 256),
    (PairFirst, -1, 1024, 256),
    (LineFirst, -1, 1280, 256),
    (PairFirst, -1, 1536, 256),
    (LineFirst, -1, 1792, 256),
    (LineFirst, -1, 2048, 256),
    (PairFirst, 0, 0, 1024),
    (PairFirst, 1, 0, 1024),
    (PairFirst, 2, 0, 1024),
)

STEPS = (
    (1, ((1, 0),), ()),
    (0, ((0, 0),), ()),
    (3, (), ()),
    (2, (), ()),
    (7, ((7, 0), (2, 0)), ((1, 0),)),
    (6, (), ((2, 0), (6, 0))),
    (4, (), ()),
    (5, (), ((0, 2),)),
    (27, ((5, 0), (4, 0)), ()),
    (28, ((3, 0), (6, 0)), ()),
    (8, (), ((7, 2),)),
    (9, (), ((0, 3),)),
    (10, ((2, 1),), ((5, 2), (4, 0))),
    (24, (), ((7, 3),)),
    (11, (), ()),
    (25, ((1, 1),), ()),
    (12, ((4, 1), (0, 3), (6, 1)), ((5, 3), (2, 1), (2, 2))),
    (13, (), ((3, 2), (2, 3), (1, 1))),
    (29, ((8, 0), (7, 3)), ((4, 1), (4, 2), (6, 1))),
    (26, ((5, 3), (0, 4)), ((1, 2), (6, 2), (3, 3))),
    (31, (), ((8, 2),)),
    (18, ((7, 4),), ((1, 3),)),
    (23, (), ((11, 0), (10, 0))),
    (21, ((10, 0),), ((9, 0), (6, 3))),
    (19, ((0, 5), (7, 5), (9, 0), (11, 0), (2, 3), (1, 3), (3, 3)), ((8, 3), (4, 3), (0, 5), (7, 5))),
    (20, ((10, 1),), ()),
    (16, (), ((0, 6), (10, 1), (2, 5))),
    (14, ((9, 1), (5, 4), (11, 1)), ((11, 1), (7, 6), (9, 1), (10, 2), (1, 5), (9, 2), (10, 3), (2, 6), (11, 2), (1, 6), (6, 5))),
    (32, ((6, 3),), ((9, 3), (11, 3), (4, 5), (5, 5))),
    (35, ((4, 3),), ((6, 6),)),
    (15, (), ((10, 5),)),
    (17, ((5, 5), (8, 3), (10, 3)), ((4, 6),)),
    (22, ((3, 4), (9, 3), (0, 6), (11, 3), (3, 5), (8, 4), (6, 6), (1, 6), (4, 6), (8, 5)), ()),
    (33, ((2, 6), (7, 6), (10, 6)), ((5, 6), (9, 5), (11, 5), (10, 6), (3, 5), (9, 6))),
    (34, (), ((11, 6), (8, 5))),
    (30, ((9, 6), (11, 6)), ((3, 6),)),
    (36, ((8, 6), (3, 6), (5, 6)), ((8, 6),)),
)


def greet(ring):
    barrier = pltpu.get_barrier_semaphore()
    s, t, count = ring.s, ring.t, ring.count

    def signal(to):
        pl.semaphore_signal(barrier, inc=1, device_id=to, device_id_type=MESH)

    signal((s, mate(t, 1)))
    signal((s, mate(t, 2)))
    total = jnp.int32(2)
    bit = 1
    while bit < count:
        signal((mate(s, bit), t))
        total = total + 1
        bit *= 2
    for hop in (-2, -1, 1, 2):
        ok = (s + hop >= 0) & (s + hop < count)

        @pl.when(ok)
        def _():
            signal((s + hop, t))

        total = total + ok.astype(jnp.int32)
    pl.semaphore_wait(barrier, total)


def mate(place, bit):
    return place + bit - 2 * bit * ((place // bit) % 2)


def dot(a, b):
    return jnp.dot(a, b, preferred_element_type=F32)


def dot_rows(a, b):
    return lax.dot_general(a, b, (((0,), (0,)), ((), ())), preferred_element_type=F32)


def dot_columns(a, b):
    return lax.dot_general(a, b, (((1,), (1,)), ((), ())), preferred_element_type=F32)


def layer_kernel(
    count, rows, names, *refs
):
    r = SimpleNamespace(**dict(zip(names, refs)))
    ring = Ring(count)
    s, t = ring.s, ring.t
    blocks = rows // BLOCK
    per_pack = PACK // BLOCK
    x_all, g_all, ln = r.x_all, r.g_all, r.ln
    wqkv, wo, win, wout = r.wqkv, r.wo, r.win, r.wout
    width, hidden = win.shape
    hidden_tiles = hidden // BLOCK
    width_tiles = width // BLOCK

    def blk(b):
        return pl.ds(b * BLOCK, BLOCK) if isinstance(b, int) else pl.ds(pl.multiple_of(b * BLOCK, BLOCK), BLOCK)

    loads = {}

    def load(name, src, dst):
        copy = pltpu.make_async_copy(src, dst, r.load_sem.at[len(loads)])
        loads[name] = copy
        copy.start()

    load("x", r.x_in, x_all.at[:, blk(t)])
    load("wqkv", r.wqkv_in, wqkv)
    load("win", r.win_in, win)
    load("g", r.g_in, g_all.at[:, blk(t)])
    load("wout", r.wout_in, wout)
    load("wo", r.wo_in, wo)
    for b in range(blocks):
        place = (blocks * s + b) % per_pack
        load(("cos", b), r.cos_in.at[place], r.cos.at[b])
        load(("sin", b), r.sin_in.at[place], r.sin.at[b])
    greet(ring)

    def gather(which, b, kind):
        src_ref, whole = ((r.x_in, x_all), (r.g_in, g_all))[which]
        to = mate(t, 2) if kind == 1 else mate(t, 1)
        shard = mate(t, 2) if kind == 2 else t
        dst = whole.at[blk(b), blk(shard)]
        src = dst if kind == 2 else src_ref.at[blk(b)]
        return pltpu.make_async_remote_copy(
            src_ref=src,
            dst_ref=dst,
            send_sem=r.ag_send.at[which, b, kind],
            recv_sem=r.ag_recv.at[which, b, kind],
            device_id=(s, to),
            device_id_type=MESH,
        )

    for which in (0, 1):
        for b in range(blocks):
            gather(which, b, 1).start()
            gather(which, b, 0).start()
    r.dk[...] = jnp.zeros(r.dk.shape, F32)
    r.dv[...] = jnp.zeros(r.dv.shape, F32)

    def relay(which, b):
        gather(which, b, 1).wait_recv()
        gather(which, b, 2).start()

    def arrived(which, b):
        gather(which, b, 0).wait_recv()
        gather(which, b, 2).wait_recv()

    lane = lax.broadcasted_iota(jnp.int32, (BLOCK, BLOCK), 1)
    gain_own = r.gain[:, blk(t)]

    def norm(b):
        xb = x_all[blk(b), :].astype(F32)
        mean = jnp.mean(xb, -1, keepdims=True)
        center = xb - mean
        inverse = lax.rsqrt(jnp.mean(center * center, -1, keepdims=True) + EPSILON)
        ln[blk(b), :] = (center * inverse * r.gain[...] + r.bias[...]).astype(BF)
        own = x_all[blk(b), blk(t)].astype(F32)
        r.normed[blk(b), :] = (own - mean) * inverse
        r.inv[blk(b), :] = jnp.broadcast_to(inverse, (BLOCK, 128))

    def turn(v, b, sense):
        cosine = jnp.concatenate([r.cos[b]] * 2, 1)
        sine = jnp.concatenate([r.sin[b]] * 2, 1)
        swapped = jnp.where(lane % 2 == 0, pltpu.roll(v, BLOCK - 1, 1), pltpu.roll(v, 1, 1))
        return v * cosine + sense * sine * swapped

    def goes_on(place, b):
        return ((blocks * place + b) // per_pack == (blocks * (place + 1)) // per_pack) & (
            place < count - 1
        )

    def forward(b, which):
        here, there = blk(blocks + b), blk(b)
        if which == 2:
            src, dst = r.kt.at[blocks + b], r.kt.at[b]
        else:
            ref = (r.kb, r.vb)[which]
            src, dst = ref.at[here], ref.at[there]
        return pltpu.make_async_remote_copy(
            src_ref=src,
            dst_ref=dst,
            send_sem=r.kv_send.at[b, which],
            recv_sem=r.kv_recv.at[b, which],
            device_id=(s + 1, t),
            device_id_type=MESH,
        )

    def row_of(ref, b):
        return ref[blk(b)].reshape(1, BLOCK)

    def project(b):
        lnb = ln[blk(b), :]
        tags = jnp.where(row_of(r.pad, b) == 1, row_of(r.seg, b), -1)
        r.kt[blocks + b] = jnp.broadcast_to(tags, (8, BLOCK))
        r.kb[blk(blocks + b), :] = turn(dot(lnb, wqkv[1]), b, 1.0).astype(BF)
        r.vb[blk(blocks + b), :] = dot(lnb, wqkv[2]).astype(BF)

        @pl.when(goes_on(s, b))
        def _():
            for which in range(3):
                forward(b, which).start()

        r.q[blk(b), :] = turn(dot(lnb, wqkv[0]), b, 1.0).astype(BF)

    for b in range(blocks):
        relay(0, b)
    loads["x"].wait()
    for b in range(blocks):
        arrived(0, b)
        norm(b)
        if b == 0:
            loads["wqkv"].wait()
            for b2 in range(blocks):
                loads[("cos", b2)].wait()
                loads[("sin", b2)].wait()
        project(b)

    loads["win"].wait()

    def expand(j):
        for b in range(blocks):
            pre = dot(ln[blk(b), :], win[:, blk(j)]) + r.b_in[:, blk(j)]
            scale = 0.7978845608028654
            square = pre * pre
            th = jnp.tanh(scale * (pre + 0.044715 * (square * pre)))
            half = 0.5 * (1.0 + th)
            r.act[blk(b), blk(j)] = (pre * half).astype(BF)
            r.dg[blk(b), blk(j)] = half + (0.5 * scale) * pre * (1.0 - th * th) * (
                1.0 + (3 * 0.044715) * square
            )

    for j in range(hidden_tiles):
        expand(j)
        if j < blocks:
            relay(1, j)
    loads["g"].wait()
    loads["wout"].wait()
    loads["wo"].wait()
    for b in range(blocks):
        arrived(1, b)

    units = []
    slots = {}
    for u, (kind, slab, first, size) in enumerate(UNITS):
        if slab < 0:
            out, base = (
                (r.wout_out, 0)
                if first < hidden
                else (r.win_out, hidden)
                if first < hidden + width
                else (r.wo_out, hidden + width)
            )
            part, out_first = r.wide.at[pl.ds(first, size)], first - base
        else:
            part, out, out_first = r.tall.at[slab, pl.ds(first, size)], r.qkv_out.at[slab], first
        key = group(kind, slab, size)
        slot = slots.get(key, 0)
        slots[key] = slot + 1
        units.append(
            kind(
                ring,
                u,
                part,
                out,
                out_first,
                size,
                getattr(r, "pair" + key).at[slot],
                getattr(r, "line" + key).at[slot],
                r.w_send,
                r.w_recv,
                r.w_own,
            )
        )

    def grad_out_tile(j):
        bin_sum = jnp.zeros((1, BLOCK), F32)
        for b in range(blocks):
            pulled = dot_columns(g_all[blk(b), :], wout[blk(j), :])
            gh = (pulled * r.dg[blk(b), blk(j)]).astype(BF)
            r.gh[blk(b), blk(j)] = gh
            bin_sum = bin_sum + jnp.sum(gh.astype(F32), 0, keepdims=True)
        r.vec[0, 0:1, blk(j)] = bin_sum
        r.wide[blk(j), :] = dot_rows(r.act[:, blk(j)], g_all[...]).astype(BF)

    def grad_in_tile(j):
        r.wide[blk(hidden_tiles + j), :] = dot_rows(ln[:, blk(j)], r.gh[...]).astype(BF)

    def context_pull():
        for b in range(blocks):
            r.gc[blk(b), :] = dot_columns(g_all[blk(b), :], wo[...])
        own = g_all[:, blk(t)].astype(F32)
        r.vec[0, 1:2, blk(2)] = jnp.sum(own, 0, keepdims=True)

    def receive_keys():
        for b in range(blocks):

            @pl.when(goes_on(s - 1, b) & (s > 0))
            def _():
                for which in range(3):
                    forward(b, which).wait_recv()

    def attend(i, part):
        held = (blocks * s + i) % per_pack + 1
        for nb in range(1, per_pack + 1):
            if blocks + i - nb + 1 >= 0:

                @pl.when(held == nb)
                def _():
                    attend_window(i, nb, part)

    def attend_window(i, nb, part):
        n = nb * BLOCK
        first = blocks + i - nb + 1
        window = pl.ds(first * BLOCK, n)
        if part == 0:
            row = lax.broadcasted_iota(jnp.int32, (BLOCK, BLOCK), 0)
            wide_row = jnp.broadcast_to(row_of(r.seg, i), (128, BLOCK))
            seg = wide_row.T[:, 0:1]
            for c in range(nb):
                same = r.kt[first + c, 0:1, :] == seg
                if c == nb - 1:
                    same = (same & (lane <= row)) | (lane == row)
                r.mask[:, blk(c)] = jnp.where(same, 0.0, -1e30)
        qb = r.q[blk(i), :]
        gcb = r.gc[blk(i), :]
        kw = r.kb[window, :]
        vw = r.vb[window, :]

        def head(h, carry):
            mine = lane // 64 == h
            at = pl.ds(pl.multiple_of(h * BLOCK, BLOCK), BLOCK)
            qm = jnp.where(mine, qb, jnp.zeros_like(qb))
            r.qm[at, :] = qm
            logit = dot_columns(qm, kw) * (0.125 * LOG2E) + r.mask[:, :n]
            ceiling = jnp.floor(jnp.max(logit, -1, keepdims=True))
            weight = jnp.exp2(logit - ceiling)
            total = 1.0 / jnp.sum(weight, -1, keepdims=True)
            low = weight.astype(BF)
            r.wl[at, :n] = low
            context = dot(low, vw) * total
            gm = jnp.where(mine, gcb, 0.0)
            ga = (gm * total).astype(BF)
            r.gm[at, :] = ga
            offset = jnp.sum(gm * context, -1, keepdims=True) * total
            ds = (weight * (dot_columns(ga, vw) - offset)).astype(BF)
            r.ds[at, :n] = ds
            dq = dot(ds, kw)
            ctx, dqs = carry
            return (jnp.where(mine, context, ctx), jnp.where(mine, dq, dqs))

        zero = jnp.zeros((BLOCK, BLOCK), F32)
        start = (zero, zero) if part == 0 else (r.both[0], r.both[1])
        ctx, dqs = lax.fori_loop(2 * part, 2 * part + 2, head, start)
        if part == 0:
            r.both[0] = ctx
            r.both[1] = dqs
            return
        r.ctx[blk(i), :] = ctx.astype(BF)
        r.g3[blk(i), 0:BLOCK] = turn(0.125 * dqs, i, -1.0).astype(BF)
        for c in range(nb):
            r.dk[blk(first + c), :] += dot_rows(r.ds[:, blk(c)], r.qm[...])
            r.dv[blk(first + c), :] += dot_rows(r.wl[:, blk(c)], r.gm[...])

    def backward(b, which):
        return pltpu.make_async_remote_copy(
            src_ref=r.dks.at[which, blk(b)],
            dst_ref=r.dkr.at[which, blk(b)],
            send_sem=r.dk_send.at[b, which],
            recv_sem=r.dk_recv.at[b, which],
            device_id=(s - 1, t),
            device_id_type=MESH,
        )

    def send_key_grads(i):
        for b in range(blocks):

            @pl.when(goes_on(s - 1, b) & (s > 0) & ((blocks * s) % per_pack == per_pack - 1 - i))
            def _():
                for which, ref in enumerate((r.dk, r.dv)):
                    r.dks[which, blk(b), :] = ref[blk(b), :].astype(BF)
                    backward(b, which).start()

    def grad_wo_tile():
        r.wide[blk(2 * hidden_tiles), :] = dot_rows(r.ctx[...], g_all[...]).astype(BF)

    def split(which, slot):
        to = mate(t, 2) if slot == 2 else mate(t, 1)
        return pltpu.make_async_remote_copy(
            src_ref=r.tp_out.at[which, slot],
            dst_ref=r.tp_got.at[which, slot],
            send_sem=r.tp_send.at[which, slot],
            recv_sem=r.tp_recv.at[which, slot],
            device_id=(s, to),
            device_id_type=MESH,
        )

    def share(which, owner, b):
        if which == 0:
            return dot(r.ctx[blk(b), :], wo[:, blk(owner)]) + dot(
                r.act[blk(b), :], wout[:, blk(owner)]
            )
        total = dot_columns(r.gh[blk(b), :], win[blk(owner), :])
        for k in range(3):
            total = total + dot_columns(r.g3[blk(b), blk(k)], wqkv[k, blk(owner), :])
        return total

    far_mate = mate(mate(t, 1), 2)

    def split_near(which):
        for slot, owner in ((1, far_mate), (0, mate(t, 1))):
            for b in range(blocks):
                r.tp_out[which, slot, blk(b), :] = share(which, owner, b).astype(BF)
            split(which, slot).start()

    def split_far(which):
        split(which, 1).wait_recv()
        for b in range(blocks):
            mine = share(which, mate(t, 2), b)
            r.tp_out[which, 2, blk(b), :] = (
                mine + r.tp_got[which, 1, blk(b), :].astype(F32)
            ).astype(BF)
        split(which, 2).start()

    def split_own(which):
        for b in range(blocks):
            r.tp_sum[which, blk(b), :] = share(which, t, b)

    def split_join(which):
        split(which, 0).wait_recv()
        split(which, 2).wait_recv()
        for b in range(blocks):
            r.tp_sum[which, blk(b), :] += r.tp_got[which, 0, blk(b), :].astype(F32) + r.tp_got[which, 2, blk(b), :].astype(F32)

    def join_branch():
        split_join(0)
        r.summed[...] = r.tp_sum[0]

    def join_key_grads():
        for b in range(blocks):
            for which, ref in enumerate((r.dk, r.dv)):

                @pl.when(goes_on(s, b))
                def _():
                    backward_in = pltpu.make_async_remote_copy(
                        src_ref=r.dks.at[which, blk(b)],
                        dst_ref=r.dkr.at[which, blk(b)],
                        send_sem=r.dk_send.at[b, which],
                        recv_sem=r.dk_recv.at[b, which],
                        device_id=(s + 1, t),
                        device_id_type=MESH,
                    )
                    backward_in.wait_recv()
                    ref[blk(blocks + b), :] += r.dkr[which, blk(b), :].astype(F32)

            r.g3[blk(b), blk(1)] = turn(0.125 * r.dk[blk(blocks + b), :], b, -1.0).astype(BF)
            r.g3[blk(b), blk(2)] = r.dv[blk(blocks + b), :].astype(BF)

    def grad_qkv_tiles(part):
        half = width_tiles // 2
        for j in range(part * half, part * half + half):
            tile = dot_rows(ln[:, blk(j)], r.g3[...]).astype(BF)
            for k in range(3):
                r.tall[k, blk(j), :] = tile[:, k * BLOCK : (k + 1) * BLOCK]

    def stats_copy(level):
        return pltpu.make_async_remote_copy(
            src_ref=r.stats.at[level],
            dst_ref=r.stats_got.at[level],
            send_sem=r.st_send.at[level],
            recv_sem=r.st_recv.at[level],
            device_id=(s, mate(t, 1 << level)),
            device_id_type=MESH,
        )

    def norm_grad():
        split_join(1)
        gain_sum = jnp.zeros((1, BLOCK), F32)
        bias_sum = jnp.zeros((1, BLOCK), F32)
        lane_one = lax.broadcasted_iota(jnp.int32, (BLOCK, 128), 1)
        for b in range(blocks):
            grad = r.tp_sum[1, blk(b), :]
            normed = r.normed[blk(b), :]
            gain_sum = gain_sum + jnp.sum(grad * normed, 0, keepdims=True)
            bias_sum = bias_sum + jnp.sum(grad, 0, keepdims=True)
            hat = grad * gain_own
            first = jnp.sum(hat, -1, keepdims=True)
            second = jnp.sum(hat * normed, -1, keepdims=True)
            both = jnp.where(lane_one == 0, first, second)
            r.stats[0, :, blk(b)] = both.T[0:8, :]
        r.vec[0, 1:2, blk(0)] = gain_sum
        r.vec[0, 1:2, blk(1)] = bias_sum
        stats_copy(0).start()

    def stats_join():
        stats_copy(0).wait_recv()
        r.stats[1] = r.stats[0] + r.stats_got[0]
        stats_copy(1).start()

    def input_grad():
        stats_copy(1).wait_recv()
        for b in range(blocks):
            both = (r.stats[1, :, blk(b)] + r.stats_got[1, :, blk(b)]) * (1.0 / ln.shape[1])
            columns = jnp.concatenate([both] * 16, 0).T
            hat = r.tp_sum[1, blk(b), :] * gain_own
            r.pulled[blk(b), :] = r.inv[blk(b), 0:1] * (
                hat - columns[:, 0:1] - r.normed[blk(b), :] * columns[:, 1:2]
            )

    levels = count.bit_length() - 1

    def vec_copy(level):
        return pltpu.make_async_remote_copy(
            src_ref=r.vec.at[level],
            dst_ref=r.vec_got.at[level],
            send_sem=r.v_send.at[level],
            recv_sem=r.v_recv.at[level],
            device_id=(mate(s, 1 << level), t),
            device_id_type=MESH,
        )

    def vec_start():
        vec_copy(0).start()

    def vec_step(level):
        vec_copy(level).wait_recv()
        r.vec[level + 1] = r.vec[level] + r.vec_got[level]
        if level + 1 < levels:
            vec_copy(level + 1).start()

    def vec_rest():
        for level in range(2, levels):
            vec_step(level)
        r.vec_out[...] = r.vec[levels]

    part = functools.partial
    tasks = [part(grad_out_tile, j) for j in range(hidden_tiles)]
    tasks += [part(grad_in_tile, j) for j in range(width_tiles)]
    tasks += [part(attend, i, half) for i in range(blocks) for half in (0, 1)]
    for which in (0, 1):
        tasks += [part(step, which) for step in (split_near, split_far, split_own, vec_step)]
        tasks.append(part(grad_qkv_tiles, which))
    tasks += [part(send_key_grads, i) for i in range(blocks)]
    tasks += [context_pull, receive_keys, grad_wo_tile, join_branch, join_key_grads]
    tasks += [norm_grad, stats_join, input_grad, vec_start, vec_rest]
    r.vec[0] = jnp.zeros(r.vec.shape[1:], F32)
    at_end = (ring.z == 0) | (ring.z == ring.m - 1)

    def messages(events, end):
        for who, role in events:
            units[who].end = end
            getattr(units[who], ROLES[role])()

    for task, ends, middles in STEPS:
        tasks[task]()

        @pl.when(at_end)
        def _():
            messages(ends, True)

        @pl.when(jnp.logical_not(at_end))
        def _():
            messages(middles, False)

    closing = [(u, len(ROLES) - 1) for u in range(len(units))]

    @pl.when(at_end)
    def _():
        messages(closing, True)

    @pl.when(jnp.logical_not(at_end))
    def _():
        messages(closing, False)

    for which in (0, 1):
        for b in range(blocks):
            for kind in range(3):
                gather(which, b, kind).wait_send()
        for slot in range(3):
            split(which, slot).wait_send()
        stats_copy(which).wait_send()
    for level in range(levels):
        vec_copy(level).wait_send()
    for b in range(blocks):

        @pl.when(goes_on(s, b))
        def _():
            for which in range(3):
                forward(b, which).wait_send()

        @pl.when(goes_on(s - 1, b) & (s > 0))
        def _():
            for which in range(2):
                backward(b, which).wait_send()


def group(kind, slab, size):
    return "%s%d_%d" % (kind.__name__[0], slab < 0, size)


def rotary_tables():
    places = np.arange(PACK, dtype=np.float32)
    inverse = (10000.0 ** (-(np.arange(16, dtype=np.float32) * 2.0) / 32.0)).astype(np.float32)
    phase = (places[:, None] * inverse[None, :]).astype(np.float32)
    cosine, sine = np.cos(phase), np.sin(phase)
    cos_head = np.ones((PACK, 64), np.float32)
    sin_head = np.zeros((PACK, 64), np.float32)
    cos_head[:, 0:32] = np.repeat(cosine, 2, 1)
    sin_head[:, 0:32:2] = -sine
    sin_head[:, 1:32:2] = sine
    shape = (PACK // BLOCK, BLOCK, 128)
    return (
        np.concatenate([cos_head] * 2, 1).reshape(shape),
        np.concatenate([sin_head] * 2, 1).reshape(shape),
    )


def shards(
    x_in, ln_gain, ln_bias, w_qkv, w_o, w_in, b_in, w_out, b_out, grad_out, segment_ids, pad_mask
):
    count = lax.axis_size("seq")
    rows, own_width = x_in.shape
    width = w_in.shape[0]
    hidden = w_in.shape[1]
    blocks = rows // BLOCK
    assert own_width == BLOCK and rows % BLOCK == 0 and w_qkv.shape[2] == BLOCK
    assert hidden == width == 4 * BLOCK and lax.axis_size("tp") == 4 and rows < PACK
    assert count & (count - 1) == 0 and count >= 8 and (count * rows) % PACK == 0
    cos_table, sin_table = rotary_tables()
    levels = count.bit_length() - 1
    groups = {}
    for kind, slab, first, size in UNITS:
        key = group(kind, slab, size)
        groups[key] = (kind, 1024 if slab < 0 else BLOCK, size, groups.get(key, (0, 0, 0, 0))[3] + 1)
    hbm = pl.BlockSpec(memory_space=pl.ANY)
    vmem = pl.BlockSpec(memory_space=pltpu.VMEM)
    vm = pltpu.VMEM
    dma = pltpu.SemaphoreType.DMA
    ins = dict(
        x_in=(x_in, hbm),
        g_in=(grad_out, hbm),
        gain=(ln_gain.reshape(1, -1), vmem),
        bias=(ln_bias.reshape(1, -1), vmem),
        b_in=(b_in.reshape(1, -1), vmem),
        wqkv_in=(w_qkv, hbm),
        wo_in=(w_o, hbm),
        win_in=(w_in, hbm),
        wout_in=(w_out, hbm),
        seg=(segment_ids, vmem),
        pad=(pad_mask, vmem),
        cos_in=(jnp.asarray(cos_table), hbm),
        sin_in=(jnp.asarray(sin_table), hbm),
    )
    outs = dict(
        wout_out=(w_out.shape, BF, hbm),
        win_out=(w_in.shape, BF, hbm),
        wo_out=(w_o.shape, BF, hbm),
        qkv_out=(w_qkv.shape, BF, hbm),
        vec_out=((8, width), F32, vmem),
        summed=((rows, BLOCK), F32, vmem),
        pulled=((rows, BLOCK), F32, vmem),
    )
    scratch = dict(
        x_all=vm((rows, width), BF),
        g_all=vm((rows, width), BF),
        ln=vm((rows, width), BF),
        wqkv=vm(w_qkv.shape, BF),
        wo=vm(w_o.shape, BF),
        win=vm(w_in.shape, BF),
        wout=vm(w_out.shape, BF),
        act=vm((rows, hidden), BF),
        dg=vm((rows, hidden), F32),
        gh=vm((rows, hidden), BF),
        q=vm((rows, BLOCK), BF),
        kb=vm((2 * rows, BLOCK), BF),
        vb=vm((2 * rows, BLOCK), BF),
        kt=vm((2 * blocks, 8, BLOCK), jnp.int32),
        gc=vm((rows, BLOCK), F32),
        dk=vm((2 * rows, BLOCK), F32),
        dv=vm((2 * rows, BLOCK), F32),
        ctx=vm((rows, BLOCK), BF),
        g3=vm((rows, 3 * BLOCK), BF),
        mask=vm((BLOCK, PACK), F32),
        ds=vm((4 * BLOCK, PACK), BF),
        wl=vm((4 * BLOCK, PACK), BF),
        qm=vm((4 * BLOCK, BLOCK), BF),
        gm=vm((4 * BLOCK, BLOCK), BF),
        dks=vm((2, rows, BLOCK), BF),
        dkr=vm((2, rows, BLOCK), BF),
        tp_out=vm((2, 3, rows, BLOCK), BF),
        tp_got=vm((2, 3, rows, BLOCK), BF),
        tp_sum=vm((2, rows, BLOCK), F32),
        normed=vm((rows, BLOCK), F32),
        inv=vm((rows, 128), F32),
        cos=vm((blocks, BLOCK, 128), F32),
        sin=vm((blocks, BLOCK, 128), F32),
        stats=vm((2, 8, rows), F32),
        stats_got=vm((2, 8, rows), F32),
        vec=vm((levels + 1, 8, width), F32),
        vec_got=vm((levels, 8, width), F32),
        wide=vm((9 * 256, 1024), BF),
        tall=vm((3, 1024, 256), BF),
        load_sem=dma((6 + 2 * blocks,)),
        ag_send=dma((2, blocks, 3)),
        ag_recv=dma((2, blocks, 3)),
        kv_send=dma((blocks, 3)),
        kv_recv=dma((blocks, 3)),
        dk_send=dma((blocks, 2)),
        dk_recv=dma((blocks, 2)),
        tp_send=dma((2, 3)),
        tp_recv=dma((2, 3)),
        st_send=dma((2,)),
        st_recv=dma((2,)),
        v_send=dma((levels,)),
        v_recv=dma((levels,)),
        w_send=dma((len(UNITS), 11)),
        w_recv=dma((len(UNITS), 11)),
        w_own=dma((len(UNITS),)),
        both=vm((2, BLOCK, BLOCK), F32),
    )
    for key, (kind, columns, size, number) in groups.items():
        pair, line = (2, 4) if kind is PairFirst else (4, 2)
        pieces = 3 if kind is MiddleLast else 2
        scratch["pair" + key] = vm((number, size // pair, columns), BF)
        scratch["line" + key] = vm((number, pieces, size // line, columns), BF)
    names = list(ins) + list(outs) + list(scratch)
    wout, win, wo, qkv, vec, summed, pulled = pl.pallas_call(
        functools.partial(layer_kernel, count, rows, names),
        out_shape=[jax.ShapeDtypeStruct(o[0], o[1]) for o in outs.values()],
        in_specs=[i[1] for i in ins.values()],
        out_specs=[o[2] for o in outs.values()],
        scratch_shapes=list(scratch.values()),
        compiler_params=pltpu.CompilerParams(
            collective_id=0, has_side_effects=True, vmem_limit_bytes=62 * 2**20
        ),
    )(*[i[0] for i in ins.values()])
    return finish(x_in, grad_out, b_out, wout, win, wo, qkv, vec, summed, pulled)


def finish_kernel(
    x_in, g_in, b_out, wout, win, wo, qkv, vec, summed, pulled,
    mixed, grad_input, gain, bias, qkv_out, wo_out, win_out, bin_out, wout_out, bout_out,
):
    wout_out[...] = wout[...].astype(F32)
    win_out[...] = win[...].astype(F32)
    wo_out[...] = wo[...].astype(F32)
    qkv_out[...] = qkv[...].astype(F32)
    mixed[...] = (x_in[...].astype(F32) + summed[...] + b_out[...]).astype(BF)
    grad_input[...] = pulled[...] + g_in[...].astype(F32)

    @pl.when(pl.program_id(0) == 0)
    def _():
        gain[...] = vec[1:2, 0:BLOCK]
        bias[...] = vec[1:2, BLOCK : 2 * BLOCK]
        bout_out[...] = vec[1:2, 2 * BLOCK : 3 * BLOCK]
        bin_out[...] = vec[0:1, :]


def finish(x_in, grad_out, b_out, wout, win, wo, qkv, vec, summed, pulled):
    steps = 1

    def split(shape):
        if len(shape) == 3:
            return pl.BlockSpec((shape[0], shape[1] // steps, shape[2]), lambda i: (0, i, 0))
        return pl.BlockSpec((shape[0] // steps, shape[1]), lambda i: (i, 0))

    def whole(shape):
        return pl.BlockSpec(shape, lambda i: (0,) * len(shape))

    def struct(shape, kind=F32):
        return jax.ShapeDtypeStruct(shape, kind)

    row = (1, BLOCK)
    outs = pl.pallas_call(
        finish_kernel,
        grid=(steps,),
        in_specs=[
            split(x_in.shape),
            split(grad_out.shape),
            whole(row),
            split(wout.shape),
            split(win.shape),
            split(wo.shape),
            split(qkv.shape),
            whole(vec.shape),
            split(summed.shape),
            split(pulled.shape),
        ],
        out_specs=[
            split(x_in.shape),
            split(x_in.shape),
            whole(row),
            whole(row),
            split(qkv.shape),
            split(wo.shape),
            split(win.shape),
            whole((1, vec.shape[1])),
            split(wout.shape),
            whole(row),
        ],
        out_shape=[
            struct(x_in.shape, BF),
            struct(x_in.shape),
            struct(row),
            struct(row),
            struct(qkv.shape),
            struct(wo.shape),
            struct(win.shape),
            struct((1, vec.shape[1])),
            struct(wout.shape),
            struct(row),
        ],
        compiler_params=pltpu.CompilerParams(vmem_limit_bytes=62 * 2**20),
    )(x_in, grad_out, b_out.reshape(row), wout, win, wo, qkv, vec, summed, pulled)
    outs = list(outs)
    for i in (2, 3, 7, 9):
        outs[i] = outs[i].reshape(-1)
    return tuple(outs)


def solution(mesh):
    return jax.shard_map(
        shards,
        mesh=mesh,
        in_specs=(
            P("seq", "tp"),
            P(),
            P(),
            P(None, None, "tp"),
            P("tp", None),
            P(None, "tp"),
            P("tp"),
            P("tp", None),
            P("tp"),
            P("seq", "tp"),
            P("seq"),
            P("seq"),
        ),
        out_specs=(
            P("seq", "tp"),
            P("seq", "tp"),
            P("tp"),
            P("tp"),
            P(None, None, "tp"),
            P("tp", None),
            P(None, "tp"),
            P("tp"),
            P("tp", None),
            P("tp"),
        ),
        check_vma=False,
    )
```

```python
import functools
from types import SimpleNamespace

import jax
import jax.numpy as jnp
import numpy as np
from jax import lax
from jax.experimental import pallas as pl
from jax.experimental.pallas import tpu as pltpu
from jax.sharding import PartitionSpec as P

PACK = 1024
LOG2E = 1.4426950408889634
EPSILON = 1e-05
BLOCK = 256
MESH = pl.DeviceIdType.MESH
BF = jnp.bfloat16
F32 = jnp.float32


class Ring:
    def __init__(self, seq_count):
        self.count = seq_count
        self.m = seq_count // 2
        self.s = lax.axis_index("seq")
        self.t = lax.axis_index("tp")
        self.z = self.s // 2
        self.x = self.s % 2
        low = (self.z < self.m // 2).astype(jnp.int32)
        self.near = low
        self.far = 1 - low

    def at(self, z, x):
        return (z * 2 + x, self.t)

    def peer(self):
        return self.at(self.z, 1 - self.x)

    def step(self, piece, sign):
        return self.at(self.z + sign * (2 * piece - 1), self.x)


def aligned(value):
    return pl.multiple_of(value, 16)


def add_rows(acc, acc_first, got, rows):
    step = 16 if rows % 32 else 32

    def body(i, carry):
        at = pl.ds(aligned(acc_first + i * step), step)
        here = pl.ds(aligned(i * step), step)
        acc[at, :] = (acc[at, :].astype(jnp.float32) + got[here, :].astype(jnp.float32)).astype(
            acc.dtype
        )
        return carry

    lax.fori_loop(0, rows // step, body, 0)


class Unit:
    def __init__(self, ring, index, part, out, out_first, rows, pair_buf, line_buf, send, recv, own):
        self.r, self.u = ring, index
        self.part, self.out, self.out_first, self.rows = part, out, out_first, rows
        self.pair_buf, self.line_buf = pair_buf, line_buf
        self.send, self.recv, self.own = send, recv, own

    def copy(self, src, dst, kind, to, send_kind=None):
        return pltpu.make_async_remote_copy(
            src_ref=src,
            dst_ref=dst,
            send_sem=self.send.at[self.u, kind if send_kind is None else send_kind],
            recv_sem=self.recv.at[self.u, kind],
            device_id=to,
            device_id_type=MESH,
        )

    def p(self, first, rows):
        return self.part.at[pl.ds(aligned(first), rows)]

    def o(self, first, rows):
        return self.out.at[pl.ds(aligned(self.out_first + first), rows)]

    def keep(self, first, rows):
        return pltpu.make_async_copy(self.p(first, rows), self.o(first, rows), self.own.at[self.u])


class PairFirst(Unit):
    def pair(self):
        half = self.rows // 2
        return self.copy(self.p((1 - self.r.x) * half, half), self.pair_buf, 0, self.r.peer())

    def first_row(self, piece, member):
        return member * (self.rows // 2) + piece * (self.rows // 4)

    def line(self, piece):
        return self.copy(
            self.p(self.first_row(piece, self.r.x), self.rows // 4),
            self.line_buf.at[piece],
            1 + piece,
            self.r.step(piece, 1),
        )

    def result(self, piece, origin):
        at = self.p if origin else self.o
        return at(self.first_row(piece, self.r.x), self.rows // 4)

    def back(self, piece, origin):
        dst = self.result(piece, False)
        return self.copy(self.result(piece, origin), dst, 3 + piece, self.r.step(piece, -1))

    def over(self, piece, origin):
        dst = self.result(piece, False)
        return self.copy(self.result(piece, origin), dst, 5 + piece, self.r.peer())

    def add(self, piece):
        self.line(piece).wait_recv()
        row = self.first_row(piece, self.r.x)
        add_rows(self.part, row, self.line_buf.at[piece], self.rows // 4)

    def start(self):
        self.pair().start()

    def paired(self):
        half = self.rows // 2
        self.pair().wait_recv()
        add_rows(self.part, self.r.x * half, self.pair_buf, half)
        if self.end:
            self.line(self.r.near).start()

    def chain_near(self):
        if not self.end:
            self.add(self.r.near)
            self.line(self.r.near).start()

    def chain_far(self):
        piece = self.r.far
        self.add(piece)
        if self.end:
            self.back(piece, True).start()
            self.over(piece, True).start()
            self.keep(self.first_row(piece, self.r.x), self.rows // 4).start()
        else:
            self.line(piece).start()

    def back_near(self):
        piece = self.r.far
        if not self.end:
            self.back(piece, False).wait_recv()
            self.back(piece, False).start()
            self.over(piece, False).start()

    def back_far(self):
        piece = self.r.near
        self.back(piece, False).wait_recv()
        if not self.end:
            self.back(piece, False).start()
        self.over(piece, False).start()

    def finish(self):
        quarter = self.rows // 4
        for piece in (0, 1):
            row = self.first_row(piece, 1 - self.r.x)
            self.copy(self.o(row, quarter), self.o(row, quarter), 5 + piece, self.r.peer()).wait_recv()
            self.over(piece, False).wait_send()
        self.pair().wait_send()
        self.line(self.r.near).wait_send()
        self.back(self.r.far, False).wait_send()
        if self.end:
            self.keep(self.first_row(self.r.far, self.r.x), quarter).wait()
        else:
            self.line(self.r.far).wait_send()
            self.back(self.r.near, False).wait_send()


class LineFirst(Unit):
    def line(self, piece):
        half = self.rows // 2
        return self.copy(
            self.p(piece * half, half), self.line_buf.at[piece], 1 + piece, self.r.step(piece, 1)
        )

    def row_of(self, piece, member):
        return piece * (self.rows // 2) + member * (self.rows // 4)

    def pair(self, piece):
        quarter = self.rows // 4
        return self.copy(
            self.p(self.row_of(piece, 1 - self.r.x), quarter), self.pair_buf, 0, self.r.peer()
        )

    def result(self, piece, member, origin):
        at = self.p if origin else self.o
        return at(self.row_of(piece, member), self.rows // 4)

    def over(self, piece, member, origin):
        dst = self.result(piece, member, False)
        return self.copy(self.result(piece, member, origin), dst, 3, self.r.peer())

    def back(self, piece, member, origin):
        dst = self.result(piece, member, False)
        to = self.r.step(piece, -1)
        return self.copy(self.result(piece, member, origin), dst, 4 + 2 * piece + member, to)

    def add(self, piece):
        half = self.rows // 2
        self.line(piece).wait_recv()
        add_rows(self.part, piece * half, self.line_buf.at[piece], half)

    def start(self):
        if self.end:
            self.line(self.r.near).start()

    def chain_near(self):
        if not self.end:
            self.add(self.r.near)
            self.line(self.r.near).start()

    def chain_far(self):
        piece = self.r.far
        self.add(piece)
        if self.end:
            self.pair(piece).start()
        else:
            self.line(piece).start()

    def exchanged(self):
        piece = self.r.far
        quarter = self.rows // 4
        if self.end:
            self.pair(piece).wait_recv()
            row = self.row_of(piece, self.r.x)
            add_rows(self.part, row, self.pair_buf, quarter)
            self.over(piece, self.r.x, True).start()
            self.back(piece, self.r.x, True).start()
            self.keep(row, quarter).start()

    def back_near(self):
        piece = self.r.far
        other = 1 - self.r.x
        if self.end:
            self.over(piece, other, False).wait_recv()
            self.back(piece, other, False).start()
        else:
            for member in (self.r.x, other):
                self.back(piece, member, False).wait_recv()
                self.back(piece, member, False).start()

    def back_far(self):
        piece = self.r.near
        for member in (self.r.x, 1 - self.r.x):
            self.back(piece, member, False).wait_recv()
            if not self.end:
                self.back(piece, member, False).start()

    def finish(self):
        self.line(self.r.near).wait_send()
        for member in (0, 1):
            self.back(self.r.far, member, False).wait_send()
        if self.end:
            piece = self.r.far
            self.pair(piece).wait_send()
            self.over(piece, self.r.x, False).wait_send()
            self.keep(self.row_of(piece, self.r.x), self.rows // 4).wait()
        else:
            self.line(self.r.far).wait_send()
            for member in (0, 1):
                self.back(self.r.near, member, False).wait_send()


class MiddleLast(LineFirst):
    def by_place(self, run):
        middle = self.r.m // 2
        if self.end:
            run(False)
        elif middle == 2:
            run(True)
        else:
            owner = (self.r.z == middle - 1) | (self.r.z == middle)
            pl.when(owner)(lambda: run(True))
            pl.when(jnp.logical_not(owner))(lambda: run(False))

    def inner(self):
        return self.r.step(self.r.near, 1)

    def outer(self):
        return self.r.step(self.r.near, -1)

    def line(self, piece, slot):
        half = self.rows // 2
        return self.copy(
            self.p(piece * half, half), self.line_buf.at[slot], 1 + slot, self.inner()
        )

    def add(self, piece, slot):
        half = self.rows // 2
        self.line(piece, slot).wait_recv()
        add_rows(self.part, piece * half, self.line_buf.at[slot], half)

    def over(self, piece, member, origin):
        dst = self.result(piece, member, False)
        return self.copy(self.result(piece, member, origin), dst, 4, self.r.peer())

    def back(self, piece, member, origin, outward, again=False):
        dst = self.result(piece, member, False)
        kind = 5 + 2 * piece + member
        to = self.outer() if outward else self.inner()
        src = self.result(piece, member, origin)
        return self.copy(src, dst, kind, to, 9 + member if again else kind)

    def start(self):
        if self.end:
            self.line(self.r.near, self.r.near).start()
            self.line(self.r.far, self.r.far).start()

    def chain_near(self):
        def run(owner):
            near, far = self.r.near, self.r.far
            self.add(near, near)
            self.line(near, 2 if owner else near).start()
            if not owner:
                self.add(far, far)
                self.line(far, far).start()

        if not self.end:
            self.by_place(run)

    def chain_far(self):
        def run(owner):
            if owner:
                self.add(self.r.far, self.r.far)
                self.add(self.r.far, 2)
                self.pair(self.r.far).start()

        self.by_place(run)

    def own_back(self, member, origin):
        self.back(self.r.far, member, origin, False).start()
        self.back(self.r.far, member, origin, True, True).start()

    def exchanged(self):
        def run(owner):
            if owner:
                piece, quarter = self.r.far, self.rows // 4
                self.pair(piece).wait_recv()
                row = self.row_of(piece, self.r.x)
                add_rows(self.part, row, self.pair_buf, quarter)
                self.over(piece, self.r.x, True).start()
                self.own_back(self.r.x, True)
                self.keep(row, quarter).start()

        self.by_place(run)

    def back_near(self):
        def run(owner):
            if owner:
                other = 1 - self.r.x
                self.over(self.r.far, other, False).wait_recv()
                self.own_back(other, False)

        self.by_place(run)

    def back_far(self):
        def run(owner):
            for piece in (self.r.near,) if owner else (self.r.far, self.r.near):
                for member in (self.r.x, 1 - self.r.x):
                    self.back(piece, member, False, False).wait_recv()
                    if not self.end:
                        self.back(piece, member, False, True).start()

        self.by_place(run)

    def finish(self):
        def run(owner):
            near, far = self.r.near, self.r.far
            self.line(near, 2 if owner else near).wait_send()
            if not owner:
                self.line(far, far).wait_send()
            if not self.end:
                for member in (0, 1):
                    self.back(near, member, False, True).wait_send()
                    self.back(far, member, False, True).wait_send()
            if owner:
                for member in (0, 1):
                    self.back(far, member, False, True, True).wait_send()
                self.pair(far).wait_send()
                self.over(far, self.r.x, False).wait_send()
                self.keep(self.row_of(far, self.r.x), self.rows // 4).wait()

        self.by_place(run)


ROLES = ("start", "paired", "chain_near", "chain_far", "exchanged", "back_near", "back_far", "finish")


UNITS = (
    (LineFirst, -1, 0, 256),
    (PairFirst, -1, 256, 256),
    (PairFirst, -1, 512, 256),
    (LineFirst, -1, 768, 256),
    (PairFirst, -1, 1024, 256),
    (LineFirst, -1, 1280, 256),
    (PairFirst, -1, 1536, 256),
    (LineFirst, -1, 1792, 256),
    (LineFirst, -1, 2048, 256),
    (PairFirst, 0, 0, 1024),
    (PairFirst, 1, 0, 1024),
    (PairFirst, 2, 0, 1024),
)

STEPS = (
    (0, ((0, 0),), ()),
    (1, ((1, 0),), ()),
    (2, (), ()),
    (3, (), ()),
    (7, ((7, 0), (2, 0)), ()),
    (5, (), ((2, 0), (0, 2), (1, 0))),
    (28, (), ()),
    (4, (), ()),
    (27, (), ()),
    (6, ((6, 0), (3, 0)), ()),
    (8, ((5, 0), (4, 0)), ((6, 0), (4, 0), (7, 2), (0, 3))),
    (9, (), ((3, 2),)),
    (24, (), ()),
    (10, (), ((7, 3),)),
    (11, ((0, 3), (6, 1), (1, 1)), ((6, 1),)),
    (25, (), ((5, 2), (3, 3))),
    (12, ((4, 1), (2, 1)), ((4, 1), (5, 3), (1, 1), (1, 2))),
    (13, (), ()),
    (26, (), ()),
    (29, (), ((2, 1), (4, 2), (1, 3), (6, 2))),
    (14, ((8, 0), (7, 3)), ()),
    (18, (), ()),
    (31, (), ((2, 2),)),
    (23, ((11, 0),), ((11, 0), (10, 0), (6, 3), (9, 0), (4, 3), (8, 2))),
    (15, ((0, 4),), ()),
    (19, ((10, 0), (11, 1), (0, 5), (7, 4), (9, 0), (5, 3)), ((11, 1), (2, 3), (11, 2), (8, 3), (0, 5), (10, 1))),
    (20, (), ((11, 3), (10, 2), (0, 6), (7, 5), (9, 1), (10, 3), (1, 5), (2, 5), (7, 6), (9, 2), (1, 6), (6, 5))),
    (21, ((10, 1), (7, 5), (1, 3), (2, 3), (9, 1), (6, 3)), ((2, 6),)),
    (32, (), ()),
    (35, ((5, 4),), ((9, 3), (4, 5), (5, 5), (6, 6))),
    (16, ((4, 3),), ((4, 6), (11, 5), (10, 5))),
    (17, ((8, 3), (5, 5), (10, 3), (3, 3), (11, 3)), ((5, 6),)),
    (33, ((8, 4), (9, 3)), ((9, 5), (11, 6), (10, 6), (8, 5))),
    (30, ((3, 4),), ((9, 6),)),
    (22, ((2, 6), (8, 5), (6, 6)), ()),
    (34, ((1, 6), (4, 6), (3, 5), (11, 6)), ((3, 5), (8, 6))),
    (36, ((9, 6), (10, 6), (3, 6), (7, 6), (8, 6), (5, 6), (0, 6)), ((3, 6),)),
)


def greet(ring):
    barrier = pltpu.get_barrier_semaphore()
    s, t, count = ring.s, ring.t, ring.count

    def signal(to):
        pl.semaphore_signal(barrier, inc=1, device_id=to, device_id_type=MESH)

    signal((s, mate(t, 1)))
    signal((s, mate(t, 2)))
    total = jnp.int32(2)
    bit = 1
    while bit < count:
        signal((mate(s, bit), t))
        total = total + 1
        bit *= 2
    for hop in (-2, -1, 1, 2):
        ok = (s + hop >= 0) & (s + hop < count)

        @pl.when(ok)
        def _():
            signal((s + hop, t))

        total = total + ok.astype(jnp.int32)
    pl.semaphore_wait(barrier, total)


def mate(place, bit):
    return place + bit - 2 * bit * ((place // bit) % 2)


def dot(a, b):
    return jnp.dot(a, b, preferred_element_type=F32)


def dot_rows(a, b):
    return lax.dot_general(a, b, (((0,), (0,)), ((), ())), preferred_element_type=F32)


def dot_columns(a, b):
    return lax.dot_general(a, b, (((1,), (1,)), ((), ())), preferred_element_type=F32)


def layer_kernel(
    count, rows, names, *refs
):
    r = SimpleNamespace(**dict(zip(names, refs)))
    ring = Ring(count)
    s, t = ring.s, ring.t
    blocks = rows // BLOCK
    per_pack = PACK // BLOCK
    x_all, g_all, ln = r.x_all, r.g_all, r.ln
    wqkv, wo, win, wout = r.wqkv, r.wo, r.win, r.wout
    width, hidden = win.shape
    hidden_tiles = hidden // BLOCK
    width_tiles = width // BLOCK

    def blk(b):
        return pl.ds(b * BLOCK, BLOCK) if isinstance(b, int) else pl.ds(pl.multiple_of(b * BLOCK, BLOCK), BLOCK)

    loads = {}

    def load(name, src, dst):
        copy = pltpu.make_async_copy(src, dst, r.load_sem.at[len(loads)])
        loads[name] = copy
        copy.start()

    load("x", r.x_in, x_all.at[:, blk(t)])
    load("wqkv", r.wqkv_in, wqkv)
    load("win", r.win_in, win)
    load("g", r.g_in, g_all.at[:, blk(t)])
    load("wout", r.wout_in, wout)
    load("wo", r.wo_in, wo)
    for b in range(blocks):
        place = (blocks * s + b) % per_pack
        load(("cos", b), r.cos_in.at[place], r.cos.at[b])
        load(("sin", b), r.sin_in.at[place], r.sin.at[b])
    greet(ring)

    def gather(which, b, kind):
        src_ref, whole = ((r.x_in, x_all), (r.g_in, g_all))[which]
        to = mate(t, 2) if kind == 1 else mate(t, 1)
        shard = mate(t, 2) if kind == 2 else t
        dst = whole.at[blk(b), blk(shard)]
        src = dst if kind == 2 else src_ref.at[blk(b)]
        return pltpu.make_async_remote_copy(
            src_ref=src,
            dst_ref=dst,
            send_sem=r.ag_send.at[which, b, kind],
            recv_sem=r.ag_recv.at[which, b, kind],
            device_id=(s, to),
            device_id_type=MESH,
        )

    for which in (0, 1):
        for b in range(blocks):
            gather(which, b, 1).start()
            gather(which, b, 0).start()
    r.dk[...] = jnp.zeros(r.dk.shape, F32)
    r.dv[...] = jnp.zeros(r.dv.shape, F32)

    def relay(which, b):
        gather(which, b, 1).wait_recv()
        gather(which, b, 2).start()

    def arrived(which, b):
        gather(which, b, 0).wait_recv()
        gather(which, b, 2).wait_recv()

    lane = lax.broadcasted_iota(jnp.int32, (BLOCK, BLOCK), 1)
    gain_own = r.gain[:, blk(t)]

    def norm(b):
        xb = x_all[blk(b), :].astype(F32)
        mean = jnp.mean(xb, -1, keepdims=True)
        center = xb - mean
        inverse = lax.rsqrt(jnp.mean(center * center, -1, keepdims=True) + EPSILON)
        ln[blk(b), :] = (center * inverse * r.gain[...] + r.bias[...]).astype(BF)
        own = x_all[blk(b), blk(t)].astype(F32)
        r.normed[blk(b), :] = (own - mean) * inverse
        r.inv[blk(b), :] = jnp.broadcast_to(inverse, (BLOCK, 128))

    def turn(v, b, sense):
        cosine = jnp.concatenate([r.cos[b]] * 2, 1)
        sine = jnp.concatenate([r.sin[b]] * 2, 1)
        swapped = jnp.where(lane % 2 == 0, pltpu.roll(v, BLOCK - 1, 1), pltpu.roll(v, 1, 1))
        return v * cosine + sense * sine * swapped

    def goes_on(place, b):
        return ((blocks * place + b) // per_pack == (blocks * (place + 1)) // per_pack) & (
            place < count - 1
        )

    def forward(b, which):
        here, there = blk(blocks + b), blk(b)
        if which == 2:
            src, dst = r.kt.at[blocks + b], r.kt.at[b]
        else:
            ref = (r.kb, r.vb)[which]
            src, dst = ref.at[here], ref.at[there]
        return pltpu.make_async_remote_copy(
            src_ref=src,
            dst_ref=dst,
            send_sem=r.kv_send.at[b, which],
            recv_sem=r.kv_recv.at[b, which],
            device_id=(s + 1, t),
            device_id_type=MESH,
        )

    def row_of(ref, b):
        return ref[blk(b)].reshape(1, BLOCK)

    def project(b):
        lnb = ln[blk(b), :]
        tags = jnp.where(row_of(r.pad, b) == 1, row_of(r.seg, b), -1)
        r.kt[blocks + b] = jnp.broadcast_to(tags, (8, BLOCK))
        r.kb[blk(blocks + b), :] = turn(dot(lnb, wqkv[1]), b, 1.0).astype(BF)
        r.vb[blk(blocks + b), :] = dot(lnb, wqkv[2]).astype(BF)

        @pl.when(goes_on(s, b))
        def _():
            for which in range(3):
                forward(b, which).start()

        r.q[blk(b), :] = turn(dot(lnb, wqkv[0]), b, 1.0).astype(BF)

    for b in range(blocks):
        relay(0, b)
    loads["x"].wait()
    for b in range(blocks):
        arrived(0, b)
        norm(b)
        if b == 0:
            loads["wqkv"].wait()
            for b2 in range(blocks):
                loads[("cos", b2)].wait()
                loads[("sin", b2)].wait()
        project(b)

    loads["win"].wait()

    def expand(j):
        for b in range(blocks):
            pre = dot(ln[blk(b), :], win[:, blk(j)]) + r.b_in[:, blk(j)]
            scale = 0.7978845608028654
            square = pre * pre
            th = jnp.tanh(scale * (pre + 0.044715 * (square * pre)))
            half = 0.5 * (1.0 + th)
            r.act[blk(b), blk(j)] = (pre * half).astype(BF)
            r.dg[blk(b), blk(j)] = half + (0.5 * scale) * pre * (1.0 - th * th) * (
                1.0 + (3 * 0.044715) * square
            )

    for j in range(hidden_tiles):
        expand(j)
        if j < blocks:
            relay(1, j)
    loads["g"].wait()
    loads["wout"].wait()
    loads["wo"].wait()
    for b in range(blocks):
        arrived(1, b)

    units = []
    slots = {}
    for u, (kind, slab, first, size) in enumerate(UNITS):
        if slab < 0:
            out, base = (
                (r.wout_out, 0)
                if first < hidden
                else (r.win_out, hidden)
                if first < hidden + width
                else (r.wo_out, hidden + width)
            )
            part, out_first = r.wide.at[pl.ds(first, size)], first - base
        else:
            part, out, out_first = r.tall.at[slab, pl.ds(first, size)], r.qkv_out.at[slab], first
        key = group(kind, slab, size)
        slot = slots.get(key, 0)
        slots[key] = slot + 1
        units.append(
            kind(
                ring,
                u,
                part,
                out,
                out_first,
                size,
                getattr(r, "pair" + key).at[slot],
                getattr(r, "line" + key).at[slot],
                r.w_send,
                r.w_recv,
                r.w_own,
            )
        )

    def grad_out_tile(j):
        bin_sum = jnp.zeros((1, BLOCK), F32)
        for b in range(blocks):
            pulled = dot_columns(g_all[blk(b), :], wout[blk(j), :])
            gh = (pulled * r.dg[blk(b), blk(j)]).astype(BF)
            r.gh[blk(b), blk(j)] = gh
            bin_sum = bin_sum + jnp.sum(gh.astype(F32), 0, keepdims=True)
        r.vec[0, 0:1, blk(j)] = bin_sum
        r.wide[blk(j), :] = dot_rows(r.act[:, blk(j)], g_all[...]).astype(BF)

    def grad_in_tile(j):
        r.wide[blk(hidden_tiles + j), :] = dot_rows(ln[:, blk(j)], r.gh[...]).astype(BF)

    def context_pull():
        for b in range(blocks):
            r.gc[blk(b), :] = dot_columns(g_all[blk(b), :], wo[...])
        own = g_all[:, blk(t)].astype(F32)
        r.vec[0, 1:2, blk(2)] = jnp.sum(own, 0, keepdims=True)

    def receive_keys():
        for b in range(blocks):

            @pl.when(goes_on(s - 1, b) & (s > 0))
            def _():
                for which in range(3):
                    forward(b, which).wait_recv()

    def attend(i, part):
        held = (blocks * s + i) % per_pack + 1
        for nb in range(1, per_pack + 1):
            if blocks + i - nb + 1 >= 0:

                @pl.when(held == nb)
                def _():
                    attend_window(i, nb, part)

    def attend_window(i, nb, part):
        n = nb * BLOCK
        first = blocks + i - nb + 1
        window = pl.ds(first * BLOCK, n)
        if part == 0:
            row = lax.broadcasted_iota(jnp.int32, (BLOCK, BLOCK), 0)
            wide_row = jnp.broadcast_to(row_of(r.seg, i), (128, BLOCK))
            seg = wide_row.T[:, 0:1]
            for c in range(nb):
                same = r.kt[first + c, 0:1, :] == seg
                if c == nb - 1:
                    same = (same & (lane <= row)) | (lane == row)
                r.mask[:, blk(c)] = jnp.where(same, 0.0, -1e30)
        qb = r.q[blk(i), :]
        gcb = r.gc[blk(i), :]
        kw = r.kb[window, :]
        vw = r.vb[window, :]

        def head(h, carry):
            mine = lane // 64 == h
            at = pl.ds(pl.multiple_of(h * BLOCK, BLOCK), BLOCK)
            qm = jnp.where(mine, qb, jnp.zeros_like(qb))
            r.qm[at, :] = qm
            logit = dot_columns(qm, kw) * (0.125 * LOG2E) + r.mask[:, :n]
            ceiling = jnp.floor(jnp.max(logit, -1, keepdims=True))
            weight = jnp.exp2(logit - ceiling)
            total = 1.0 / jnp.sum(weight, -1, keepdims=True)
            low = weight.astype(BF)
            r.wl[at, :n] = low
            context = dot(low, vw) * total
            gm = jnp.where(mine, gcb, 0.0)
            ga = (gm * total).astype(BF)
            r.gm[at, :] = ga
            offset = jnp.sum(gm * context, -1, keepdims=True) * total
            ds = (weight * (dot_columns(ga, vw) - offset)).astype(BF)
            r.ds[at, :n] = ds
            dq = dot(ds, kw)
            ctx, dqs = carry
            return (jnp.where(mine, context, ctx), jnp.where(mine, dq, dqs))

        zero = jnp.zeros((BLOCK, BLOCK), F32)
        start = (zero, zero) if part == 0 else (r.both[0], r.both[1])
        ctx, dqs = lax.fori_loop(2 * part, 2 * part + 2, head, start)
        if part == 0:
            r.both[0] = ctx
            r.both[1] = dqs
            return
        r.ctx[blk(i), :] = ctx.astype(BF)
        r.g3[blk(i), 0:BLOCK] = turn(0.125 * dqs, i, -1.0).astype(BF)
        for c in range(nb):
            r.dk[blk(first + c), :] += dot_rows(r.ds[:, blk(c)], r.qm[...])
            r.dv[blk(first + c), :] += dot_rows(r.wl[:, blk(c)], r.gm[...])

    def backward(b, which):
        return pltpu.make_async_remote_copy(
            src_ref=r.dks.at[which, blk(b)],
            dst_ref=r.dkr.at[which, blk(b)],
            send_sem=r.dk_send.at[b, which],
            recv_sem=r.dk_recv.at[b, which],
            device_id=(s - 1, t),
            device_id_type=MESH,
        )

    def send_key_grads(i):
        for b in range(blocks):

            @pl.when(goes_on(s - 1, b) & (s > 0) & ((blocks * s) % per_pack == per_pack - 1 - i))
            def _():
                for which, ref in enumerate((r.dk, r.dv)):
                    r.dks[which, blk(b), :] = ref[blk(b), :].astype(BF)
                    backward(b, which).start()

    def grad_wo_tile():
        r.wide[blk(2 * hidden_tiles), :] = dot_rows(r.ctx[...], g_all[...]).astype(BF)

    def split(which, slot):
        to = mate(t, 2) if slot == 2 else mate(t, 1)
        return pltpu.make_async_remote_copy(
            src_ref=r.tp_out.at[which, slot],
            dst_ref=r.tp_got.at[which, slot],
            send_sem=r.tp_send.at[which, slot],
            recv_sem=r.tp_recv.at[which, slot],
            device_id=(s, to),
            device_id_type=MESH,
        )

    def share(which, owner, b):
        if which == 0:
            return dot(r.ctx[blk(b), :], wo[:, blk(owner)]) + dot(
                r.act[blk(b), :], wout[:, blk(owner)]
            )
        total = dot_columns(r.gh[blk(b), :], win[blk(owner), :])
        for k in range(3):
            total = total + dot_columns(r.g3[blk(b), blk(k)], wqkv[k, blk(owner), :])
        return total

    far_mate = mate(mate(t, 1), 2)

    def split_near(which):
        for slot, owner in ((1, far_mate), (0, mate(t, 1))):
            for b in range(blocks):
                r.tp_out[which, slot, blk(b), :] = share(which, owner, b).astype(BF)
            split(which, slot).start()

    def split_far(which):
        split(which, 1).wait_recv()
        for b in range(blocks):
            mine = share(which, mate(t, 2), b)
            r.tp_out[which, 2, blk(b), :] = (
                mine + r.tp_got[which, 1, blk(b), :].astype(F32)
            ).astype(BF)
        split(which, 2).start()

    def split_own(which):
        for b in range(blocks):
            r.tp_sum[which, blk(b), :] = share(which, t, b)

    def split_join(which):
        split(which, 0).wait_recv()
        split(which, 2).wait_recv()
        for b in range(blocks):
            r.tp_sum[which, blk(b), :] += r.tp_got[which, 0, blk(b), :].astype(F32) + r.tp_got[which, 2, blk(b), :].astype(F32)

    def result(which):
        return pltpu.make_async_copy(
            r.tp_sum.at[which], (r.summed, r.pulled)[which], r.out_sem.at[which]
        )

    def join_branch():
        split_join(0)
        result(0).start()

    def join_key_grads():
        for b in range(blocks):
            for which, ref in enumerate((r.dk, r.dv)):

                @pl.when(goes_on(s, b))
                def _():
                    backward_in = pltpu.make_async_remote_copy(
                        src_ref=r.dks.at[which, blk(b)],
                        dst_ref=r.dkr.at[which, blk(b)],
                        send_sem=r.dk_send.at[b, which],
                        recv_sem=r.dk_recv.at[b, which],
                        device_id=(s + 1, t),
                        device_id_type=MESH,
                    )
                    backward_in.wait_recv()
                    ref[blk(blocks + b), :] += r.dkr[which, blk(b), :].astype(F32)

            r.g3[blk(b), blk(1)] = turn(0.125 * r.dk[blk(blocks + b), :], b, -1.0).astype(BF)
            r.g3[blk(b), blk(2)] = r.dv[blk(blocks + b), :].astype(BF)

    def grad_qkv_tiles(part):
        first, last = ((0, 1), (1, 3))[part]
        for j in range(width_tiles):
            tile = dot_rows(ln[:, blk(j)], r.g3[:, first * BLOCK : last * BLOCK]).astype(BF)
            for k in range(first, last):
                at = (k - first) * BLOCK
                r.tall[k, blk(j), :] = tile[:, at : at + BLOCK]

    def stats_copy(level):
        return pltpu.make_async_remote_copy(
            src_ref=r.stats.at[level],
            dst_ref=r.stats_got.at[level],
            send_sem=r.st_send.at[level],
            recv_sem=r.st_recv.at[level],
            device_id=(s, mate(t, 1 << level)),
            device_id_type=MESH,
        )

    def norm_grad():
        split_join(1)
        gain_sum = jnp.zeros((1, BLOCK), F32)
        bias_sum = jnp.zeros((1, BLOCK), F32)
        lane_one = lax.broadcasted_iota(jnp.int32, (BLOCK, 128), 1)
        for b in range(blocks):
            grad = r.tp_sum[1, blk(b), :]
            normed = r.normed[blk(b), :]
            gain_sum = gain_sum + jnp.sum(grad * normed, 0, keepdims=True)
            bias_sum = bias_sum + jnp.sum(grad, 0, keepdims=True)
            hat = grad * gain_own
            first = jnp.sum(hat, -1, keepdims=True)
            second = jnp.sum(hat * normed, -1, keepdims=True)
            both = jnp.where(lane_one == 0, first, second)
            r.stats[0, :, blk(b)] = both.T[0:8, :]
        r.vec[0, 1:2, blk(0)] = gain_sum
        r.vec[0, 1:2, blk(1)] = bias_sum
        stats_copy(0).start()

    def stats_join():
        stats_copy(0).wait_recv()
        r.stats[1] = r.stats[0] + r.stats_got[0]
        stats_copy(1).start()

    def input_grad():
        stats_copy(1).wait_recv()
        for b in range(blocks):
            both = (r.stats[1, :, blk(b)] + r.stats_got[1, :, blk(b)]) * (1.0 / ln.shape[1])
            columns = jnp.concatenate([both] * 16, 0).T
            hat = r.tp_sum[1, blk(b), :] * gain_own
            r.tp_sum[1, blk(b), :] = r.inv[blk(b), 0:1] * (
                hat - columns[:, 0:1] - r.normed[blk(b), :] * columns[:, 1:2]
            )
        result(1).start()

    levels = count.bit_length() - 1

    def vec_copy(level):
        return pltpu.make_async_remote_copy(
            src_ref=r.vec.at[level],
            dst_ref=r.vec_got.at[level],
            send_sem=r.v_send.at[level],
            recv_sem=r.v_recv.at[level],
            device_id=(mate(s, 1 << level), t),
            device_id_type=MESH,
        )

    def vec_start():
        vec_copy(0).start()

    def vec_step(level):
        vec_copy(level).wait_recv()
        r.vec[level + 1] = r.vec[level] + r.vec_got[level]
        if level + 1 < levels:
            vec_copy(level + 1).start()

    def vec_rest():
        for level in range(2, levels):
            vec_step(level)
        r.vec_out[...] = r.vec[levels]

    part = functools.partial
    tasks = [part(grad_out_tile, j) for j in range(hidden_tiles)]
    tasks += [part(grad_in_tile, j) for j in range(width_tiles)]
    tasks += [part(attend, i, half) for i in range(blocks) for half in (0, 1)]
    for which in (0, 1):
        tasks += [part(step, which) for step in (split_near, split_far, split_own, vec_step)]
        tasks.append(part(grad_qkv_tiles, which))
    tasks += [part(send_key_grads, i) for i in range(blocks)]
    tasks += [context_pull, receive_keys, grad_wo_tile, join_branch, join_key_grads]
    tasks += [norm_grad, stats_join, input_grad, vec_start, vec_rest]
    r.vec[0] = jnp.zeros(r.vec.shape[1:], F32)
    at_end = (ring.z == 0) | (ring.z == ring.m - 1)

    def messages(events, end):
        for who, role in events:
            units[who].end = end
            getattr(units[who], ROLES[role])()

    for task, ends, middles in STEPS:
        tasks[task]()

        @pl.when(at_end)
        def _():
            messages(ends, True)

        @pl.when(jnp.logical_not(at_end))
        def _():
            messages(middles, False)

    closing = [(u, len(ROLES) - 1) for u in range(len(units))]

    @pl.when(at_end)
    def _():
        messages(closing, True)

    @pl.when(jnp.logical_not(at_end))
    def _():
        messages(closing, False)

    for which in (0, 1):
        for b in range(blocks):
            for kind in range(3):
                gather(which, b, kind).wait_send()
        for slot in range(3):
            split(which, slot).wait_send()
        stats_copy(which).wait_send()
        result(which).wait()
    for level in range(levels):
        vec_copy(level).wait_send()
    for b in range(blocks):

        @pl.when(goes_on(s, b))
        def _():
            for which in range(3):
                forward(b, which).wait_send()

        @pl.when(goes_on(s - 1, b) & (s > 0))
        def _():
            for which in range(2):
                backward(b, which).wait_send()


def group(kind, slab, size):
    return "%s%d_%d" % (kind.__name__[0], slab < 0, size)


def rotary_tables():
    places = np.arange(PACK, dtype=np.float32)
    inverse = (10000.0 ** (-(np.arange(16, dtype=np.float32) * 2.0) / 32.0)).astype(np.float32)
    phase = (places[:, None] * inverse[None, :]).astype(np.float32)
    cosine, sine = np.cos(phase), np.sin(phase)
    cos_head = np.ones((PACK, 64), np.float32)
    sin_head = np.zeros((PACK, 64), np.float32)
    cos_head[:, 0:32] = np.repeat(cosine, 2, 1)
    sin_head[:, 0:32:2] = -sine
    sin_head[:, 1:32:2] = sine
    shape = (PACK // BLOCK, BLOCK, 128)
    return (
        np.concatenate([cos_head] * 2, 1).reshape(shape),
        np.concatenate([sin_head] * 2, 1).reshape(shape),
    )


def shards(
    x_in, ln_gain, ln_bias, w_qkv, w_o, w_in, b_in, w_out, b_out, grad_out, segment_ids, pad_mask
):
    count = lax.axis_size("seq")
    rows, own_width = x_in.shape
    width = w_in.shape[0]
    hidden = w_in.shape[1]
    blocks = rows // BLOCK
    assert own_width == BLOCK and rows % BLOCK == 0 and w_qkv.shape[2] == BLOCK
    assert hidden == width == 4 * BLOCK and lax.axis_size("tp") == 4 and rows < PACK
    assert count & (count - 1) == 0 and count >= 8 and (count * rows) % PACK == 0
    cos_table, sin_table = rotary_tables()
    levels = count.bit_length() - 1
    groups = {}
    for kind, slab, first, size in UNITS:
        key = group(kind, slab, size)
        groups[key] = (kind, 1024 if slab < 0 else BLOCK, size, groups.get(key, (0, 0, 0, 0))[3] + 1)
    hbm = pl.BlockSpec(memory_space=pl.ANY)
    vmem = pl.BlockSpec(memory_space=pltpu.VMEM)
    vm = pltpu.VMEM
    dma = pltpu.SemaphoreType.DMA
    ins = dict(
        x_in=(x_in, hbm),
        g_in=(grad_out, hbm),
        gain=(ln_gain.reshape(1, -1), vmem),
        bias=(ln_bias.reshape(1, -1), vmem),
        b_in=(b_in.reshape(1, -1), vmem),
        wqkv_in=(w_qkv, hbm),
        wo_in=(w_o, hbm),
        win_in=(w_in, hbm),
        wout_in=(w_out, hbm),
        seg=(segment_ids, vmem),
        pad=(pad_mask, vmem),
        cos_in=(jnp.asarray(cos_table), hbm),
        sin_in=(jnp.asarray(sin_table), hbm),
    )
    outs = dict(
        wout_out=(w_out.shape, BF, hbm),
        win_out=(w_in.shape, BF, hbm),
        wo_out=(w_o.shape, BF, hbm),
        qkv_out=(w_qkv.shape, BF, hbm),
        vec_out=((8, width), F32, vmem),
        summed=((rows, BLOCK), F32, hbm),
        pulled=((rows, BLOCK), F32, hbm),
    )
    scratch = dict(
        x_all=vm((rows, width), BF),
        g_all=vm((rows, width), BF),
        ln=vm((rows, width), BF),
        wqkv=vm(w_qkv.shape, BF),
        wo=vm(w_o.shape, BF),
        win=vm(w_in.shape, BF),
        wout=vm(w_out.shape, BF),
        act=vm((rows, hidden), BF),
        dg=vm((rows, hidden), F32),
        gh=vm((rows, hidden), BF),
        q=vm((rows, BLOCK), BF),
        kb=vm((2 * rows, BLOCK), BF),
        vb=vm((2 * rows, BLOCK), BF),
        kt=vm((2 * blocks, 8, BLOCK), jnp.int32),
        gc=vm((rows, BLOCK), F32),
        dk=vm((2 * rows, BLOCK), F32),
        dv=vm((2 * rows, BLOCK), F32),
        ctx=vm((rows, BLOCK), BF),
        g3=vm((rows, 3 * BLOCK), BF),
        mask=vm((BLOCK, PACK), F32),
        ds=vm((4 * BLOCK, PACK), BF),
        wl=vm((4 * BLOCK, PACK), BF),
        qm=vm((4 * BLOCK, BLOCK), BF),
        gm=vm((4 * BLOCK, BLOCK), BF),
        dks=vm((2, rows, BLOCK), BF),
        dkr=vm((2, rows, BLOCK), BF),
        tp_out=vm((2, 3, rows, BLOCK), BF),
        tp_got=vm((2, 3, rows, BLOCK), BF),
        tp_sum=vm((2, rows, BLOCK), F32),
        normed=vm((rows, BLOCK), F32),
        inv=vm((rows, 128), F32),
        cos=vm((blocks, BLOCK, 128), F32),
        sin=vm((blocks, BLOCK, 128), F32),
        stats=vm((2, 8, rows), F32),
        stats_got=vm((2, 8, rows), F32),
        vec=vm((levels + 1, 8, width), F32),
        vec_got=vm((levels, 8, width), F32),
        wide=vm((9 * 256, 1024), BF),
        tall=vm((3, 1024, 256), BF),
        load_sem=dma((6 + 2 * blocks,)),
        ag_send=dma((2, blocks, 3)),
        ag_recv=dma((2, blocks, 3)),
        kv_send=dma((blocks, 3)),
        kv_recv=dma((blocks, 3)),
        dk_send=dma((blocks, 2)),
        dk_recv=dma((blocks, 2)),
        tp_send=dma((2, 3)),
        tp_recv=dma((2, 3)),
        st_send=dma((2,)),
        st_recv=dma((2,)),
        v_send=dma((levels,)),
        v_recv=dma((levels,)),
        w_send=dma((len(UNITS), 11)),
        w_recv=dma((len(UNITS), 11)),
        w_own=dma((len(UNITS),)),
        out_sem=dma((2,)),
        both=vm((2, BLOCK, BLOCK), F32),
    )
    for key, (kind, columns, size, number) in groups.items():
        pair, line = (2, 4) if kind is PairFirst else (4, 2)
        pieces = 3 if kind is MiddleLast else 2
        scratch["pair" + key] = vm((number, size // pair, columns), BF)
        scratch["line" + key] = vm((number, pieces, size // line, columns), BF)
    names = list(ins) + list(outs) + list(scratch)
    wout, win, wo, qkv, vec, summed, pulled = pl.pallas_call(
        functools.partial(layer_kernel, count, rows, names),
        out_shape=[jax.ShapeDtypeStruct(o[0], o[1]) for o in outs.values()],
        in_specs=[i[1] for i in ins.values()],
        out_specs=[o[2] for o in outs.values()],
        scratch_shapes=list(scratch.values()),
        compiler_params=pltpu.CompilerParams(
            collective_id=0, has_side_effects=True, vmem_limit_bytes=62 * 2**20
        ),
    )(*[i[0] for i in ins.values()])
    return finish(x_in, grad_out, b_out, wout, win, wo, qkv, vec, summed, pulled)


def finish_kernel(
    x_in, g_in, b_out, wout, win, wo, qkv, vec, summed, pulled,
    mixed, grad_input, gain, bias, qkv_out, wo_out, win_out, bin_out, wout_out, bout_out,
):
    wout_out[...] = wout[...].astype(F32)
    win_out[...] = win[...].astype(F32)
    wo_out[...] = wo[...].astype(F32)
    qkv_out[...] = qkv[...].astype(F32)
    mixed[...] = (x_in[...].astype(F32) + summed[...] + b_out[...]).astype(BF)
    grad_input[...] = pulled[...] + g_in[...].astype(F32)

    @pl.when(pl.program_id(0) == 0)
    def _():
        gain[...] = vec[1:2, 0:BLOCK]
        bias[...] = vec[1:2, BLOCK : 2 * BLOCK]
        bout_out[...] = vec[1:2, 2 * BLOCK : 3 * BLOCK]
        bin_out[...] = vec[0:1, :]


def finish(x_in, grad_out, b_out, wout, win, wo, qkv, vec, summed, pulled):
    steps = 1

    def split(shape):
        if len(shape) == 3:
            return pl.BlockSpec((shape[0], shape[1] // steps, shape[2]), lambda i: (0, i, 0))
        return pl.BlockSpec((shape[0] // steps, shape[1]), lambda i: (i, 0))

    def whole(shape):
        return pl.BlockSpec(shape, lambda i: (0,) * len(shape))

    def struct(shape, kind=F32):
        return jax.ShapeDtypeStruct(shape, kind)

    row = (1, BLOCK)
    outs = pl.pallas_call(
        finish_kernel,
        grid=(steps,),
        in_specs=[
            split(x_in.shape),
            split(grad_out.shape),
            whole(row),
            split(wout.shape),
            split(win.shape),
            split(wo.shape),
            split(qkv.shape),
            whole(vec.shape),
            split(summed.shape),
            split(pulled.shape),
        ],
        out_specs=[
            split(x_in.shape),
            split(x_in.shape),
            whole(row),
            whole(row),
            split(qkv.shape),
            split(wo.shape),
            split(win.shape),
            whole((1, vec.shape[1])),
            split(wout.shape),
            whole(row),
        ],
        out_shape=[
            struct(x_in.shape, BF),
            struct(x_in.shape),
            struct(row),
            struct(row),
            struct(qkv.shape),
            struct(wo.shape),
            struct(win.shape),
            struct((1, vec.shape[1])),
            struct(wout.shape),
            struct(row),
        ],
        compiler_params=pltpu.CompilerParams(vmem_limit_bytes=62 * 2**20),
    )(x_in, grad_out, b_out.reshape(row), wout, win, wo, qkv, vec, summed, pulled)
    outs = list(outs)
    for i in (2, 3, 7, 9):
        outs[i] = outs[i].reshape(-1)
    return tuple(outs)


def solution(mesh):
    return jax.shard_map(
        shards,
        mesh=mesh,
        in_specs=(
            P("seq", "tp"),
            P(),
            P(),
            P(None, None, "tp"),
            P("tp", None),
            P(None, "tp"),
            P("tp"),
            P("tp", None),
            P("tp"),
            P("seq", "tp"),
            P("seq"),
            P("seq"),
        ),
        out_specs=(
            P("seq", "tp"),
            P("seq", "tp"),
            P("tp"),
            P("tp"),
            P(None, None, "tp"),
            P("tp", None),
            P(None, "tp"),
            P("tp"),
            P("tp", None),
            P("tp"),
        ),
        check_vma=False,
    )
```

```python
import functools
from types import SimpleNamespace

import jax
import jax.numpy as jnp
import numpy as np
from jax import lax
from jax.experimental import pallas as pl
from jax.experimental.pallas import tpu as pltpu
from jax.sharding import PartitionSpec as P

PACK = 1024
LOG2E = 1.4426950408889634
EPSILON = 1e-05
BLOCK = 256
MESH = pl.DeviceIdType.MESH
BF = jnp.bfloat16
F32 = jnp.float32


class Ring:
    def __init__(self, seq_count):
        self.count = seq_count
        self.m = seq_count // 2
        self.s = lax.axis_index("seq")
        self.t = lax.axis_index("tp")
        self.z = self.s // 2
        self.x = self.s % 2
        low = (self.z < self.m // 2).astype(jnp.int32)
        self.near = low
        self.far = 1 - low

    def at(self, z, x):
        return (z * 2 + x, self.t)

    def peer(self):
        return self.at(self.z, 1 - self.x)

    def step(self, piece, sign):
        return self.at(self.z + sign * (2 * piece - 1), self.x)


def aligned(value):
    return pl.multiple_of(value, 16)


def add_rows(acc, acc_first, got, rows):
    step = 16 if rows % 32 else 32

    def body(i, carry):
        at = pl.ds(aligned(acc_first + i * step), step)
        here = pl.ds(aligned(i * step), step)
        acc[at, :] = (acc[at, :].astype(jnp.float32) + got[here, :].astype(jnp.float32)).astype(
            acc.dtype
        )
        return carry

    lax.fori_loop(0, rows // step, body, 0)


class Unit:
    def __init__(self, ring, index, part, out, out_first, rows, pair_buf, line_buf, send, recv, own):
        self.r, self.u = ring, index
        self.part, self.out, self.out_first, self.rows = part, out, out_first, rows
        self.pair_buf, self.line_buf = pair_buf, line_buf
        self.send, self.recv, self.own = send, recv, own

    def copy(self, src, dst, kind, to, send_kind=None):
        return pltpu.make_async_remote_copy(
            src_ref=src,
            dst_ref=dst,
            send_sem=self.send.at[self.u, kind if send_kind is None else send_kind],
            recv_sem=self.recv.at[self.u, kind],
            device_id=to,
            device_id_type=MESH,
        )

    def p(self, first, rows):
        return self.part.at[pl.ds(aligned(first), rows)]

    def o(self, first, rows):
        return self.out.at[pl.ds(aligned(self.out_first + first), rows)]

    def keep(self, first, rows):
        return pltpu.make_async_copy(self.p(first, rows), self.o(first, rows), self.own.at[self.u])


class PairFirst(Unit):
    def pair(self):
        half = self.rows // 2
        return self.copy(self.p((1 - self.r.x) * half, half), self.pair_buf, 0, self.r.peer())

    def first_row(self, piece, member):
        return member * (self.rows // 2) + piece * (self.rows // 4)

    def line(self, piece):
        return self.copy(
            self.p(self.first_row(piece, self.r.x), self.rows // 4),
            self.line_buf.at[piece],
            1 + piece,
            self.r.step(piece, 1),
        )

    def result(self, piece, origin):
        at = self.p if origin else self.o
        return at(self.first_row(piece, self.r.x), self.rows // 4)

    def back(self, piece, origin):
        dst = self.result(piece, False)
        return self.copy(self.result(piece, origin), dst, 3 + piece, self.r.step(piece, -1))

    def over(self, piece, origin):
        dst = self.result(piece, False)
        return self.copy(self.result(piece, origin), dst, 5 + piece, self.r.peer())

    def add(self, piece):
        self.line(piece).wait_recv()
        row = self.first_row(piece, self.r.x)
        add_rows(self.part, row, self.line_buf.at[piece], self.rows // 4)

    def start(self):
        self.pair().start()

    def paired(self):
        half = self.rows // 2
        self.pair().wait_recv()
        add_rows(self.part, self.r.x * half, self.pair_buf, half)
        if self.end:
            self.line(self.r.near).start()

    def chain_near(self):
        if not self.end:
            self.add(self.r.near)
            self.line(self.r.near).start()

    def chain_far(self):
        piece = self.r.far
        self.add(piece)
        if self.end:
            self.back(piece, True).start()
            self.over(piece, True).start()
            self.keep(self.first_row(piece, self.r.x), self.rows // 4).start()
        else:
            self.line(piece).start()

    def back_near(self):
        piece = self.r.far
        if not self.end:
            self.back(piece, False).wait_recv()
            self.back(piece, False).start()
            self.over(piece, False).start()

    def back_far(self):
        piece = self.r.near
        self.back(piece, False).wait_recv()
        if not self.end:
            self.back(piece, False).start()
        self.over(piece, False).start()

    def finish(self):
        quarter = self.rows // 4
        for piece in (0, 1):
            row = self.first_row(piece, 1 - self.r.x)
            self.copy(self.o(row, quarter), self.o(row, quarter), 5 + piece, self.r.peer()).wait_recv()
            self.over(piece, False).wait_send()
        self.pair().wait_send()
        self.line(self.r.near).wait_send()
        self.back(self.r.far, False).wait_send()
        if self.end:
            self.keep(self.first_row(self.r.far, self.r.x), quarter).wait()
        else:
            self.line(self.r.far).wait_send()
            self.back(self.r.near, False).wait_send()


class LineFirst(Unit):
    def line(self, piece):
        half = self.rows // 2
        return self.copy(
            self.p(piece * half, half), self.line_buf.at[piece], 1 + piece, self.r.step(piece, 1)
        )

    def row_of(self, piece, member):
        return piece * (self.rows // 2) + member * (self.rows // 4)

    def pair(self, piece):
        quarter = self.rows // 4
        return self.copy(
            self.p(self.row_of(piece, 1 - self.r.x), quarter), self.pair_buf, 0, self.r.peer()
        )

    def result(self, piece, member, origin):
        at = self.p if origin else self.o
        return at(self.row_of(piece, member), self.rows // 4)

    def over(self, piece, member, origin):
        dst = self.result(piece, member, False)
        return self.copy(self.result(piece, member, origin), dst, 3, self.r.peer())

    def back(self, piece, member, origin):
        dst = self.result(piece, member, False)
        to = self.r.step(piece, -1)
        return self.copy(self.result(piece, member, origin), dst, 4 + 2 * piece + member, to)

    def add(self, piece):
        half = self.rows // 2
        self.line(piece).wait_recv()
        add_rows(self.part, piece * half, self.line_buf.at[piece], half)

    def start(self):
        if self.end:
            self.line(self.r.near).start()

    def chain_near(self):
        if not self.end:
            self.add(self.r.near)
            self.line(self.r.near).start()

    def chain_far(self):
        piece = self.r.far
        self.add(piece)
        if self.end:
            self.pair(piece).start()
        else:
            self.line(piece).start()

    def exchanged(self):
        piece = self.r.far
        quarter = self.rows // 4
        if self.end:
            self.pair(piece).wait_recv()
            row = self.row_of(piece, self.r.x)
            add_rows(self.part, row, self.pair_buf, quarter)
            self.over(piece, self.r.x, True).start()
            self.back(piece, self.r.x, True).start()
            self.keep(row, quarter).start()

    def back_near(self):
        piece = self.r.far
        other = 1 - self.r.x
        if self.end:
            self.over(piece, other, False).wait_recv()
            self.back(piece, other, False).start()
        else:
            for member in (self.r.x, other):
                self.back(piece, member, False).wait_recv()
                self.back(piece, member, False).start()

    def back_far(self):
        piece = self.r.near
        for member in (self.r.x, 1 - self.r.x):
            self.back(piece, member, False).wait_recv()
            if not self.end:
                self.back(piece, member, False).start()

    def finish(self):
        self.line(self.r.near).wait_send()
        for member in (0, 1):
            self.back(self.r.far, member, False).wait_send()
        if self.end:
            piece = self.r.far
            self.pair(piece).wait_send()
            self.over(piece, self.r.x, False).wait_send()
            self.keep(self.row_of(piece, self.r.x), self.rows // 4).wait()
        else:
            self.line(self.r.far).wait_send()
            for member in (0, 1):
                self.back(self.r.near, member, False).wait_send()


class MiddleLast(LineFirst):
    def by_place(self, run):
        middle = self.r.m // 2
        if self.end:
            run(False)
        elif middle == 2:
            run(True)
        else:
            owner = (self.r.z == middle - 1) | (self.r.z == middle)
            pl.when(owner)(lambda: run(True))
            pl.when(jnp.logical_not(owner))(lambda: run(False))

    def inner(self):
        return self.r.step(self.r.near, 1)

    def outer(self):
        return self.r.step(self.r.near, -1)

    def line(self, piece, slot):
        half = self.rows // 2
        return self.copy(
            self.p(piece * half, half), self.line_buf.at[slot], 1 + slot, self.inner()
        )

    def add(self, piece, slot):
        half = self.rows // 2
        self.line(piece, slot).wait_recv()
        add_rows(self.part, piece * half, self.line_buf.at[slot], half)

    def over(self, piece, member, origin):
        dst = self.result(piece, member, False)
        return self.copy(self.result(piece, member, origin), dst, 4, self.r.peer())

    def back(self, piece, member, origin, outward, again=False):
        dst = self.result(piece, member, False)
        kind = 5 + 2 * piece + member
        to = self.outer() if outward else self.inner()
        src = self.result(piece, member, origin)
        return self.copy(src, dst, kind, to, 9 + member if again else kind)

    def start(self):
        if self.end:
            self.line(self.r.near, self.r.near).start()
            self.line(self.r.far, self.r.far).start()

    def chain_near(self):
        def run(owner):
            near, far = self.r.near, self.r.far
            self.add(near, near)
            self.line(near, 2 if owner else near).start()
            if not owner:
                self.add(far, far)
                self.line(far, far).start()

        if not self.end:
            self.by_place(run)

    def chain_far(self):
        def run(owner):
            if owner:
                self.add(self.r.far, self.r.far)
                self.add(self.r.far, 2)
                self.pair(self.r.far).start()

        self.by_place(run)

    def own_back(self, member, origin):
        self.back(self.r.far, member, origin, False).start()
        self.back(self.r.far, member, origin, True, True).start()

    def exchanged(self):
        def run(owner):
            if owner:
                piece, quarter = self.r.far, self.rows // 4
                self.pair(piece).wait_recv()
                row = self.row_of(piece, self.r.x)
                add_rows(self.part, row, self.pair_buf, quarter)
                self.over(piece, self.r.x, True).start()
                self.own_back(self.r.x, True)
                self.keep(row, quarter).start()

        self.by_place(run)

    def back_near(self):
        def run(owner):
            if owner:
                other = 1 - self.r.x
                self.over(self.r.far, other, False).wait_recv()
                self.own_back(other, False)

        self.by_place(run)

    def back_far(self):
        def run(owner):
            for piece in (self.r.near,) if owner else (self.r.far, self.r.near):
                for member in (self.r.x, 1 - self.r.x):
                    self.back(piece, member, False, False).wait_recv()
                    if not self.end:
                        self.back(piece, member, False, True).start()

        self.by_place(run)

    def finish(self):
        def run(owner):
            near, far = self.r.near, self.r.far
            self.line(near, 2 if owner else near).wait_send()
            if not owner:
                self.line(far, far).wait_send()
            if not self.end:
                for member in (0, 1):
                    self.back(near, member, False, True).wait_send()
                    self.back(far, member, False, True).wait_send()
            if owner:
                for member in (0, 1):
                    self.back(far, member, False, True, True).wait_send()
                self.pair(far).wait_send()
                self.over(far, self.r.x, False).wait_send()
                self.keep(self.row_of(far, self.r.x), self.rows // 4).wait()

        self.by_place(run)


ROLES = ("start", "paired", "chain_near", "chain_far", "exchanged", "back_near", "back_far", "finish")


UNITS = (
    (LineFirst, -1, 0, 256),
    (PairFirst, -1, 256, 256),
    (PairFirst, -1, 512, 256),
    (LineFirst, -1, 768, 256),
    (PairFirst, -1, 1024, 256),
    (LineFirst, -1, 1280, 256),
    (PairFirst, -1, 1536, 256),
    (LineFirst, -1, 1792, 256),
    (LineFirst, -1, 2048, 256),
    (PairFirst, 0, 0, 1024),
    (PairFirst, 1, 0, 1024),
    (PairFirst, 2, 0, 1024),
)

STEPS = (
    (0, ((0, 0),), ()),
    (1, ((1, 0),), ()),
    (2, (), ()),
    (3, (), ()),
    (7, ((7, 0), (2, 0)), ()),
    (5, (), ((2, 0), (0, 2), (1, 0))),
    (28, (), ()),
    (4, (), ()),
    (27, (), ()),
    (6, ((6, 0), (3, 0)), ()),
    (8, ((5, 0), (4, 0)), ((6, 0), (4, 0), (7, 2), (0, 3))),
    (9, (), ((3, 2),)),
    (24, (), ()),
    (10, (), ((7, 3),)),
    (11, ((0, 3), (6, 1), (1, 1)), ((6, 1),)),
    (25, (), ((5, 2), (3, 3))),
    (12, ((4, 1), (2, 1)), ((4, 1), (5, 3), (1, 1), (1, 2))),
    (13, (), ()),
    (26, (), ()),
    (29, (), ((2, 1), (4, 2), (1, 3), (6, 2))),
    (14, ((8, 0), (7, 3)), ()),
    (18, (), ()),
    (31, (), ((2, 2),)),
    (23, ((11, 0),), ((11, 0), (10, 0), (6, 3), (9, 0), (4, 3), (8, 2))),
    (15, ((0, 4),), ()),
    (19, ((10, 0), (11, 1), (0, 5), (7, 4), (9, 0), (5, 3)), ((11, 1), (2, 3), (11, 2), (8, 3), (0, 5), (10, 1))),
    (20, (), ((11, 3), (10, 2), (0, 6), (7, 5), (9, 1), (10, 3), (1, 5), (2, 5), (7, 6), (9, 2), (1, 6), (6, 5))),
    (21, ((10, 1), (7, 5), (1, 3), (2, 3), (9, 1), (6, 3)), ((2, 6),)),
    (32, (), ()),
    (35, ((5, 4),), ((9, 3), (4, 5), (5, 5), (6, 6))),
    (16, ((4, 3),), ((4, 6), (11, 5), (10, 5))),
    (17, ((8, 3), (5, 5), (10, 3), (3, 3), (11, 3)), ((5, 6),)),
    (33, ((8, 4), (9, 3)), ((9, 5), (11, 6), (10, 6), (8, 5))),
    (30, ((3, 4),), ((9, 6),)),
    (22, ((2, 6), (8, 5), (6, 6)), ()),
    (34, ((1, 6), (4, 6), (3, 5), (11, 6)), ((3, 5), (8, 6))),
    (36, ((9, 6), (10, 6), (3, 6), (7, 6), (8, 6), (5, 6), (0, 6)), ((3, 6),)),
)


def greet(ring):
    barrier = pltpu.get_barrier_semaphore()
    s, t, count = ring.s, ring.t, ring.count

    def signal(to):
        pl.semaphore_signal(barrier, inc=1, device_id=to, device_id_type=MESH)

    signal((s, mate(t, 1)))
    signal((s, mate(t, 2)))
    total = jnp.int32(2)
    bit = 1
    while bit < count:
        signal((mate(s, bit), t))
        total = total + 1
        bit *= 2
    for hop in (-2, -1, 1, 2):
        ok = (s + hop >= 0) & (s + hop < count)

        @pl.when(ok)
        def _():
            signal((s + hop, t))

        total = total + ok.astype(jnp.int32)
    pl.semaphore_wait(barrier, total)


def mate(place, bit):
    return place + bit - 2 * bit * ((place // bit) % 2)


def dot(a, b):
    return jnp.dot(a, b, preferred_element_type=F32)


def dot_rows(a, b):
    return lax.dot_general(a, b, (((0,), (0,)), ((), ())), preferred_element_type=F32)


def dot_columns(a, b):
    return lax.dot_general(a, b, (((1,), (1,)), ((), ())), preferred_element_type=F32)


def layer_kernel(
    count, rows, names, *refs
):
    r = SimpleNamespace(**dict(zip(names, refs)))
    ring = Ring(count)
    s, t = ring.s, ring.t
    blocks = rows // BLOCK
    per_pack = PACK // BLOCK
    x_all, g_all, ln = r.x_all, r.g_all, r.ln
    wqkv, wo, win, wout = r.wqkv, r.wo, r.win, r.wout
    width, hidden = win.shape
    hidden_tiles = hidden // BLOCK
    width_tiles = width // BLOCK

    def blk(b):
        return pl.ds(b * BLOCK, BLOCK) if isinstance(b, int) else pl.ds(pl.multiple_of(b * BLOCK, BLOCK), BLOCK)

    loads = {}

    def load(name, src, dst):
        copy = pltpu.make_async_copy(src, dst, r.load_sem.at[len(loads)])
        loads[name] = copy
        copy.start()

    load("x", r.x_in, x_all.at[:, blk(t)])
    load("wqkv", r.wqkv_in, wqkv)
    load("win", r.win_in, win)
    load("g", r.g_in, g_all.at[:, blk(t)])
    load("wout", r.wout_in, wout)
    load("wo", r.wo_in, wo)
    for b in range(blocks):
        place = (blocks * s + b) % per_pack
        load(("cos", b), r.cos_in.at[place], r.cos.at[b])
        load(("sin", b), r.sin_in.at[place], r.sin.at[b])
    greet(ring)

    def gather(which, b, kind):
        src_ref, whole = ((r.x_in, x_all), (r.g_in, g_all))[which]
        to = mate(t, 2) if kind == 1 else mate(t, 1)
        shard = mate(t, 2) if kind == 2 else t
        dst = whole.at[blk(b), blk(shard)]
        src = dst if kind == 2 else src_ref.at[blk(b)]
        return pltpu.make_async_remote_copy(
            src_ref=src,
            dst_ref=dst,
            send_sem=r.ag_send.at[which, b, kind],
            recv_sem=r.ag_recv.at[which, b, kind],
            device_id=(s, to),
            device_id_type=MESH,
        )

    for which in (0, 1):
        for b in range(blocks):
            gather(which, b, 1).start()
            gather(which, b, 0).start()
    r.dk[...] = jnp.zeros(r.dk.shape, F32)
    r.dv[...] = jnp.zeros(r.dv.shape, F32)

    def relay(which, b):
        gather(which, b, 1).wait_recv()
        gather(which, b, 2).start()

    def arrived(which, b):
        gather(which, b, 0).wait_recv()
        gather(which, b, 2).wait_recv()

    lane = lax.broadcasted_iota(jnp.int32, (BLOCK, BLOCK), 1)
    gain_own = r.gain[:, blk(t)]

    def norm(b):
        xb = x_all[blk(b), :].astype(F32)
        mean = jnp.mean(xb, -1, keepdims=True)
        center = xb - mean
        inverse = lax.rsqrt(jnp.mean(center * center, -1, keepdims=True) + EPSILON)
        ln[blk(b), :] = (center * inverse * r.gain[...] + r.bias[...]).astype(BF)
        own = x_all[blk(b), blk(t)].astype(F32)
        r.normed[blk(b), :] = (own - mean) * inverse
        r.inv[blk(b), :] = jnp.broadcast_to(inverse, (BLOCK, 128))

    def turn(v, b, sense):
        cosine = jnp.concatenate([r.cos[b]] * 2, 1)
        sine = jnp.concatenate([r.sin[b]] * 2, 1)
        swapped = jnp.where(lane % 2 == 0, pltpu.roll(v, BLOCK - 1, 1), pltpu.roll(v, 1, 1))
        return v * cosine + sense * sine * swapped

    def goes_on(place, b):
        return ((blocks * place + b) // per_pack == (blocks * (place + 1)) // per_pack) & (
            place < count - 1
        )

    def forward(b, which):
        here, there = blk(blocks + b), blk(b)
        if which == 2:
            src, dst = r.kt.at[blocks + b], r.kt.at[b]
        else:
            ref = (r.kb, r.vb)[which]
            src, dst = ref.at[here], ref.at[there]
        return pltpu.make_async_remote_copy(
            src_ref=src,
            dst_ref=dst,
            send_sem=r.kv_send.at[b, which],
            recv_sem=r.kv_recv.at[b, which],
            device_id=(s + 1, t),
            device_id_type=MESH,
        )

    def row_of(ref, b):
        return ref[blk(b)].reshape(1, BLOCK)

    def project(b):
        lnb = ln[blk(b), :]
        tags = jnp.where(row_of(r.pad, b) == 1, row_of(r.seg, b), -1)
        r.kt[blocks + b] = jnp.broadcast_to(tags, (8, BLOCK))
        r.kb[blk(blocks + b), :] = turn(dot(lnb, wqkv[1]), b, 1.0).astype(BF)
        r.vb[blk(blocks + b), :] = dot(lnb, wqkv[2]).astype(BF)

        @pl.when(goes_on(s, b))
        def _():
            for which in range(3):
                forward(b, which).start()

        r.q[blk(b), :] = turn(dot(lnb, wqkv[0]), b, 1.0).astype(BF)

    relay(0, 0)
    relay(0, 1)
    loads["x"].wait()
    for b in range(blocks):
        if 1 <= b < blocks - 1:
            relay(0, b + 1)
        arrived(0, b)
        norm(b)
        if b == 0:
            loads["wqkv"].wait()
            for b2 in range(blocks):
                loads[("cos", b2)].wait()
                loads[("sin", b2)].wait()
        project(b)

    loads["win"].wait()

    def expand(j):
        for b in range(blocks):
            pre = dot(ln[blk(b), :], win[:, blk(j)]) + r.b_in[:, blk(j)]
            scale = 0.7978845608028654
            square = pre * pre
            th = jnp.tanh(scale * (pre + 0.044715 * (square * pre)))
            half = 0.5 * (1.0 + th)
            r.act[blk(b), blk(j)] = (pre * half).astype(BF)
            r.dg[blk(b), blk(j)] = half + (0.5 * scale) * pre * (1.0 - th * th) * (
                1.0 + (3 * 0.044715) * square
            )

    relay(1, 0)
    for j in range(hidden_tiles):
        expand(j)
        if j + 1 < blocks:
            relay(1, j + 1)
    loads["g"].wait()
    loads["wout"].wait()
    loads["wo"].wait()
    for b in range(blocks):
        arrived(1, b)

    units = []
    slots = {}
    for u, (kind, slab, first, size) in enumerate(UNITS):
        if slab < 0:
            out, base = (
                (r.wout_out, 0)
                if first < hidden
                else (r.win_out, hidden)
                if first < hidden + width
                else (r.wo_out, hidden + width)
            )
            part, out_first = r.wide.at[pl.ds(first, size)], first - base
        else:
            part, out, out_first = r.tall.at[slab, pl.ds(first, size)], r.qkv_out.at[slab], first
        key = group(kind, slab, size)
        slot = slots.get(key, 0)
        slots[key] = slot + 1
        units.append(
            kind(
                ring,
                u,
                part,
                out,
                out_first,
                size,
                getattr(r, "pair" + key).at[slot],
                getattr(r, "line" + key).at[slot],
                r.w_send,
                r.w_recv,
                r.w_own,
            )
        )

    def grad_out_tile(j):
        bin_sum = jnp.zeros((1, BLOCK), F32)
        for b in range(blocks):
            pulled = dot_columns(g_all[blk(b), :], wout[blk(j), :])
            gh = (pulled * r.dg[blk(b), blk(j)]).astype(BF)
            r.gh[blk(b), blk(j)] = gh
            bin_sum = bin_sum + jnp.sum(gh.astype(F32), 0, keepdims=True)
        r.vec[0, 0:1, blk(j)] = bin_sum
        r.wide[blk(j), :] = dot_rows(r.act[:, blk(j)], g_all[...]).astype(BF)

    def grad_in_tile(j):
        r.wide[blk(hidden_tiles + j), :] = dot_rows(ln[:, blk(j)], r.gh[...]).astype(BF)

    def context_pull():
        for b in range(blocks):
            r.gc[blk(b), :] = dot_columns(g_all[blk(b), :], wo[...])
        own = g_all[:, blk(t)].astype(F32)
        r.vec[0, 1:2, blk(2)] = jnp.sum(own, 0, keepdims=True)

    def receive_keys():
        for b in range(blocks):

            @pl.when(goes_on(s - 1, b) & (s > 0))
            def _():
                for which in range(3):
                    forward(b, which).wait_recv()

    def attend(i, part):
        held = (blocks * s + i) % per_pack + 1
        for nb in range(1, per_pack + 1):
            if blocks + i - nb + 1 >= 0:

                @pl.when(held == nb)
                def _():
                    attend_window(i, nb, part)

    def attend_window(i, nb, part):
        n = nb * BLOCK
        first = blocks + i - nb + 1
        window = pl.ds(first * BLOCK, n)
        if part == 0:
            row = lax.broadcasted_iota(jnp.int32, (BLOCK, BLOCK), 0)
            wide_row = jnp.broadcast_to(row_of(r.seg, i), (128, BLOCK))
            seg = wide_row.T[:, 0:1]
            for c in range(nb):
                same = r.kt[first + c, 0:1, :] == seg
                if c == nb - 1:
                    same = (same & (lane <= row)) | (lane == row)
                r.mask[:, blk(c)] = jnp.where(same, 0.0, -1e30)
        qb = r.q[blk(i), :]
        gcb = r.gc[blk(i), :]
        kw = r.kb[window, :]
        vw = r.vb[window, :]

        def head(h, carry):
            mine = lane // 64 == h
            at = pl.ds(pl.multiple_of(h * BLOCK, BLOCK), BLOCK)
            qm = jnp.where(mine, qb, jnp.zeros_like(qb))
            r.qm[at, :] = qm
            logit = dot_columns(qm, kw) * (0.125 * LOG2E) + r.mask[:, :n]
            ceiling = jnp.floor(jnp.max(logit, -1, keepdims=True))
            weight = jnp.exp2(logit - ceiling)
            total = 1.0 / jnp.sum(weight, -1, keepdims=True)
            low = weight.astype(BF)
            r.wl[at, :n] = low
            context = dot(low, vw) * total
            gm = jnp.where(mine, gcb, 0.0)
            ga = (gm * total).astype(BF)
            r.gm[at, :] = ga
            offset = jnp.sum(gm * context, -1, keepdims=True) * total
            ds = (weight * (dot_columns(ga, vw) - offset)).astype(BF)
            r.ds[at, :n] = ds
            dq = dot(ds, kw)
            ctx, dqs = carry
            return (jnp.where(mine, context, ctx), jnp.where(mine, dq, dqs))

        zero = jnp.zeros((BLOCK, BLOCK), F32)
        start = (zero, zero) if part == 0 else (r.both[0], r.both[1])
        ctx, dqs = lax.fori_loop(2 * part, 2 * part + 2, head, start)
        if part == 0:
            r.both[0] = ctx
            r.both[1] = dqs
            return
        r.ctx[blk(i), :] = ctx.astype(BF)
        r.g3[blk(i), 0:BLOCK] = turn(0.125 * dqs, i, -1.0).astype(BF)
        for c in range(nb):
            r.dk[blk(first + c), :] += dot_rows(r.ds[:, blk(c)], r.qm[...])
            r.dv[blk(first + c), :] += dot_rows(r.wl[:, blk(c)], r.gm[...])

    def backward(b, which):
        return pltpu.make_async_remote_copy(
            src_ref=r.dks.at[which, blk(b)],
            dst_ref=r.dkr.at[which, blk(b)],
            send_sem=r.dk_send.at[b, which],
            recv_sem=r.dk_recv.at[b, which],
            device_id=(s - 1, t),
            device_id_type=MESH,
        )

    def send_key_grads(i):
        for b in range(blocks):

            @pl.when(goes_on(s - 1, b) & (s > 0) & ((blocks * s) % per_pack == per_pack - 1 - i))
            def _():
                for which, ref in enumerate((r.dk, r.dv)):
                    r.dks[which, blk(b), :] = ref[blk(b), :].astype(BF)
                    backward(b, which).start()

    def grad_wo_tile():
        r.wide[blk(2 * hidden_tiles), :] = dot_rows(r.ctx[...], g_all[...]).astype(BF)

    def split(which, slot):
        to = mate(t, 2) if slot == 2 else mate(t, 1)
        return pltpu.make_async_remote_copy(
            src_ref=r.tp_out.at[which, slot],
            dst_ref=r.tp_got.at[which, slot],
            send_sem=r.tp_send.at[which, slot],
            recv_sem=r.tp_recv.at[which, slot],
            device_id=(s, to),
            device_id_type=MESH,
        )

    def share(which, owner, b):
        if which == 0:
            return dot(r.ctx[blk(b), :], wo[:, blk(owner)]) + dot(
                r.act[blk(b), :], wout[:, blk(owner)]
            )
        total = dot_columns(r.gh[blk(b), :], win[blk(owner), :])
        for k in range(3):
            total = total + dot_columns(r.g3[blk(b), blk(k)], wqkv[k, blk(owner), :])
        return total

    far_mate = mate(mate(t, 1), 2)

    def split_near(which):
        for slot, owner in ((1, far_mate), (0, mate(t, 1))):
            for b in range(blocks):
                r.tp_out[which, slot, blk(b), :] = share(which, owner, b).astype(BF)
            split(which, slot).start()

    def split_far(which):
        split(which, 1).wait_recv()
        for b in range(blocks):
            mine = share(which, mate(t, 2), b)
            r.tp_out[which, 2, blk(b), :] = (
                mine + r.tp_got[which, 1, blk(b), :].astype(F32)
            ).astype(BF)
        split(which, 2).start()

    def split_own(which):
        for b in range(blocks):
            r.tp_sum[which, blk(b), :] = share(which, t, b)

    def split_join(which):
        split(which, 0).wait_recv()
        split(which, 2).wait_recv()
        for b in range(blocks):
            r.tp_sum[which, blk(b), :] += r.tp_got[which, 0, blk(b), :].astype(F32) + r.tp_got[which, 2, blk(b), :].astype(F32)

    def result(which):
        return pltpu.make_async_copy(
            r.tp_sum.at[which], (r.summed, r.pulled)[which], r.out_sem.at[which]
        )

    def join_branch():
        split_join(0)
        result(0).start()

    def join_key_grads():
        for b in range(blocks):
            for which, ref in enumerate((r.dk, r.dv)):

                @pl.when(goes_on(s, b))
                def _():
                    backward_in = pltpu.make_async_remote_copy(
                        src_ref=r.dks.at[which, blk(b)],
                        dst_ref=r.dkr.at[which, blk(b)],
                        send_sem=r.dk_send.at[b, which],
                        recv_sem=r.dk_recv.at[b, which],
                        device_id=(s + 1, t),
                        device_id_type=MESH,
                    )
                    backward_in.wait_recv()
                    ref[blk(blocks + b), :] += r.dkr[which, blk(b), :].astype(F32)

            r.g3[blk(b), blk(1)] = turn(0.125 * r.dk[blk(blocks + b), :], b, -1.0).astype(BF)
            r.g3[blk(b), blk(2)] = r.dv[blk(blocks + b), :].astype(BF)

    def grad_qkv_tiles(part):
        first, last = ((0, 1), (1, 3))[part]
        for j in range(width_tiles):
            tile = dot_rows(ln[:, blk(j)], r.g3[:, first * BLOCK : last * BLOCK]).astype(BF)
            for k in range(first, last):
                at = (k - first) * BLOCK
                r.tall[k, blk(j), :] = tile[:, at : at + BLOCK]

    def stats_copy(level):
        return pltpu.make_async_remote_copy(
            src_ref=r.stats.at[level],
            dst_ref=r.stats_got.at[level],
            send_sem=r.st_send.at[level],
            recv_sem=r.st_recv.at[level],
            device_id=(s, mate(t, 1 << level)),
            device_id_type=MESH,
        )

    def norm_grad():
        split_join(1)
        gain_sum = jnp.zeros((1, BLOCK), F32)
        bias_sum = jnp.zeros((1, BLOCK), F32)
        lane_one = lax.broadcasted_iota(jnp.int32, (BLOCK, 128), 1)
        for b in range(blocks):
            grad = r.tp_sum[1, blk(b), :]
            normed = r.normed[blk(b), :]
            gain_sum = gain_sum + jnp.sum(grad * normed, 0, keepdims=True)
            bias_sum = bias_sum + jnp.sum(grad, 0, keepdims=True)
            hat = grad * gain_own
            first = jnp.sum(hat, -1, keepdims=True)
            second = jnp.sum(hat * normed, -1, keepdims=True)
            both = jnp.where(lane_one == 0, first, second)
            r.stats[0, :, blk(b)] = both.T[0:8, :]
        r.vec[0, 1:2, blk(0)] = gain_sum
        r.vec[0, 1:2, blk(1)] = bias_sum
        stats_copy(0).start()

    def stats_join():
        stats_copy(0).wait_recv()
        r.stats[1] = r.stats[0] + r.stats_got[0]
        stats_copy(1).start()

    def input_grad():
        stats_copy(1).wait_recv()
        for b in range(blocks):
            both = (r.stats[1, :, blk(b)] + r.stats_got[1, :, blk(b)]) * (1.0 / ln.shape[1])
            columns = jnp.concatenate([both] * 16, 0).T
            hat = r.tp_sum[1, blk(b), :] * gain_own
            r.tp_sum[1, blk(b), :] = r.inv[blk(b), 0:1] * (
                hat - columns[:, 0:1] - r.normed[blk(b), :] * columns[:, 1:2]
            )
        result(1).start()

    levels = count.bit_length() - 1

    def vec_copy(level):
        return pltpu.make_async_remote_copy(
            src_ref=r.vec.at[level],
            dst_ref=r.vec_got.at[level],
            send_sem=r.v_send.at[level],
            recv_sem=r.v_recv.at[level],
            device_id=(mate(s, 1 << level), t),
            device_id_type=MESH,
        )

    def vec_start():
        vec_copy(0).start()

    def vec_step(level):
        vec_copy(level).wait_recv()
        r.vec[level + 1] = r.vec[level] + r.vec_got[level]
        if level + 1 < levels:
            vec_copy(level + 1).start()

    def vec_rest():
        for level in range(2, levels):
            vec_step(level)
        r.vec_out[...] = r.vec[levels]

    part = functools.partial
    tasks = [part(grad_out_tile, j) for j in range(hidden_tiles)]
    tasks += [part(grad_in_tile, j) for j in range(width_tiles)]
    tasks += [part(attend, i, half) for i in range(blocks) for half in (0, 1)]
    for which in (0, 1):
        tasks += [part(step, which) for step in (split_near, split_far, split_own, vec_step)]
        tasks.append(part(grad_qkv_tiles, which))
    tasks += [part(send_key_grads, i) for i in range(blocks)]
    tasks += [context_pull, receive_keys, grad_wo_tile, join_branch, join_key_grads]
    tasks += [norm_grad, stats_join, input_grad, vec_start, vec_rest]
    r.vec[0] = jnp.zeros(r.vec.shape[1:], F32)
    at_end = (ring.z == 0) | (ring.z == ring.m - 1)

    def messages(events, end):
        for who, role in events:
            units[who].end = end
            getattr(units[who], ROLES[role])()

    for task, ends, middles in STEPS:
        tasks[task]()

        @pl.when(at_end)
        def _():
            messages(ends, True)

        @pl.when(jnp.logical_not(at_end))
        def _():
            messages(middles, False)

    closing = [(u, len(ROLES) - 1) for u in range(len(units))]

    @pl.when(at_end)
    def _():
        messages(closing, True)

    @pl.when(jnp.logical_not(at_end))
    def _():
        messages(closing, False)

    for which in (0, 1):
        for b in range(blocks):
            for kind in range(3):
                gather(which, b, kind).wait_send()
        for slot in range(3):
            split(which, slot).wait_send()
        stats_copy(which).wait_send()
        result(which).wait()
    for level in range(levels):
        vec_copy(level).wait_send()
    for b in range(blocks):

        @pl.when(goes_on(s, b))
        def _():
            for which in range(3):
                forward(b, which).wait_send()

        @pl.when(goes_on(s - 1, b) & (s > 0))
        def _():
            for which in range(2):
                backward(b, which).wait_send()


def group(kind, slab, size):
    return "%s%d_%d" % (kind.__name__[0], slab < 0, size)


def rotary_tables():
    places = np.arange(PACK, dtype=np.float32)
    inverse = (10000.0 ** (-(np.arange(16, dtype=np.float32) * 2.0) / 32.0)).astype(np.float32)
    phase = (places[:, None] * inverse[None, :]).astype(np.float32)
    cosine, sine = np.cos(phase), np.sin(phase)
    cos_head = np.ones((PACK, 64), np.float32)
    sin_head = np.zeros((PACK, 64), np.float32)
    cos_head[:, 0:32] = np.repeat(cosine, 2, 1)
    sin_head[:, 0:32:2] = -sine
    sin_head[:, 1:32:2] = sine
    shape = (PACK // BLOCK, BLOCK, 128)
    return (
        np.concatenate([cos_head] * 2, 1).reshape(shape),
        np.concatenate([sin_head] * 2, 1).reshape(shape),
    )


def shards(
    x_in, ln_gain, ln_bias, w_qkv, w_o, w_in, b_in, w_out, b_out, grad_out, segment_ids, pad_mask
):
    count = lax.axis_size("seq")
    rows, own_width = x_in.shape
    width = w_in.shape[0]
    hidden = w_in.shape[1]
    blocks = rows // BLOCK
    assert own_width == BLOCK and rows % BLOCK == 0 and w_qkv.shape[2] == BLOCK
    assert hidden == width == 4 * BLOCK and lax.axis_size("tp") == 4 and rows < PACK
    assert count & (count - 1) == 0 and count >= 8 and (count * rows) % PACK == 0
    cos_table, sin_table = rotary_tables()
    levels = count.bit_length() - 1
    groups = {}
    for kind, slab, first, size in UNITS:
        key = group(kind, slab, size)
        groups[key] = (kind, 1024 if slab < 0 else BLOCK, size, groups.get(key, (0, 0, 0, 0))[3] + 1)
    hbm = pl.BlockSpec(memory_space=pl.ANY)
    vmem = pl.BlockSpec(memory_space=pltpu.VMEM)
    vm = pltpu.VMEM
    dma = pltpu.SemaphoreType.DMA
    ins = dict(
        x_in=(x_in, hbm),
        g_in=(grad_out, hbm),
        gain=(ln_gain.reshape(1, -1), vmem),
        bias=(ln_bias.reshape(1, -1), vmem),
        b_in=(b_in.reshape(1, -1), vmem),
        wqkv_in=(w_qkv, hbm),
        wo_in=(w_o, hbm),
        win_in=(w_in, hbm),
        wout_in=(w_out, hbm),
        seg=(segment_ids, vmem),
        pad=(pad_mask, vmem),
        cos_in=(jnp.asarray(cos_table), hbm),
        sin_in=(jnp.asarray(sin_table), hbm),
    )
    outs = dict(
        wout_out=(w_out.shape, BF, hbm),
        win_out=(w_in.shape, BF, hbm),
        wo_out=(w_o.shape, BF, hbm),
        qkv_out=(w_qkv.shape, BF, hbm),
        vec_out=((8, width), F32, vmem),
        summed=((rows, BLOCK), F32, hbm),
        pulled=((rows, BLOCK), F32, hbm),
    )
    scratch = dict(
        x_all=vm((rows, width), BF),
        g_all=vm((rows, width), BF),
        ln=vm((rows, width), BF),
        wqkv=vm(w_qkv.shape, BF),
        wo=vm(w_o.shape, BF),
        win=vm(w_in.shape, BF),
        wout=vm(w_out.shape, BF),
        act=vm((rows, hidden), BF),
        dg=vm((rows, hidden), F32),
        gh=vm((rows, hidden), BF),
        q=vm((rows, BLOCK), BF),
        kb=vm((2 * rows, BLOCK), BF),
        vb=vm((2 * rows, BLOCK), BF),
        kt=vm((2 * blocks, 8, BLOCK), jnp.int32),
        gc=vm((rows, BLOCK), F32),
        dk=vm((2 * rows, BLOCK), F32),
        dv=vm((2 * rows, BLOCK), F32),
        ctx=vm((rows, BLOCK), BF),
        g3=vm((rows, 3 * BLOCK), BF),
        mask=vm((BLOCK, PACK), F32),
        ds=vm((4 * BLOCK, PACK), BF),
        wl=vm((4 * BLOCK, PACK), BF),
        qm=vm((4 * BLOCK, BLOCK), BF),
        gm=vm((4 * BLOCK, BLOCK), BF),
        dks=vm((2, rows, BLOCK), BF),
        dkr=vm((2, rows, BLOCK), BF),
        tp_out=vm((2, 3, rows, BLOCK), BF),
        tp_got=vm((2, 3, rows, BLOCK), BF),
        tp_sum=vm((2, rows, BLOCK), F32),
        normed=vm((rows, BLOCK), F32),
        inv=vm((rows, 128), F32),
        cos=vm((blocks, BLOCK, 128), F32),
        sin=vm((blocks, BLOCK, 128), F32),
        stats=vm((2, 8, rows), F32),
        stats_got=vm((2, 8, rows), F32),
        vec=vm((levels + 1, 8, width), F32),
        vec_got=vm((levels, 8, width), F32),
        wide=vm((9 * 256, 1024), BF),
        tall=vm((3, 1024, 256), BF),
        load_sem=dma((6 + 2 * blocks,)),
        ag_send=dma((2, blocks, 3)),
        ag_recv=dma((2, blocks, 3)),
        kv_send=dma((blocks, 3)),
        kv_recv=dma((blocks, 3)),
        dk_send=dma((blocks, 2)),
        dk_recv=dma((blocks, 2)),
        tp_send=dma((2, 3)),
        tp_recv=dma((2, 3)),
        st_send=dma((2,)),
        st_recv=dma((2,)),
        v_send=dma((levels,)),
        v_recv=dma((levels,)),
        w_send=dma((len(UNITS), 11)),
        w_recv=dma((len(UNITS), 11)),
        w_own=dma((len(UNITS),)),
        out_sem=dma((2,)),
        both=vm((2, BLOCK, BLOCK), F32),
    )
    for key, (kind, columns, size, number) in groups.items():
        pair, line = (2, 4) if kind is PairFirst else (4, 2)
        pieces = 3 if kind is MiddleLast else 2
        scratch["pair" + key] = vm((number, size // pair, columns), BF)
        scratch["line" + key] = vm((number, pieces, size // line, columns), BF)
    names = list(ins) + list(outs) + list(scratch)
    wout, win, wo, qkv, vec, summed, pulled = pl.pallas_call(
        functools.partial(layer_kernel, count, rows, names),
        out_shape=[jax.ShapeDtypeStruct(o[0], o[1]) for o in outs.values()],
        in_specs=[i[1] for i in ins.values()],
        out_specs=[o[2] for o in outs.values()],
        scratch_shapes=list(scratch.values()),
        compiler_params=pltpu.CompilerParams(
            collective_id=0, has_side_effects=True, vmem_limit_bytes=62 * 2**20
        ),
    )(*[i[0] for i in ins.values()])
    return finish(x_in, grad_out, b_out, wout, win, wo, qkv, vec, summed, pulled)


def finish_kernel(
    x_in, g_in, b_out, wout, win, wo, qkv, vec, summed, pulled,
    mixed, grad_input, gain, bias, qkv_out, wo_out, win_out, bin_out, wout_out, bout_out,
):
    wout_out[...] = wout[...].astype(F32)
    win_out[...] = win[...].astype(F32)
    wo_out[...] = wo[...].astype(F32)
    qkv_out[...] = qkv[...].astype(F32)
    mixed[...] = (x_in[...].astype(F32) + summed[...] + b_out[...]).astype(BF)
    grad_input[...] = pulled[...] + g_in[...].astype(F32)

    @pl.when(pl.program_id(0) == 0)
    def _():
        gain[...] = vec[1:2, 0:BLOCK]
        bias[...] = vec[1:2, BLOCK : 2 * BLOCK]
        bout_out[...] = vec[1:2, 2 * BLOCK : 3 * BLOCK]
        bin_out[...] = vec[0:1, :]


def finish(x_in, grad_out, b_out, wout, win, wo, qkv, vec, summed, pulled):
    steps = 1

    def split(shape):
        if len(shape) == 3:
            return pl.BlockSpec((shape[0], shape[1] // steps, shape[2]), lambda i: (0, i, 0))
        return pl.BlockSpec((shape[0] // steps, shape[1]), lambda i: (i, 0))

    def whole(shape):
        return pl.BlockSpec(shape, lambda i: (0,) * len(shape))

    def struct(shape, kind=F32):
        return jax.ShapeDtypeStruct(shape, kind)

    row = (1, BLOCK)
    outs = pl.pallas_call(
        finish_kernel,
        grid=(steps,),
        in_specs=[
            split(x_in.shape),
            split(grad_out.shape),
            whole(row),
            split(wout.shape),
            split(win.shape),
            split(wo.shape),
            split(qkv.shape),
            whole(vec.shape),
            split(summed.shape),
            split(pulled.shape),
        ],
        out_specs=[
            split(x_in.shape),
            split(x_in.shape),
            whole(row),
            whole(row),
            split(qkv.shape),
            split(wo.shape),
            split(win.shape),
            whole((1, vec.shape[1])),
            split(wout.shape),
            whole(row),
        ],
        out_shape=[
            struct(x_in.shape, BF),
            struct(x_in.shape),
            struct(row),
            struct(row),
            struct(qkv.shape),
            struct(wo.shape),
            struct(win.shape),
            struct((1, vec.shape[1])),
            struct(wout.shape),
            struct(row),
        ],
        compiler_params=pltpu.CompilerParams(vmem_limit_bytes=62 * 2**20),
    )(x_in, grad_out, b_out.reshape(row), wout, win, wo, qkv, vec, summed, pulled)
    outs = list(outs)
    for i in (2, 3, 7, 9):
        outs[i] = outs[i].reshape(-1)
    return tuple(outs)


def solution(mesh):
    return jax.shard_map(
        shards,
        mesh=mesh,
        in_specs=(
            P("seq", "tp"),
            P(),
            P(),
            P(None, None, "tp"),
            P("tp", None),
            P(None, "tp"),
            P("tp"),
            P("tp", None),
            P("tp"),
            P("seq", "tp"),
            P("seq"),
            P("seq"),
        ),
        out_specs=(
            P("seq", "tp"),
            P("seq", "tp"),
            P("tp"),
            P("tp"),
            P(None, None, "tp"),
            P("tp", None),
            P(None, "tp"),
            P("tp"),
            P("tp", None),
            P("tp"),
        ),
        check_vma=False,
    )
```
